128 devices in a mesh: dp: 16 (over z_lo, y, core), tensor: 8 (over z_hi, x).
Axes of the slice: x: 4, y: 4, z: 4 (z_hi: 2, z_lo: 2; z = z_hi * 2 + z_lo), core: 2. Of those that a mesh axis runs over, the one named last changes fastest.
Arguments:
- tokens: bfloat16 [16384, 2048], P('dp'), may hold values from -6 to 6
- ln_gain: bfloat16 [2048], P('dp'), may hold values from 0.099609375 to 1.8984375
- ln_bias: bfloat16 [2048], P('dp'), may hold values from -2 to 2
- w_qkv: bfloat16 [2048, 3, 2048], P('dp', None, 'tensor'), may hold values from -0.125 to 0.125
- b_qkv: bfloat16 [3, 32, 64], P(None, 'tensor', 'dp'), may hold values from -2 to 2
- w_out: bfloat16 [2048, 2048], P('tensor', 'dp'), may hold values from -1 to 1
- b_out: bfloat16 [2048], P('dp'), may hold values from -2 to 2
- w_up: bfloat16 [2048, 8192], P('dp', 'tensor'), may hold values from -0.125 to 0.125
- b_up: bfloat16 [8, 1024], P('tensor', 'dp'), may hold values from -2 to 2
- w_down: bfloat16 [8192, 2048], P('tensor', 'dp'), may hold values from -0.0625 to 0.0625
- b_down: bfloat16 [2048], P('dp'), may hold values from -2 to 2
- cotangent: bfloat16 [16384, 2048], P('dp'), may hold values from -6 to 6
Outputs:
- mixed: bfloat16 [16384, 2048], P('dp')
- input_grad: bfloat16 [16384, 2048], P('dp')
- grad_ln_gain: float32 [2048], P('dp')
- grad_ln_bias: float32 [2048], P('dp')
- grad_w_qkv: float32 [2048, 3, 2048], P('dp', None, 'tensor')
- grad_b_qkv: float32 [3, 32, 64], P(None, 'tensor', 'dp')
- grad_w_out: float32 [2048, 2048], P('tensor', 'dp')
- grad_b_out: float32 [2048], P('dp')
- grad_w_up: float32 [2048, 8192], P('dp', 'tensor')
- grad_b_up: float32 [8, 1024], P('tensor', 'dp')
- grad_w_down: float32 [8192, 2048], P('tensor', 'dp')
- grad_b_down: float32 [2048], P('dp')
The draws below stay inside these ranges and needn't reach their ends.
All inputs are finite; a program needn't handle non-finite values.
Results may differ from the reference program's by a relative error of at most 0.012.
Values may be sent and summed in bfloat16 or wider, within the bound.
A program may use at most 192 MiB of HBM per device.

```python
import jax
import jax.numpy as jnp
from jax import lax

D = 2048
H = 32
HD = 64
ROT = 32
FF = 8192
LEN = 1024
TOKENS = 16384
N_TENSOR = 8


def block_levels(rng, shape, pieces, smallest, top_value):
    factor_of = 1.0
    for axis_at, parts in pieces:
        draws = jax.random.uniform(jax.random.fold_in(jax.random.fold_in(rng, 6), axis_at), (parts,), jnp.float32, smallest / len(pieces), top_value / len(pieces))
        factor_of = factor_of * jnp.repeat(jnp.exp(draws), shape[axis_at] // parts).reshape((-1,) + (1,) * (len(shape) - 1 - axis_at))
    return factor_of


def noise(rng, dims, width, reach, pieces=(), held_as=jnp.bfloat16):
    level = block_levels(rng, dims, pieces, -0.22, 0.18) if pieces else 1.0
    values = jax.random.normal(rng, dims, jnp.float32) * width * level
    return jnp.minimum(jnp.maximum(values, -reach), reach).astype(held_as)


def setup_inputs(seed: int = 0) -> dict:
    key_of = jax.random.split(jax.random.key(seed), 13)
    tokens = noise(key_of[0], (TOKENS, D), 1.0, 6.0, ((0, 16),))
    ln_gain = jnp.clip(1.0 + 0.18 * jax.random.normal(key_of[1], (D,), jnp.float32), 0.099609375, 1.8984375).astype(jnp.bfloat16)
    ln_bias = noise(key_of[2], (D,), 0.3, 2.0, ((0, 16),))
    w_qkv = noise(key_of[3], (D, 3, D), D ** -0.5, 0.125, ((0, 16), (2, 8)))
    b_qkv = noise(key_of[4], (3, H, HD), 0.3, 2.0, ((1, 8), (2, 16)))
    w_out = noise(key_of[5], (D, D), (D // 64) ** -0.5, 1.0, ((0, 8), (1, 16)))
    b_out = noise(key_of[6], (D,), 0.3, 2.0, ((0, 16),))
    w_up = noise(key_of[7], (D, FF), D ** -0.5, 0.125, ((0, 16), (1, 8)))
    b_up = noise(key_of[8], (N_TENSOR, FF // N_TENSOR), 0.3, 2.0, ((0, 8), (1, 16)))
    w_down = noise(key_of[9], (FF, D), FF ** -0.5, 0.0625, ((0, 8), (1, 16)))
    b_down = noise(key_of[10], (D,), 0.3, 2.0, ((0, 16),))
    cotangent = noise(key_of[11], (TOKENS, D), 1.0, 6.0, ((0, 16),))
    return {"tokens": tokens, "ln_gain": ln_gain, "ln_bias": ln_bias, "w_qkv": w_qkv, "b_qkv": b_qkv, "w_out": w_out, "b_out": b_out, "w_up": w_up, "b_up": b_up, "w_down": w_down, "b_down": b_down, "cotangent": cotangent}


norm_epsilon = 1e-05
rope_base = 10000.0
highest_precision = lax.Precision.HIGHEST

@jax.custom_vjp
def low(v):
    return lax.optimization_barrier(v.astype(jnp.bfloat16)).astype(jnp.float32)

@jax.custom_vjp
def low_back(v):
    return v

def low_keep(v):
    return (low(v), None)

def low_pass(kept, grad):
    return (grad,)

def back_keep(v):
    return (v, None)

def back_low(kept, grad):
    return (low(grad),)
low.defvjp(low_keep, low_pass)
low_back.defvjp(back_keep, back_low)

def rotary_tables(length, rot_dims):
    positions = jnp.arange(length, dtype=jnp.float32)
    frequency = rope_base ** (-jnp.arange(0, rot_dims, 2, dtype=jnp.float32) / rot_dims)
    angles = positions[:, None] * frequency[None, :]
    angles = jnp.concatenate([angles, angles], axis=-1)
    return (jnp.cos(angles), jnp.sin(angles))

def rotate(values_in, cosine_table, sine_table):
    rot_dims = cosine_table.shape[-1]
    half_dims = rot_dims // 2
    rotated_part = values_in[..., :rot_dims]
    turned = jnp.concatenate([-rotated_part[..., half_dims:], rotated_part[..., :half_dims]], axis=-1)
    return jnp.concatenate([rotated_part * cosine_table + turned * sine_table, values_in[..., rot_dims:]], axis=-1)

def forward(inputs, ln_gain, ln_bias, w_qkv, b_qkv, w_out, b_out, w_up, b_up, w_down, b_down):
    length = inputs.shape[0]
    row_mean = lax.optimization_barrier(jnp.mean(inputs, axis=-1, keepdims=True))
    centred = inputs - row_mean
    row_variance = lax.optimization_barrier(jnp.mean(centred * centred, axis=-1, keepdims=True))
    normed = low(centred * lax.rsqrt(row_variance + norm_epsilon) * ln_gain + ln_bias)
    projected = jnp.einsum('td,dce->tce', normed, w_qkv, precision=highest_precision) + b_qkv.reshape(3, D)
    projected = projected.reshape(length, 3, H, HD)
    cosine_table, sine_table = rotary_tables(length, ROT)
    cosine_table = cosine_table[:, None, :]
    sine_table = sine_table[:, None, :]
    queries = low(rotate(low_back(projected[:, 0]), cosine_table, sine_table))
    key_rows = low(rotate(low_back(projected[:, 1]), cosine_table, sine_table))
    value_rows = low(low_back(projected[:, 2]))
    scores = jnp.einsum('qhe,khe->hqk', queries, key_rows, precision=highest_precision) * HD ** (-0.5)
    scores = low_back(scores)
    causal = jnp.arange(length)[:, None] >= jnp.arange(length)[None, :]
    scores = jnp.where(causal[None], scores, -1e+30)
    weights = low(jax.nn.softmax(scores, axis=-1))
    attended = jnp.einsum('hqk,khe->qhe', weights, value_rows, precision=highest_precision).reshape(length, D)
    attended = low_back(low(attended))
    attn_out = jnp.dot(attended, w_out, precision=highest_precision)
    hidden_pre = low_back(jnp.dot(normed, w_up, precision=highest_precision) + b_up.reshape(FF))
    activated = low(jax.nn.gelu(hidden_pre, approximate=True))
    mlp_out = jnp.dot(activated, w_down, precision=highest_precision)
    return inputs + attn_out + mlp_out + b_out + b_down

def reference(tokens, ln_gain, ln_bias, w_qkv, b_qkv, w_out, b_out, w_up, b_up, w_down, b_down, cotangent):
    parameters = tuple((item.astype(jnp.float32) for item in (ln_gain, ln_bias, w_qkv, b_qkv, w_out, b_out, w_up, b_up, w_down, b_down)))
    sequences = tokens.astype(jnp.float32).reshape(-1, LEN, D)
    upstreams = cotangent.astype(jnp.float32).reshape(-1, LEN, D)

    def one_sequence(running, sequence_pair):
        inputs, upstream = sequence_pair
        outputs, pullback = jax.vjp(forward, inputs, *parameters)
        gradients = pullback(upstream)
        running = tuple((left + right for left, right in zip(running, gradients[1:])))
        return (running, (outputs.astype(jnp.bfloat16), gradients[0].astype(jnp.bfloat16)))
    zero_grads = tuple((jnp.zeros_like(item) for item in parameters))
    summed_grads, (mixed, input_grad) = lax.scan(one_sequence, zero_grads, (sequences, upstreams))
    return (mixed.reshape(TOKENS, D), input_grad.reshape(TOKENS, D), summed_grads[0], summed_grads[1], summed_grads[2], summed_grads[3], summed_grads[4], summed_grads[5], summed_grads[6], summed_grads[7], summed_grads[8], summed_grads[9])
```

```python
from functools import partial

import jax
import jax.numpy as jnp
import numpy as np
from jax import lax
from jax.sharding import PartitionSpec as P
from jax.experimental import pallas as pl
from jax.experimental.pallas import tpu as pltpu

HD = 64
ROT = 32
LEN = 1024
norm_epsilon = 1e-05
rope_base = 10000.0
MESH = pl.DeviceIdType.MESH

def place():
    dp = lax.axis_index("dp"); tn = lax.axis_index("tensor")
    return dp % 2, (dp // 2) % 4, dp // 8, tn % 4, tn // 4

def peer(c, y, zl, x, zh):
    return (zl * 8 + y * 2 + c, zh * 4 + x)

RELS = [(0, 0), (0, 1), (0, 3), (0, 2), (1, 0), (1, 1), (1, 3), (1, 2)]

def enter(devices):
    bar = pltpu.get_barrier_semaphore()
    for d in devices:
        pl.semaphore_signal(bar, inc=1, device_id=d, device_id_type=MESH)
    pl.semaphore_wait(bar, len(devices))

class Gather:
    def __init__(s, shard, full, axis, ss, rs):
        s.axis, s.ss, s.rs, s.full = axis, ss, rs, full
        s.c, s.y, s.zl, x, zh = place()
        c, y, zl = s.c, s.y, s.zl
        s.total = shard.shape[1 if axis == 2 else 0]
        s.shard = shard
        s.up = peer(c, (y + 1) % 4, zl, x, zh); s.down = peer(c, (y + 3) % 4, zl, x, zh)
        s.z = peer(c, y, 1 - zl, x, zh); s.sib = peer(1 - c, y, zl, x, zh)
        s.sends = []
    def slot(s, dz, dy, c=None, half=None):
        c = s.c if c is None else c
        d = ((s.zl + dz) % 2) * 8 + ((s.y + dy) % 4) * 2 + c
        n = s.total if half is None else s.total // 2
        lo = 0 if half is None else half * n
        if s.axis == 0: return s.full.at[pl.ds(pl.multiple_of(d * s.total + lo, 16), n)]
        if s.axis == 2: return s.full.at[:, pl.ds(pl.multiple_of(d * s.total + lo, 16), n)]
        return s.full.at[pl.ds(lo, n), pl.ds(pl.multiple_of(d * 128, 128), 128)]
    def send(s, kind, src, dst, dev):
        cp = pltpu.make_async_remote_copy(src, dst, s.ss.at[kind], s.rs.at[kind], device_id=dev, device_id_type=MESH)
        cp.start(); s.sends.append(cp)
    def got(s, kind, dst):
        pltpu.make_async_remote_copy(dst, dst, s.ss.at[kind], s.rs.at[kind], device_id=s.sib, device_id_type=MESH).wait_recv()
    def start(s):
        own = s.slot(0, 0)
        s.send(0, s.shard, own, s.up); s.send(1, s.shard, own, s.down); s.send(2, s.shard, own, s.z)
        s.send(8, s.shard, own, s.sib)
    def relay(s, rel):
        b = s.slot(*RELS[rel]); s.send(8 + rel, b, b, s.sib)
    def serve(s):
        a = s.slot(0, 3); s.got(0, a); h = s.slot(0, 3, half=0); s.send(5, h, h, s.up)
        b = s.slot(0, 1); s.got(1, b); h = s.slot(0, 1, half=1); s.send(6, h, h, s.down)
        z = s.slot(1, 0); s.got(2, z); s.send(3, z, z, s.up); s.send(4, z, z, s.down)
        s.relay(2); s.relay(1); s.relay(4)
    def serve2(s):
        s.got(5, s.slot(0, 2, half=0)); s.got(6, s.slot(0, 2, half=1))
        f = s.slot(0, 2); s.send(7, f, f, s.z); s.relay(3)
    def serve3(s):
        s.got(3, s.slot(1, 3)); s.relay(6)
        s.got(4, s.slot(1, 1)); s.relay(5)
        s.got(7, s.slot(1, 2)); s.relay(7)
    def arrived(s):
        for r in range(8): s.got(8 + r, s.slot(*RELS[r], c=1 - s.c))

f32 = jnp.float32
bf16 = jnp.bfloat16

def by_rows(rows, step, fn):
    def go(i, carry):
        fn(pl.ds(pl.multiple_of(i * step, step), step))
        return carry
    lax.fori_loop(0, rows // step, go, 0)

def add_into(dst, terms, rows, step, lo=0):
    def go(r):
        if lo: r = pl.ds(pl.multiple_of(r.start + lo, step), step)
        total = terms[0][r, :].astype(f32)
        for t in terms[1:]: total = total + t[r, :].astype(f32)
        dst[r, :] = total.astype(dst.dtype)
    by_rows(rows, step, go)

class Link:
    def __init__(s, ss, rs):
        s.ss, s.rs, s.sends = ss, rs, []
        c, y, zl, x, zh = s.at = place()
        s.c, s.y, s.zl, s.x, s.zh = s.at
        s.sib = peer(1 - c, y, zl, x, zh)
        s.yu, s.yd, s.yf = (peer(c, (y + k) % 4, zl, x, zh) for k in (1, 3, 2))
        s.zn = peer(c, y, 1 - zl, x, zh)
        s.xu, s.xd, s.xf = (peer(c, y, zl, (x + k) % 4, zh) for k in (1, 3, 2))
        s.zf = peer(c, y, zl, x, 1 - zh)
    def send(s, kind, src, dst, dev):
        cp = pltpu.make_async_remote_copy(src, dst, s.ss.at[kind], s.rs.at[kind], device_id=dev, device_id_type=MESH)
        cp.start(); s.sends.append(cp)
    def got(s, kind, dst):
        pltpu.make_async_remote_copy(dst, dst, s.ss.at[kind], s.rs.at[kind], device_id=s.sib, device_id_type=MESH).wait_recv()
    def drain(s):
        for cp in s.sends: cp.wait_send()

class TensorSum(Link):
    def __init__(s, b, f, t1, t2, zs, zr, ss, rs):
        super().__init__(ss, rs)
        s.b, s.f, s.t1, s.t2, s.zs, s.zr = b, f, t1, t2, zs, zr
    def blk(s, zh, dx): return s.b.at[zh * 4 + (s.x + dx) % 4]
    LO, HI = pl.ds(0, 64), pl.ds(64, 64)
    def start_far(s): s.send(0, s.blk(1 - s.zh, 2), s.f, s.zf)
    def start_near(s):
        o = 1 - s.zh
        s.send(1, s.blk(o, 1), s.t2.at[0, o], s.xu); s.send(2, s.blk(o, 3), s.t2.at[1, o], s.xd)
        s.send(3, s.blk(s.zh, 1).at[s.HI], s.t2.at[0, s.zh, s.HI], s.xu); s.send(4, s.blk(s.zh, 3).at[s.LO], s.t2.at[1, s.zh, s.LO], s.xd)
    def middle(s):
        s.got(0, s.f); add_into(s.f, [s.f, s.blk(s.zh, 2)], 128, 32)
        s.send(5, s.f.at[s.LO], s.t1.at[s.LO], s.xu); s.send(6, s.f.at[s.HI], s.t1.at[s.HI], s.xd)
    def middle2(s):
        s.got(5, s.t1.at[s.LO]); add_into(s.t1, [s.t1, s.blk(s.zh, 1)], 64, 32)
        s.send(7, s.t1.at[s.LO], s.t2.at[0, s.zh, s.LO], s.xu)
        s.got(6, s.t1.at[s.HI]); add_into(s.t1, [s.t1, s.blk(s.zh, 3)], 64, 32, lo=64)
        s.send(8, s.t1.at[s.HI], s.t2.at[1, s.zh, s.HI], s.xd)
    def last(s):
        o = 1 - s.zh
        s.got(1, s.t2.at[0, o]); s.got(2, s.t2.at[1, o])
        add_into(s.zs, [s.blk(o, 0), s.t2.at[0, o], s.t2.at[1, o]], 128, 32)
        s.send(9, s.zs, s.zr, s.zf)
    def total(s, r):
        return (s.blk(s.zh, 0)[r, :].astype(f32) + s.t2.at[0, s.zh][r, :].astype(f32)
                + s.t2.at[1, s.zh][r, :].astype(f32) + s.zr[r, :].astype(f32))
    def arrived(s):
        z = s.zh
        s.got(3, s.t2.at[0, z, s.HI]); s.got(4, s.t2.at[1, z, s.LO]); s.got(7, s.t2.at[0, z, s.LO]); s.got(8, s.t2.at[1, z, s.HI])
        s.got(9, s.zr)

class TensorGather(Link):
    def __init__(s, o, ss, rs):
        super().__init__(ss, rs); s.o = o
    def blk(s, zh, dx): return s.o.at[zh * 4 + (s.x + dx) % 4]
    LO, HI = pl.ds(0, 64), pl.ds(64, 64)
    def start(s, own):
        b = s.blk(s.zh, 0)
        s.send(0, own, b, s.xu); s.send(1, own, b, s.xd); s.send(2, own, b, s.zf)
    def middle(s):
        b = s.blk(s.zh, 3); s.got(0, b); s.send(3, b.at[s.LO], b.at[s.LO], s.xu)
        b = s.blk(s.zh, 1); s.got(1, b); s.send(4, b.at[s.HI], b.at[s.HI], s.xd)
        b = s.blk(1 - s.zh, 0); s.got(2, b); s.send(5, b, b, s.xu); s.send(6, b, b, s.xd)
    def far(s):
        b = s.blk(s.zh, 2); s.got(3, b.at[s.LO]); s.got(4, b.at[s.HI]); s.send(7, b, b, s.zf)
    def finish(s):
        o = 1 - s.zh
        s.got(5, s.blk(o, 3)); s.got(6, s.blk(o, 1)); s.got(7, s.blk(o, 2))

class SmallSum(Link):
    def __init__(s, v, rc, rz, ry, rx, rt, acc, out, ss, rs):
        super().__init__(ss, rs)
        s.v, s.rc, s.rz, s.ry, s.rx, s.rt, s.acc, s.out = v, rc, rz, ry, rx, rt, acc, out
    def a(s): s.send(0, s.v.at[1 - s.c], s.rc, s.sib)
    def b(s):
        s.got(0, s.rc); s.rc[...] = s.rc[...] + s.v[s.c]
        s.send(1, s.rc.at[1 - s.zl], s.rz, s.zn)
    def c_(s):
        s.got(1, s.rz); s.rz[...] = s.rz[...] + s.rc[s.zl]
        s.send(2, s.rz.at[(s.y + 1) % 4], s.ry.at[0], s.yu); s.send(3, s.rz.at[(s.y + 3) % 4], s.ry.at[1], s.yd)
        s.send(4, s.rz.at[(s.y + 2) % 4], s.ry.at[2], s.yf)
    def d(s):
        for k in range(3): s.got(2 + k, s.ry.at[k])
        s.acc[0] = s.rz[s.y] + s.ry[0] + s.ry[1] + s.ry[2]
        s.send(5, s.acc.at[0], s.rx.at[0], s.xu); s.send(6, s.acc.at[0], s.rx.at[1], s.xd); s.send(7, s.acc.at[0], s.rx.at[2], s.xf)
    def e(s):
        for k in range(3): s.got(5 + k, s.rx.at[k])
        s.acc[1] = s.acc[0] + s.rx[0] + s.rx[1] + s.rx[2]
        s.send(8, s.acc.at[1], s.rt, s.zf)
    def f(s):
        s.got(8, s.rt)
        first = lax.broadcasted_iota(jnp.int32, (16, 128), 0) < 2
        s.out[...] = jnp.where(first, s.acc[1] + s.rt[...], s.acc[0])

def peers_all():
    c, y, zl, x, zh = place()
    return ([peer(1 - c, y, zl, x, zh), peer(c, y, 1 - zl, x, zh), peer(c, y, zl, x, 1 - zh)]
            + [peer(c, (y + k) % 4, zl, x, zh) for k in (1, 2, 3)] + [peer(c, y, zl, (x + k) % 4, zh) for k in (1, 2, 3)])

def norm_back_rows(r, gn, tokens, cot, gain, out, sums):
    x = tokens[r, :].astype(f32)
    mean = jnp.mean(x, axis=-1, keepdims=True); cen = x - mean
    inv = lax.rsqrt(jnp.mean(cen * cen, axis=-1, keepdims=True) + 1e-5)
    xh = cen * inv
    n = x.shape[0] // 8
    sums[0] += jnp.sum((gn * xh).reshape(n, 8, 2048), axis=0)
    sums[1] += jnp.sum(gn.reshape(n, 8, 2048), axis=0)
    sc = gn * gain
    ig = cot[r, :].astype(f32) + inv * (sc - jnp.mean(sc, axis=-1, keepdims=True) - xh * jnp.mean(sc * xh, axis=-1, keepdims=True))
    out[r, :] = ig.astype(bf16)

PLAN = ("v0", "q0", "v1", "o0", "q1", "v2", "o1", "v3", "q2", "first", "u0", "o2", "vectors", "q3", "n0", "d0", "n1", "Aq", "n2", "u1",
        "Wq", "n3", "sn", "o3", "p0", "p1", "p2", "p3", "Ao", "d1", "Wo", "u2", "ga", "a3x", "a3y", "a2x", "u3", "d2", "a2y", "a1x",
        "a1y", "Au", "a0x", "a0y", "sa", "k", "sg", "Wu", "h0", "d3", "h1", "h2", "h3")

def NT(a, b): return lax.dot_general(a, b, (((1,), (1,)), ((), ())), preferred_element_type=f32)
def NN(a, b): return lax.dot_general(a, b, (((1,), (0,)), ((), ())), preferred_element_type=f32)
def TN(a, b): return lax.dot_general(a, b, (((0,), (0,)), ((), ())), preferred_element_type=f32)

def rotary_tables():
    pos = np.arange(LEN, dtype=np.float32)
    freq = (np.float32(rope_base) ** (-np.arange(0, ROT, 2, dtype=np.float32) / np.float32(ROT))).astype(np.float32)
    ang = (pos[:, None] * freq[None, :]).astype(np.float32)
    cos, sin = np.cos(ang).astype(np.float32), np.sin(ang).astype(np.float32)
    one, zero = np.ones((LEN, 32), np.float32), np.zeros((LEN, 16), np.float32)
    c = np.concatenate([cos, cos, one], 1)
    s1 = np.concatenate([-sin, zero, zero, zero], 1)
    s2 = np.concatenate([zero, sin, zero, zero], 1)
    return np.stack([np.concatenate([t, t], 1) for t in (c, s1, s2)])

def turn(u, tab, r, sign):
    other = pltpu.roll(u, 112, 1) * tab[1, r, :] + pltpu.roll(u, 16, 1) * tab[2, r, :]
    straight = u * tab[0, r, :]
    return straight + other if sign > 0 else straight - other


def pack(vec, gain, lbias, bout, bdown, bup, bqkv):
    dp = lax.axis_index("dp")
    k = lax.broadcasted_iota(jnp.int32, (64, 128), 0); l = lax.broadcasted_iota(jnp.int32, (64, 128), 1)
    up = NN(bup[...], ((l % 64 == k) & (l // 64 == dp % 2)).astype(bf16))
    k4 = k[0:4]; l4 = l[0:4]
    on = (l4 % 4 == k4) & ((l4 % 64) // 4 == dp)
    rows = [gain[...].astype(f32), lbias[...].astype(f32), bout[...].astype(f32), bdown[...].astype(f32), up]
    for j in range(3):
        lo = NN(bqkv[j], (on & (l4 < 64)).astype(bf16)); hi = NN(bqkv[j], (on & (l4 >= 64)).astype(bf16))
        rows += [lo[0:1] + hi[1:2], lo[2:3] + hi[3:4]]
    vec[...] = jnp.concatenate(rows + [jnp.zeros((21, 128), f32)], 0).astype(bf16)

def forward_kernel(gain_s, lbias_s, bout_s, bdown_s, bup_s, bqkv_s, wq, wout, wup, wdown, tok_h, cot_h, tab_h,
                   vecs, wq_f, wout_f, wup_f, wdown_f, rows_h, nrm_h, att_h, act_h, dact_h, gp_h,
                   vec, tab, vv, wqv, woutv, wupv, tok, cot, nrm, rowsv, bqkv, bup, q, k, v, ga, att, dk, dv, gp, act, dact,
                   ss, rs, ls, ld):
    c, y, zl, x, zh = place()
    loads = {}
    def load(i, src, dst):
        loads[i] = pltpu.make_async_copy(src, dst, ld.at[i]); loads[i].start()
    load(0, tok_h, tok); load(1, cot_h, cot); load(12, tab_h, tab)
    pack(vec, gain_s, lbias_s, bout_s, bdown_s, bup_s, bqkv_s)
    enter([peer(c, (y + 1) % 4, zl, x, zh), peer(c, (y + 3) % 4, zl, x, zh), peer(c, y, 1 - zl, x, zh), peer(1 - c, y, zl, x, zh)])
    gv, gq, go, gu, gd = every = [Gather(a, b, ax, ss.at[i], rs.at[i]) for i, (a, b, ax) in enumerate(
        [(vec, vecs, 0), (wq, wq_f, 2), (wout, wout_f, 1), (wup, wup_f, 0), (wdown, wdown_f, 1)])]
    local = [pltpu.make_async_copy(g.shard, g.slot(0, 0), ls.at[i]) for i, g in enumerate(every)]
    for cp in local: cp.start()

    def norm(lo, hi):
        gain, bias = rowsv[0:1, :], rowsv[1:2, :]
        def go_(i, carry):
            r = pl.ds(pl.multiple_of(lo + i * 32, 32), 32)
            a = tok[r, :].astype(f32)
            cen = a - jnp.mean(a, axis=-1, keepdims=True)
            inv = lax.rsqrt(jnp.mean(cen * cen, axis=-1, keepdims=True) + norm_epsilon)
            nrm[r, :] = (cen * inv * gain + bias).astype(bf16)
            return carry
        lax.fori_loop(0, (hi - lo) // 32, go_, 0)

    def project(lo, hi):
        def go_(i, carry):
            r = pl.ds(pl.multiple_of(lo + i * 256, 256), 256)
            n = nrm[r, :]
            for j, dst in enumerate((q, k, v)):
                p = NN(n, wqv[j])
                for h in range(2):
                    u = p[:, h * 128:(h + 1) * 128] + bqkv[2 * j + h:2 * j + h + 1, :]
                    dst[h, r, :] = (u if j == 2 else turn(u, tab, r, 1)).astype(bf16)
            return carry
        lax.fori_loop(0, (hi - lo) // 256, go_, 0)

    def grad_attended():
        def go_(i, carry):
            r = pl.ds(pl.multiple_of(i * 256, 256), 256)
            p = NT(cot[r, :], woutv[...])
            ga[0, r, :] = p[:, 0:128].astype(bf16); ga[1, r, :] = p[:, 128:256].astype(bf16)
            return carry
        lax.fori_loop(0, 4, go_, 0)

    def attention(i):
        lax.fori_loop(0, 2, lambda p, carry: attention_pair(i, p, carry), 0)
    def attention_pair(i, p, carry=0):
            n = (i + 1) * 256
            r = pl.ds(i * 256, 256)
            cols = pl.ds(pl.multiple_of(p * 128, 128), 128)
            a_, d_, tk, tv = 0.0, 0.0, 0.0, 0.0
            for hh in range(2):
                m = ((lax.broadcasted_iota(jnp.int32, (1, 128), 1) // 64) == hh).astype(bf16)
                kk = k[p, 0:n] * m; w = v[p, 0:n] * m; qq = q[p, r] * (m * 0.125); gg = ga[p, r] * m
                s = NT(kk, qq)
                key = lax.broadcasted_iota(jnp.int32, (256, 256), 0); row = lax.broadcasted_iota(jnp.int32, (256, 256), 1)
                diag = jnp.where(row >= key, s[n - 256:], -1e30)
                s = diag if i == 0 else jnp.concatenate([s[:n - 256], diag], 0)
                e = jnp.exp(s - jnp.max(s, 0, keepdims=True))
                pr = e * (1.0 / jnp.sum(e, 0, keepdims=True))
                low = pr.astype(bf16)
                dp = NT(w, gg)
                ds = (pr * (dp - jnp.sum(pr * dp, 0, keepdims=True))).astype(bf16)
                a_ = a_ + TN(low, w); d_ = d_ + TN(ds, kk)
                tk = tk + NN(ds, qq); tv = tv + NN(low, gg)
            att[r, cols] = a_.astype(bf16)
            gp[r, cols] = turn(d_ * 0.125, tab, r, -1).astype(bf16)
            if i == 3: dk[p] = tk; dv[p] = tv
            else:
                dk[p, 0:n] += tk; dv[p, 0:n] += tv
            return carry

    def keys_done():
        def go_(i, carry):
            r = pl.ds(pl.multiple_of(i * 256, 256), 256)
            for p in range(2):
                gp[r, 256 + p * 128:384 + p * 128] = turn(dk[p, r], tab, r, -1).astype(bf16)
                gp[r, 512 + p * 128:640 + p * 128] = dv[p, r].astype(bf16)
            return carry
        lax.fori_loop(0, 4, go_, 0)

    def hidden(lo, hi):
        def go_(i, carry):
            r = pl.ds(pl.multiple_of(lo + i * 256, 256), 256)
            n = nrm[r, :]
            for j in range(4):
                cols = pl.ds(j * 256, 256)
                h = NN(n, wupv[:, cols]) + bup[0:1, cols]
                h2 = h * h
                t = jnp.tanh(0.7978845608028654 * h * (1.0 + 0.044715 * h2))
                act[r, cols] = (0.5 * h * (1.0 + t)).astype(bf16)
                dact[r, cols] = (0.5 * (1.0 + t) + 0.5 * h * (1.0 - t * t) * (0.7978845608028654 * (1.0 + 0.134145 * h2))).astype(bf16)
            return carry
        lax.fori_loop(0, (hi - lo) // 256, go_, 0)

    def first():
        gv.arrived(); local[0].wait(); load(2, vecs, vv)
    def vectors():
        loads[2].wait(); loads[0].wait()
        bq, bu = jnp.zeros((6, 128), f32), None
        for d in range(16):
            t = vv[pl.ds(d * 32, 32), :].astype(f32)
            cols = pl.ds(d * 128, 128)
            rowsv[0:1, cols] = t[0:1]; rowsv[1:2, cols] = t[1:2]; rowsv[2:3, cols] = t[2:3] + t[3:4]
            bq = bq + t[5:11]
            if d % 2 == 0: bu = t[4:5]
            else: bup[0:1, pl.ds((d // 2) * 128, 128)] = bu + t[4:5]
        bqkv[0:6, :] = bq
        load(6, rowsv, rows_h)
    def have_q():
        gq.arrived(); local[1].wait(); load(3, wq_f, wqv)
    def have_o():
        go.arrived(); local[2].wait(); load(4, wout_f, woutv)
    def have_u():
        gu.arrived(); local[3].wait(); load(7, wup_f, wupv)
    steps = {"first": first, "vectors": vectors, "Aq": have_q, "Ao": have_o, "Au": have_u,
             "Wq": lambda: (loads[3].wait(), loads[12].wait()), "Wo": lambda: (loads[4].wait(), loads[1].wait()), "Wu": lambda: loads[7].wait(),
             "ga": grad_attended, "k": keys_done, "sn": lambda: load(5, nrm, nrm_h), "sa": lambda: load(8, att, att_h), "sg": lambda: load(9, gp, gp_h)}
    for i in range(4):
        steps["n%d" % i] = partial(norm, i * 256, i * 256 + 256)
        steps["p%d" % i] = partial(project, i * 256, i * 256 + 256)
        steps["h%d" % i] = partial(hidden, i * 256, i * 256 + 256)
        steps["a%d" % i] = partial(attention, i)
        for p in range(2): steps["a%d%s" % (i, "xy"[p])] = partial(attention_pair, i, p)
    for nm, g in (("v", gv), ("q", gq), ("o", go), ("u", gu), ("d", gd)):
        steps[nm + "0"], steps[nm + "1"], steps[nm + "2"], steps[nm + "3"] = g.start, g.serve, g.serve2, g.serve3
    for name in PLAN: steps[name]()
    load(10, act, act_h); load(11, dact, dact_h)
    gd.arrived()
    for i in (5, 6, 8, 9, 10, 11): loads[i].wait()
    local[4].wait()
    for g in (gv, gq, go, gu, gd):
        for cp in g.sends: cp.wait_send()

def forward(vectors, wq, wout, wup, wdown, tokens, cot, tab):
    A = pl.BlockSpec(memory_space=pl.ANY); V = pl.BlockSpec(memory_space=pltpu.VMEM)
    S = jax.ShapeDtypeStruct
    vm = lambda sh, t=bf16: pltpu.VMEM(sh, t)
    return pl.pallas_call(forward_kernel,
        out_shape=[S((512, 128), bf16), S((3, 2048, 256), bf16), S((256, 2048), bf16), S((2048, 1024), bf16), S((1024, 2048), bf16),
                   S((8, 2048), f32), S((1024, 2048), bf16), S((1024, 256), bf16), S((1024, 1024), bf16), S((1024, 1024), bf16), S((1024, 768), bf16)],
        in_specs=[V] * 6 + [A] * 7, out_specs=[A] * 11,
        scratch_shapes=[vm((32, 128)), vm((3, 1024, 128), f32), vm((512, 128)), vm((3, 2048, 256)), vm((256, 2048)), vm((2048, 1024)), vm((1024, 2048)), vm((1024, 2048)), vm((1024, 2048)),
                        vm((8, 2048), f32), vm((8, 128), f32), vm((8, 1024), f32), vm((2, 1024, 128)), vm((2, 1024, 128)), vm((2, 1024, 128)), vm((2, 1024, 128)),
                        vm((1024, 256)), vm((2, 1024, 128), f32), vm((2, 1024, 128), f32), vm((1024, 768)), vm((1024, 1024)), vm((1024, 1024)),
                        pltpu.SemaphoreType.DMA((5, 16)), pltpu.SemaphoreType.DMA((5, 16)), pltpu.SemaphoreType.DMA((5,)), pltpu.SemaphoreType.DMA((13,))],
        compiler_params=pltpu.CompilerParams(collective_id=1, has_side_effects=True, vmem_limit_bytes=60 << 20),
        name="gather_and_forward")(*vectors, wq, wout, wup, wdown, tokens, cot, tab)

class Scatter(Link):
    def __init__(s, g, sib, mid, ss, rs, width):
        super().__init__(ss, rs)
        s.g, s.b, s.m, s.w = g, sib, mid, width
    def to_sibling(s, k):
        return pltpu.make_async_remote_copy(s.g.at[k, 1 - s.c, :, pl.ds(0, s.w)], s.b.at[k], s.ss.at[k], s.rs.at[k],
                                            device_id=s.sib, device_id_type=MESH)
    def produce(s, lhs, rhs_list):
        def go(k, carry):
            chip = (k % 2) * 4 + (s.y + 2 + 3 * (k // 2)) % 4
            a = lhs[:, pl.ds(pl.multiple_of(chip * 256, 256), 256)]
            at = 0
            for rhs in rhs_list:
                n = rhs.shape[1]
                for lo in range(0, n, 512):
                    w = min(512, n - lo)
                    p = TN(a, rhs[:, lo:lo + w]).astype(bf16)
                    s.g[k, 0, :, at:at + w] = p[0:128]; s.g[k, 1, :, at:at + w] = p[128:256]
                    at += w
            s.to_sibling(k).start()
            return carry
        lax.fori_loop(0, 8, go, 0)
    def pairs(s):
        def go(k, carry):
            s.to_sibling(k).wait()
            mine = s.g.at[k, s.c]; dst = s.b.at[k]
            def rows(i, cc):
                r = pl.ds(pl.multiple_of(i * 32, 32), 32)
                dst[r, :] = (dst[r, :].astype(f32) + mine[r, 0:s.w].astype(f32)).astype(bf16)
                return cc
            lax.fori_loop(0, 4, rows, 0)
            return carry
        lax.fori_loop(0, 8, go, 0)
    def serve1(s):
        s.send(8, s.b.at[0], s.m.at[0], s.yu); s.send(9, s.b.at[1], s.m.at[1], s.yd)
        s.send(10, s.b.at[3], s.m.at[4], s.yu); s.send(11, s.b.at[6], s.m.at[2], s.yd)
    def serve2(s):
        s.got(8, s.m.at[0]); add_into(s.b.at[2], [s.b.at[2], s.m.at[0]], 128, 32); s.send(12, s.b.at[2], s.m.at[3], s.yu)
        s.got(9, s.m.at[1]); add_into(s.b.at[7], [s.b.at[7], s.m.at[1]], 128, 32); s.send(13, s.b.at[7], s.m.at[5], s.yd)
    def serve3(s):
        for k, j in ((10, 4), (11, 2), (12, 3), (13, 5)): s.got(k, s.m.at[j])
        o = 1 - s.zl; b = s.b.at[4 + o]
        add_into(b, [b, s.m.at[2 + 2 * o], s.m.at[3 + 2 * o]], 128, 32); s.send(14, b, s.m.at[6], s.zn)
    def serve4(s, put):
        s.got(14, s.m.at[6])
        z = s.zl
        terms = (s.b.at[4 + z], s.m.at[2 + 2 * z], s.m.at[3 + 2 * z], s.m.at[6])
        def go(r):
            t = terms[0][r, :].astype(f32)
            for q in terms[1:]: t = t + q[r, :].astype(f32)
            put(r, t)
        by_rows(128, 32, go)

def backward_kernel(wq_f, wout_f, wup_f, wdown_f, rows_h, nrm_h, att_h, act_h, dact_h, gp_h, cot_h, tok_h,
                    mixed, ingrad, o2, oup, oq, osv,
                    woutv, wdownv, wqc, wuc, cot, nrm, att, act, gh, gp, rowsv, tok, brp, gnp, own,
                    fa, t1a, t2a, zsa, zra, fb, t1b, t2b, zsb, zrb, g, sib2, m2, sibu, mu, sibq, mq,
                    v, rc, rz, ry, rx, rt, acc, sums, ss, rs, ld):
    c, y, zl, x, zh = place()
    t_own = zh * 4 + x
    loads = {}
    def load(i, src, dst):
        loads[i] = pltpu.make_async_copy(src, dst, ld.at[i]); loads[i].start()
    load(0, att_h, att); load(1, act_h, act); load(2, wout_f, woutv); load(3, wdown_f, wdownv)
    load(4, cot_h, cot); load(5, dact_h, gh); load(6, gp_h, gp); load(7, nrm_h, nrm); load(8, rows_h, rowsv)
    load(9, tok_h.at[pl.ds(pl.multiple_of(t_own * 128, 128), 128)], tok)
    def chunk(j):
        s = j % 2; r = pl.ds(j * 256, 256)
        load(10 + 2 * s, wq_f.at[:, r], wqc.at[s]); load(11 + 2 * s, wup_f.at[r], wuc.at[s])
    chunk(0); chunk(1)
    enter(peers_all())
    bs = TensorSum(brp, fa, t1a, t2a, zsa, zra, ss.at[0], rs.at[0])
    gs = TensorSum(gnp, fb, t1b, t2b, zsb, zrb, ss.at[1], rs.at[1])
    mg = TensorGather(mixed, ss.at[2], rs.at[2])
    ig = TensorGather(ingrad, ss.at[3], rs.at[3])
    s2 = Scatter(g, sib2, m2, ss.at[4], rs.at[4], 1280)
    su = Scatter(g, sibu, mu, ss.at[5], rs.at[5], 1024)
    sq = Scatter(g, sibq, mq, ss.at[6], rs.at[6], 768)
    sm = SmallSum(v, rc, rz, ry, rx, rt, acc, osv, ss.at[7], rs.at[7])

    def branch(a, b):
        ra, rb = (pl.ds(pl.multiple_of(t * 128, 128), 128) for t in (a, b))
        la = jnp.concatenate([att[ra, :], att[rb, :]], 0); lb = jnp.concatenate([act[ra, :], act[rb, :]], 0)
        def go(j, carry):
            cols = pl.ds(pl.multiple_of(j * 512, 512), 512)
            p = (NN(la, woutv[:, cols]) + NN(lb, wdownv[:, cols])).astype(bf16)
            brp[a, :, cols] = p[0:128]; brp[b, :, cols] = p[128:256]
            return carry
        lax.fori_loop(0, 4, go, 0)
    def grad_hidden():
        def go(i, carry):
            r = pl.ds(pl.multiple_of(i * 256, 256), 256)
            gr = cot[r, :]
            for j in range(2):
                cols = pl.ds(j * 512, 512)
                p = NT(gr, wdownv[cols, :])
                gh[r, cols] = (p * gh[r, cols].astype(f32)).astype(bf16)
            return carry
        lax.fori_loop(0, 4, go, 0)
    def grad_normed(j):
        s = j % 2
        loads[10 + 2 * s].wait(); loads[11 + 2 * s].wait()
        def go(i, carry):
            r = pl.ds(pl.multiple_of(i * 256, 256), 256)
            p = NT(gh[r, :], wuc[s])
            for e in range(3): p = p + NT(gp[r, e * 256:(e + 1) * 256], wqc[s, e])
            p = p.astype(bf16)
            gnp[2 * i, :, j * 256:(j + 1) * 256] = p[0:128]; gnp[2 * i + 1, :, j * 256:(j + 1) * 256] = p[128:256]
            return carry
        lax.fori_loop(0, 4, go, 0)
        if j + 2 < 8: chunk(j + 2)
    def bias_sums():
        ones = jnp.ones((16, 1024), bf16)
        for d in range(8):
            w = v.at[:, d // 4, d % 4]
            gb = NN(ones, cot[:, d * 256:(d + 1) * 256])[0:1]
            gu_ = NN(ones, gh[:, d * 128:(d + 1) * 128])[0:1]
            for cc in range(2):
                w[cc, 2:3, :] = gb[:, cc * 128:(cc + 1) * 128]; w[cc, 3:4, :] = gu_
        for j in range(3):
            gqb = NN(ones, gp[:, j * 256:(j + 1) * 256])[0:1]
            for d in range(16):
                w = v.at[d % 2, d // 8, (d // 2) % 4]
                w[4 + 2 * j:5 + 2 * j, :] = gqb[:, 0:128]; w[5 + 2 * j:6 + 2 * j, :] = gqb[:, 128:256]
    def mix(r): own[0, r, :] = (tok[r, :].astype(f32) + bs.total(r) + rowsv[2:3, :]).astype(bf16)
    def norm_back():
        sums[...] = jnp.zeros_like(sums)
        cot_own = cot.at[pl.ds(pl.multiple_of(t_own * 128, 128), 128)]
        by_rows(128, 16, lambda r: norm_back_rows(r, gs.total(r), tok, cot_own, rowsv[0:1, :], own.at[1], sums))
    def norm_sums():
        sg = jnp.sum(sums[0], axis=0, keepdims=True); sb = jnp.sum(sums[1], axis=0, keepdims=True)
        for d in range(16):
            w = v.at[d % 2, d // 8, (d // 2) % 4]
            w[0:1, :] = sg[:, d * 128:(d + 1) * 128]; w[1:2, :] = sb[:, d * 128:(d + 1) * 128]
    def put2(r, t): o2[r, :] = t
    def putu(r, t): oup[r, :] = t
    def putq(r, t): oq[r, :] = t
    xp = lambda k: (x + k) % 4
    o = 1 - zh

    for i in (0, 1, 2, 3): loads[i].wait()
    branch(o * 4 + xp(2), zh * 4 + xp(2)); bs.start_far()
    branch(o * 4 + xp(1), o * 4 + xp(3)); branch(zh * 4 + xp(1), zh * 4 + xp(3)); bs.start_near()
    branch(o * 4 + xp(0), zh * 4 + xp(0))
    loads[4].wait(); loads[5].wait()
    grad_hidden()
    s2.produce(cot, [att, act])
    bs.middle(); bs.last()
    s2.pairs(); s2.serve1()
    loads[6].wait()
    for j in range(4): grad_normed(j)
    bs.middle2()
    for j in range(4, 8): grad_normed(j)
    gs.start_far(); gs.start_near()
    s2.serve2()
    loads[7].wait()
    su.produce(nrm, [gh]); su.pairs(); su.serve1()
    sq.produce(nrm, [gp]); sq.pairs(); sq.serve1()
    s2.serve3()
    gs.middle()
    bias_sums()
    su.serve2()
    gs.last()
    loads[8].wait(); loads[9].wait()
    sq.serve2()
    gs.middle2()
    bs.arrived(); by_rows(128, 32, mix)
    load(14, own.at[0], mixed.at[t_own])
    mg.start(own.at[0])
    s2.serve4(put2); su.serve3(); sq.serve3()
    gs.arrived(); norm_back()
    load(15, own.at[1], ingrad.at[t_own])
    ig.start(own.at[1])
    norm_sums(); sm.a()
    mg.middle()
    su.serve4(putu)
    sm.b()
    sq.serve4(putq)
    sm.c_(); mg.far(); sm.d(); ig.middle(); sm.e()
    ig.far(); sm.f(); mg.finish(); ig.finish()
    loads[14].wait(); loads[15].wait()
    for w in (gs, bs, mg, ig, s2, su, sq, sm): w.drain()

def backward(wq_f, wout_f, wup_f, wdown_f, rows, nrm, att, act, dact, gp, cot, tok):
    S = jax.ShapeDtypeStruct
    vm = lambda sh, t=bf16: pltpu.VMEM(sh, t)
    tsum = [vm((128, 2048)), vm((128, 2048)), vm((2, 2, 128, 2048)), vm((128, 2048)), vm((128, 2048))]
    A = pl.BlockSpec(memory_space=pl.ANY); V = pl.BlockSpec(memory_space=pltpu.VMEM)
    return pl.pallas_call(backward_kernel,
        out_shape=[S((8, 128, 2048), bf16)] * 2 + [S((128, 1280), f32), S((128, 1024), f32), S((128, 768), f32), S((16, 128), f32)],
        in_specs=[A] * 12, out_specs=[A] * 2 + [V] * 4,
        scratch_shapes=[vm((256, 2048)), vm((1024, 2048)), vm((2, 3, 256, 256)), vm((2, 256, 1024)), vm((1024, 2048)), vm((1024, 2048)), vm((1024, 256)), vm((1024, 1024)), vm((1024, 1024)),
                        vm((1024, 768)), vm((8, 2048), f32), vm((128, 2048)), vm((8, 128, 2048)), vm((8, 128, 2048)), vm((2, 128, 2048))]
        + tsum + tsum + [vm((8, 2, 128, 1280)), vm((8, 128, 1280)), vm((7, 128, 1280)), vm((8, 128, 1024)), vm((7, 128, 1024)), vm((8, 128, 768)), vm((7, 128, 768)),
            vm((2, 2, 4, 16, 128), f32), vm((2, 4, 16, 128), f32), vm((4, 16, 128), f32), vm((3, 16, 128), f32), vm((3, 16, 128), f32), vm((16, 128), f32),
            vm((2, 16, 128), f32), vm((2, 8, 2048), f32),
            pltpu.SemaphoreType.DMA((8, 16)), pltpu.SemaphoreType.DMA((8, 16)), pltpu.SemaphoreType.DMA((16,))],
        compiler_params=pltpu.CompilerParams(collective_id=2, has_side_effects=True, vmem_limit_bytes=64 << 20),
        name="backward_and_sums")(wq_f, wout_f, wup_f, wdown_f, rows, nrm, att, act, dact, gp, cot, tok)

def hand_over_kernel(mixed, ingrad, o2, oup, oq, osv, mo, io, gg, gb, gq, gbq, go, gbo, gu, gbu, gd, gbd, big, li, lo):
    dp = lax.axis_index("dp")
    ins = [pltpu.make_async_copy((mixed, ingrad)[i // 8].at[i % 8], big.at[i], li.at[i]) for i in range(16)]
    for cp in ins: cp.start()
    gg[...] = osv[0:1, :]; gb[...] = osv[1:2, :]; gbo[...] = osv[2:3, :]; gbd[...] = osv[2:3, :]
    for j in range(3): gq[j] = oq[:, j * 256:(j + 1) * 256]
    for b in range(10):
        t = o2[:, b * 128:(b + 1) * 128].T
        if b < 2: go[b * 128:(b + 1) * 128, :] = t
        else: gd[(b - 2) * 128:(b - 1) * 128, :] = t
    gu[...] = oup[...]
    l = lax.broadcasted_iota(jnp.int32, (128, 64), 0); k = lax.broadcasted_iota(jnp.int32, (128, 64), 1)
    gbu[...] = lax.dot_general(osv[3:4, :], (l == k + 64 * (dp % 2)).astype(f32), (((1,), (0,)), ((), ())), precision=lax.Precision.HIGHEST)
    l = lax.broadcasted_iota(jnp.int32, (128, 4), 0); k = lax.broadcasted_iota(jnp.int32, (128, 4), 1)
    for j in range(3):
        rows = osv[4 + 2 * j:6 + 2 * j, :]
        lo_, hi_ = (lax.dot_general(rows, (l == k + 4 * dp + 64 * h).astype(f32), (((1,), (0,)), ((), ())), precision=lax.Precision.HIGHEST) for h in (0, 1))
        gbq[j] = jnp.concatenate([lo_[0:1], hi_[0:1], lo_[1:2], hi_[1:2]], 0)
    outs = []
    for i in range(16):
        ins[i].wait()
        cp = pltpu.make_async_copy(big.at[i], (mo, io)[i // 8].at[pl.ds((i % 8) * 128, 128)], lo.at[i]); cp.start(); outs.append(cp)
    for cp in outs: cp.wait()

def hand_over(mixed, ingrad, o2, oup, oq, osv):
    S = jax.ShapeDtypeStruct
    A = pl.BlockSpec(memory_space=pl.ANY)
    full = lambda sh: pl.BlockSpec(sh, lambda: (0,) * len(sh))
    ins = [(128, 1280), (128, 1024), (128, 768), (16, 128)]
    outs = [(1, 128), (1, 128), (3, 128, 256), (3, 4, 4), (256, 128), (1, 128), (128, 1024), (1, 64), (1024, 128), (1, 128)]
    return pl.pallas_call(hand_over_kernel,
        out_shape=[S((1024, 2048), bf16)] * 2 + [S(sh, f32) for sh in outs],
        in_specs=[A] * 2 + [full(sh) for sh in ins], out_specs=[A] * 2 + [full(sh) for sh in outs],
        scratch_shapes=[pltpu.VMEM((16, 128, 2048), bf16), pltpu.SemaphoreType.DMA((16,)), pltpu.SemaphoreType.DMA((16,))],
        compiler_params=pltpu.CompilerParams(vmem_limit_bytes=40 << 20),
        name="hand_over")(mixed, ingrad, o2, oup, oq, osv)

def body(tokens, ln_gain, ln_bias, w_qkv, b_qkv, w_out, b_out, w_up, b_up, w_down, b_down, cotangent):
    row = lambda a: a.reshape(1, 128)
    vecs, wq_f, wout_f, wup_f, wdown_f, rows, nrm, att, act, dact, gp = forward(
        (row(ln_gain), row(ln_bias), row(b_out), row(b_down), b_up, b_qkv), w_qkv.transpose(1, 0, 2), w_out, w_up, w_down,
        tokens, cotangent, jnp.asarray(rotary_tables()))
    parts = backward(wq_f, wout_f, wup_f, wdown_f, rows, nrm, att, act, dact, gp, cotangent, tokens)
    mixed, ingrad, gg, gb, gq, gbq, go, gbo, gu, gbu, gd, gbd = hand_over(*parts)
    return (mixed, ingrad, gg.reshape(128), gb.reshape(128), gq.transpose(1, 0, 2), gbq, go, gbo.reshape(128), gu, gbu, gd, gbd.reshape(128))


def solution(mesh):
    in_specs = (
        P("dp", None),
        P("dp"),
        P("dp"),
        P("dp", None, "tensor"),
        P(None, "tensor", "dp"),
        P("tensor", "dp"),
        P("dp"),
        P("dp", "tensor"),
        P("tensor", "dp"),
        P("tensor", "dp"),
        P("dp"),
        P("dp", None),
    )
    out_specs = (
        P("dp", None),
        P("dp", None),
        P("dp"),
        P("dp"),
        P("dp", None, "tensor"),
        P(None, "tensor", "dp"),
        P("tensor", "dp"),
        P("dp"),
        P("dp", "tensor"),
        P("tensor", "dp"),
        P("tensor", "dp"),
        P("dp"),
    )
    return jax.shard_map(body, mesh=mesh, in_specs=in_specs, out_specs=out_specs, check_vma=False)
```

```python
from functools import partial

import jax
import jax.numpy as jnp
import numpy as np
from jax import lax
from jax.sharding import PartitionSpec as P
from jax.experimental import pallas as pl
from jax.experimental.pallas import tpu as pltpu

HD = 64
ROT = 32
LEN = 1024
norm_epsilon = 1e-05
rope_base = 10000.0
MESH = pl.DeviceIdType.MESH

def place():
    dp = lax.axis_index("dp"); tn = lax.axis_index("tensor")
    return dp % 2, (dp // 2) % 4, dp // 8, tn % 4, tn // 4

def peer(c, y, zl, x, zh):
    return (zl * 8 + y * 2 + c, zh * 4 + x)

RELS = [(0, 0), (0, 1), (0, 3), (0, 2), (1, 0), (1, 1), (1, 3), (1, 2)]

def enter(devices):
    bar = pltpu.get_barrier_semaphore()
    for d in devices:
        pl.semaphore_signal(bar, inc=1, device_id=d, device_id_type=MESH)
    pl.semaphore_wait(bar, len(devices))

class Gather:
    def __init__(s, shard, full, axis, ss, rs):
        s.axis, s.ss, s.rs, s.full = axis, ss, rs, full
        s.c, s.y, s.zl, x, zh = place()
        c, y, zl = s.c, s.y, s.zl
        s.total = shard.shape[1 if axis == 2 else 0]
        s.shard = shard
        s.up = peer(c, (y + 1) % 4, zl, x, zh); s.down = peer(c, (y + 3) % 4, zl, x, zh)
        s.z = peer(c, y, 1 - zl, x, zh); s.sib = peer(1 - c, y, zl, x, zh)
        s.sends = []
    def slot(s, dz, dy, c=None, half=None):
        c = s.c if c is None else c
        d = ((s.zl + dz) % 2) * 8 + ((s.y + dy) % 4) * 2 + c
        n = s.total if half is None else s.total // 2
        lo = 0 if half is None else half * n
        if s.axis == 0: return s.full.at[pl.ds(pl.multiple_of(d * s.total + lo, 16), n)]
        if s.axis == 2: return s.full.at[:, pl.ds(pl.multiple_of(d * s.total + lo, 16), n)]
        return s.full.at[pl.ds(lo, n), pl.ds(pl.multiple_of(d * 128, 128), 128)]
    def send(s, kind, src, dst, dev):
        cp = pltpu.make_async_remote_copy(src, dst, s.ss.at[kind], s.rs.at[kind], device_id=dev, device_id_type=MESH)
        cp.start(); s.sends.append(cp)
    def got(s, kind, dst):
        pltpu.make_async_remote_copy(dst, dst, s.ss.at[kind], s.rs.at[kind], device_id=s.sib, device_id_type=MESH).wait_recv()
    def start(s):
        own = s.slot(0, 0)
        s.send(0, s.shard, own, s.up); s.send(1, s.shard, own, s.down); s.send(2, s.shard, own, s.z)
        s.send(8, s.shard, own, s.sib)
    def relay(s, rel):
        b = s.slot(*RELS[rel]); s.send(8 + rel, b, b, s.sib)
    def serve(s):
        a = s.slot(0, 3); s.got(0, a); h = s.slot(0, 3, half=0); s.send(5, h, h, s.up)
        b = s.slot(0, 1); s.got(1, b); h = s.slot(0, 1, half=1); s.send(6, h, h, s.down)
        z = s.slot(1, 0); s.got(2, z); s.send(3, z, z, s.up); s.send(4, z, z, s.down)
        s.relay(2); s.relay(1); s.relay(4)
    def serve2(s):
        s.got(5, s.slot(0, 2, half=0)); s.got(6, s.slot(0, 2, half=1))
        f = s.slot(0, 2); s.send(7, f, f, s.z); s.relay(3)
    def serve3(s):
        s.got(3, s.slot(1, 3)); s.relay(6)
        s.got(4, s.slot(1, 1)); s.relay(5)
        s.got(7, s.slot(1, 2)); s.relay(7)
    def arrived(s):
        for r in range(8): s.got(8 + r, s.slot(*RELS[r], c=1 - s.c))

f32 = jnp.float32
bf16 = jnp.bfloat16

def by_rows(rows, step, fn):
    def go(i, carry):
        fn(pl.ds(pl.multiple_of(i * step, step), step))
        return carry
    lax.fori_loop(0, rows // step, go, 0)

def add_into(dst, terms, rows, step, lo=0):
    def go(r):
        if lo: r = pl.ds(pl.multiple_of(r.start + lo, step), step)
        total = terms[0][r, :].astype(f32)
        for t in terms[1:]: total = total + t[r, :].astype(f32)
        dst[r, :] = total.astype(dst.dtype)
    by_rows(rows, step, go)

class Link:
    def __init__(s, ss, rs):
        s.ss, s.rs, s.sends = ss, rs, []
        c, y, zl, x, zh = s.at = place()
        s.c, s.y, s.zl, s.x, s.zh = s.at
        s.sib = peer(1 - c, y, zl, x, zh)
        s.yu, s.yd, s.yf = (peer(c, (y + k) % 4, zl, x, zh) for k in (1, 3, 2))
        s.zn = peer(c, y, 1 - zl, x, zh)
        s.xu, s.xd, s.xf = (peer(c, y, zl, (x + k) % 4, zh) for k in (1, 3, 2))
        s.zf = peer(c, y, zl, x, 1 - zh)
    def send(s, kind, src, dst, dev):
        cp = pltpu.make_async_remote_copy(src, dst, s.ss.at[kind], s.rs.at[kind], device_id=dev, device_id_type=MESH)
        cp.start(); s.sends.append(cp)
    def got(s, kind, dst):
        pltpu.make_async_remote_copy(dst, dst, s.ss.at[kind], s.rs.at[kind], device_id=s.sib, device_id_type=MESH).wait_recv()
    def drain(s):
        for cp in s.sends: cp.wait_send()

class TensorSum(Link):
    def __init__(s, b, f, t1, t2, zs, zr, ss, rs):
        super().__init__(ss, rs)
        s.b, s.f, s.t1, s.t2, s.zs, s.zr = b, f, t1, t2, zs, zr
    def blk(s, zh, dx): return s.b.at[zh * 4 + (s.x + dx) % 4]
    LO, HI = pl.ds(0, 64), pl.ds(64, 64)
    def start_far(s): s.send(0, s.blk(1 - s.zh, 2), s.f, s.zf)
    def start_near(s):
        o = 1 - s.zh
        s.send(1, s.blk(o, 1), s.t2.at[0, o], s.xu); s.send(2, s.blk(o, 3), s.t2.at[1, o], s.xd)
    def start_near2(s):
        s.send(3, s.blk(s.zh, 1).at[s.HI], s.t2.at[0, s.zh, s.HI], s.xu); s.send(4, s.blk(s.zh, 3).at[s.LO], s.t2.at[1, s.zh, s.LO], s.xd)
    def middle(s):
        s.got(0, s.f); add_into(s.f, [s.f, s.blk(s.zh, 2)], 128, 32)
        s.send(5, s.f.at[s.LO], s.t1.at[s.LO], s.xu); s.send(6, s.f.at[s.HI], s.t1.at[s.HI], s.xd)
    def middle2(s):
        s.got(5, s.t1.at[s.LO]); add_into(s.t1, [s.t1, s.blk(s.zh, 1)], 64, 32)
        s.send(7, s.t1.at[s.LO], s.t2.at[0, s.zh, s.LO], s.xu)
        s.got(6, s.t1.at[s.HI]); add_into(s.t1, [s.t1, s.blk(s.zh, 3)], 64, 32, lo=64)
        s.send(8, s.t1.at[s.HI], s.t2.at[1, s.zh, s.HI], s.xd)
    def last(s):
        o = 1 - s.zh
        s.got(1, s.t2.at[0, o]); s.got(2, s.t2.at[1, o])
        add_into(s.zs, [s.blk(o, 0), s.t2.at[0, o], s.t2.at[1, o]], 128, 32)
        s.send(9, s.zs, s.zr, s.zf)
    def total(s, r):
        return (s.blk(s.zh, 0)[r, :].astype(f32) + s.t2.at[0, s.zh][r, :].astype(f32)
                + s.t2.at[1, s.zh][r, :].astype(f32) + s.zr[r, :].astype(f32))
    def arrived(s):
        z = s.zh
        s.got(3, s.t2.at[0, z, s.HI]); s.got(4, s.t2.at[1, z, s.LO]); s.got(7, s.t2.at[0, z, s.LO]); s.got(8, s.t2.at[1, z, s.HI])
        s.got(9, s.zr)

class TensorGather(Link):
    def __init__(s, o, ss, rs):
        super().__init__(ss, rs); s.o = o
    def blk(s, zh, dx): return s.o.at[zh * 4 + (s.x + dx) % 4]
    LO, HI = pl.ds(0, 64), pl.ds(64, 64)
    def start(s, own):
        b = s.blk(s.zh, 0)
        s.send(0, own, b, s.xu); s.send(1, own, b, s.xd); s.send(2, own, b, s.zf)
    def middle(s):
        b = s.blk(s.zh, 3); s.got(0, b); s.send(3, b.at[s.LO], b.at[s.LO], s.xu)
        b = s.blk(s.zh, 1); s.got(1, b); s.send(4, b.at[s.HI], b.at[s.HI], s.xd)
    def plane(s):
        b = s.blk(1 - s.zh, 0); s.got(2, b); s.send(5, b, b, s.xu); s.send(6, b, b, s.xd)
    def far(s):
        b = s.blk(s.zh, 2); s.got(3, b.at[s.LO]); s.got(4, b.at[s.HI]); s.send(7, b, b, s.zf)
    def finish(s):
        o = 1 - s.zh
        s.got(5, s.blk(o, 3)); s.got(6, s.blk(o, 1)); s.got(7, s.blk(o, 2))

class SmallSum(Link):
    def __init__(s, v, rc, rz, ry, rx, rt, acc, out, ss, rs):
        super().__init__(ss, rs)
        s.v, s.rc, s.rz, s.ry, s.rx, s.rt, s.acc, s.out = v, rc, rz, ry, rx, rt, acc, out
    def a(s): s.send(0, s.v.at[1 - s.c], s.rc, s.sib)
    def b(s):
        s.got(0, s.rc); s.rc[...] = s.rc[...] + s.v[s.c]
        s.send(1, s.rc.at[1 - s.zl], s.rz, s.zn)
    def c_(s):
        s.got(1, s.rz); s.rz[...] = s.rz[...] + s.rc[s.zl]
        s.send(2, s.rz.at[(s.y + 1) % 4], s.ry.at[0], s.yu); s.send(3, s.rz.at[(s.y + 3) % 4], s.ry.at[1], s.yd)
        s.send(4, s.rz.at[(s.y + 2) % 4], s.ry.at[2], s.yf)
    def d(s):
        for k in range(3): s.got(2 + k, s.ry.at[k])
        s.acc[0] = s.rz[s.y] + s.ry[0] + s.ry[1] + s.ry[2]
        s.send(5, s.acc.at[0], s.rx.at[0], s.xu); s.send(6, s.acc.at[0], s.rx.at[1], s.xd); s.send(7, s.acc.at[0], s.rx.at[2], s.xf)
    def e(s):
        for k in range(3): s.got(5 + k, s.rx.at[k])
        s.acc[1] = s.acc[0] + s.rx[0] + s.rx[1] + s.rx[2]
        s.send(8, s.acc.at[1], s.rt, s.zf)
    def f(s):
        s.got(8, s.rt)
        first = lax.broadcasted_iota(jnp.int32, (16, 128), 0) < 2
        s.out[...] = jnp.where(first, s.acc[1] + s.rt[...], s.acc[0])

def peers_all():
    c, y, zl, x, zh = place()
    return ([peer(1 - c, y, zl, x, zh), peer(c, y, 1 - zl, x, zh), peer(c, y, zl, x, 1 - zh)]
            + [peer(c, (y + k) % 4, zl, x, zh) for k in (1, 2, 3)] + [peer(c, y, zl, (x + k) % 4, zh) for k in (1, 2, 3)])

def norm_back_rows(r, gn, tokens, cot, gain, out, sums):
    x = tokens[r, :].astype(f32)
    mean = jnp.mean(x, axis=-1, keepdims=True); cen = x - mean
    inv = lax.rsqrt(jnp.mean(cen * cen, axis=-1, keepdims=True) + 1e-5)
    xh = cen * inv
    n = x.shape[0] // 8
    sums[0] += jnp.sum((gn * xh).reshape(n, 8, 2048), axis=0)
    sums[1] += jnp.sum(gn.reshape(n, 8, 2048), axis=0)
    sc = gn * gain
    ig = cot[r, :].astype(f32) + inv * (sc - jnp.mean(sc, axis=-1, keepdims=True) - xh * jnp.mean(sc * xh, axis=-1, keepdims=True))
    out[r, :] = ig.astype(bf16)

PLAN = ("v0", "o0", "q0", "v1", "o1", "q1", "v2", "v3", "o2", "q2", "u0", "first", "o3", "vectors", "d0", "n1", "Ao", "n2", "q3", "n0",
        "Wo", "ga", "Aq", "u1", "n3", "Wq", "sn", "p1", "p3", "p2", "p0", "d1", "u2", "a3y", "a0y", "a3x", "a1x", "u3", "a0x", "d2",
        "a2y", "a2x", "Au", "a1y", "k", "sg", "sa", "Wu", "h2", "d3", "h1", "h0", "h3")

def NT(a, b): return lax.dot_general(a, b, (((1,), (1,)), ((), ())), preferred_element_type=f32)
def NN(a, b): return lax.dot_general(a, b, (((1,), (0,)), ((), ())), preferred_element_type=f32)
def TN(a, b): return lax.dot_general(a, b, (((0,), (0,)), ((), ())), preferred_element_type=f32)

def rotary_tables():
    pos = np.arange(LEN, dtype=np.float32)
    freq = (np.float32(rope_base) ** (-np.arange(0, ROT, 2, dtype=np.float32) / np.float32(ROT))).astype(np.float32)
    ang = (pos[:, None] * freq[None, :]).astype(np.float32)
    cos, sin = np.cos(ang).astype(np.float32), np.sin(ang).astype(np.float32)
    one, zero = np.ones((LEN, 32), np.float32), np.zeros((LEN, 16), np.float32)
    c = np.concatenate([cos, cos, one], 1)
    s1 = np.concatenate([-sin, zero, zero, zero], 1)
    s2 = np.concatenate([zero, sin, zero, zero], 1)
    return np.stack([np.concatenate([t, t], 1) for t in (c, s1, s2)])

def turn(u, tab, r, sign):
    other = pltpu.roll(u, 112, 1) * tab[1, r, :] + pltpu.roll(u, 16, 1) * tab[2, r, :]
    straight = u * tab[0, r, :]
    return straight + other if sign > 0 else straight - other


def pack(vec, gain, lbias, bout, bdown, bup, bqkv):
    dp = lax.axis_index("dp")
    k = lax.broadcasted_iota(jnp.int32, (64, 128), 0); l = lax.broadcasted_iota(jnp.int32, (64, 128), 1)
    up = NN(bup[...], ((l % 64 == k) & (l // 64 == dp % 2)).astype(bf16))
    k4 = k[0:4]; l4 = l[0:4]
    on = (l4 % 4 == k4) & ((l4 % 64) // 4 == dp)
    rows = [gain[...].astype(f32), lbias[...].astype(f32), bout[...].astype(f32), bdown[...].astype(f32), up]
    for j in range(3):
        lo = NN(bqkv[j], (on & (l4 < 64)).astype(bf16)); hi = NN(bqkv[j], (on & (l4 >= 64)).astype(bf16))
        rows += [lo[0:1] + hi[1:2], lo[2:3] + hi[3:4]]
    vec[...] = jnp.concatenate(rows + [jnp.zeros((21, 128), f32)], 0).astype(bf16)

def forward_kernel(gain_s, lbias_s, bout_s, bdown_s, bup_s, bqkv_s, wq, wout, wup, wdown, tok_h, cot_h, tab_h,
                   vecs, wq_f, wout_f, wup_f, wdown_f, rows_h, nrm_h, att_h, act_h, dact_h, gp_h,
                   vec, tab, vv, wqv, woutv, wupv, tok, cot, nrm, rowsv, bqkv, bup, q, k, v, ga, att, dk, dv, gp, act, dact,
                   ss, rs, ls, ld):
    c, y, zl, x, zh = place()
    loads = {}
    def load(i, src, dst):
        loads[i] = pltpu.make_async_copy(src, dst, ld.at[i]); loads[i].start()
    load(0, tok_h, tok); load(1, cot_h, cot); load(12, tab_h, tab)
    pack(vec, gain_s, lbias_s, bout_s, bdown_s, bup_s, bqkv_s)
    enter([peer(c, (y + 1) % 4, zl, x, zh), peer(c, (y + 3) % 4, zl, x, zh), peer(c, y, 1 - zl, x, zh), peer(1 - c, y, zl, x, zh)])
    gv, gq, go, gu, gd = every = [Gather(a, b, ax, ss.at[i], rs.at[i]) for i, (a, b, ax) in enumerate(
        [(vec, vecs, 0), (wq, wq_f, 2), (wout, wout_f, 1), (wup, wup_f, 0), (wdown, wdown_f, 1)])]
    local = [pltpu.make_async_copy(g.shard, g.slot(0, 0), ls.at[i]) for i, g in enumerate(every)]
    for cp in local: cp.start()

    def norm(lo, hi):
        gain, bias = rowsv[0:1, :], rowsv[1:2, :]
        def go_(i, carry):
            r = pl.ds(pl.multiple_of(lo + i * 128, 128), 128)
            a = tok[r, :].astype(f32)
            cen = a - jnp.mean(a, axis=-1, keepdims=True)
            inv = lax.rsqrt(jnp.mean(cen * cen, axis=-1, keepdims=True) + norm_epsilon)
            nrm[r, :] = (cen * inv * gain + bias).astype(bf16)
            return carry
        lax.fori_loop(0, (hi - lo) // 128, go_, 0)

    def project(lo, hi):
        def go_(i, carry):
            r = pl.ds(pl.multiple_of(lo + i * 256, 256), 256)
            n = nrm[r, :]
            for j, dst in enumerate((q, k, v)):
                p = NN(n, wqv[j])
                for h in range(2):
                    u = p[:, h * 128:(h + 1) * 128] + bqkv[2 * j + h:2 * j + h + 1, :]
                    dst[h, r, :] = (u if j == 2 else turn(u, tab, r, 1)).astype(bf16)
            return carry
        lax.fori_loop(0, (hi - lo) // 256, go_, 0)

    def grad_attended():
        def go_(i, carry):
            r = pl.ds(pl.multiple_of(i * 256, 256), 256)
            p = NT(cot[r, :], woutv[...])
            ga[0, r, :] = p[:, 0:128].astype(bf16); ga[1, r, :] = p[:, 128:256].astype(bf16)
            return carry
        lax.fori_loop(0, 4, go_, 0)

    def attention(i):
        lax.fori_loop(0, 2, lambda p, carry: attention_pair(i, p, carry), 0)
    def attention_pair(i, p, carry=0):
            n = (i + 1) * 256
            r = pl.ds(i * 256, 256)
            cols = pl.ds(pl.multiple_of(p * 128, 128), 128)
            a_, d_, tk, tv = 0.0, 0.0, 0.0, 0.0
            for hh in range(2):
                m = ((lax.broadcasted_iota(jnp.int32, (1, 128), 1) // 64) == hh).astype(bf16)
                kk = k[p, 0:n] * m; w = v[p, 0:n] * m; qq = q[p, r] * (m * 0.125); gg = ga[p, r] * m
                s = NT(kk, qq)
                key = lax.broadcasted_iota(jnp.int32, (256, 256), 0); row = lax.broadcasted_iota(jnp.int32, (256, 256), 1)
                diag = jnp.where(row >= key, s[n - 256:], -1e30)
                s = diag if i == 0 else jnp.concatenate([s[:n - 256], diag], 0)
                e = jnp.exp(s - jnp.max(s, 0, keepdims=True))
                pr = e * (1.0 / jnp.sum(e, 0, keepdims=True))
                low = pr.astype(bf16)
                dp = NT(w, gg)
                ds = (pr * (dp - jnp.sum(pr * dp, 0, keepdims=True))).astype(bf16)
                a_ = a_ + TN(low, w); d_ = d_ + TN(ds, kk)
                tk = tk + NN(ds, qq); tv = tv + NN(low, gg)
            att[r, cols] = a_.astype(bf16)
            gp[r, cols] = turn(d_ * 0.125, tab, r, -1).astype(bf16)
            if i == 3: dk[p] = tk; dv[p] = tv
            else:
                dk[p, 0:n] += tk; dv[p, 0:n] += tv
            return carry

    def keys_done():
        def go_(i, carry):
            r = pl.ds(pl.multiple_of(i * 256, 256), 256)
            for p in range(2):
                gp[r, 256 + p * 128:384 + p * 128] = turn(dk[p, r], tab, r, -1).astype(bf16)
                gp[r, 512 + p * 128:640 + p * 128] = dv[p, r].astype(bf16)
            return carry
        lax.fori_loop(0, 4, go_, 0)

    def hidden(lo, hi):
        def go_(i, carry):
            r = pl.ds(pl.multiple_of(lo + i * 256, 256), 256)
            n = nrm[r, :]
            for j in range(4):
                cols = pl.ds(j * 256, 256)
                h = NN(n, wupv[:, cols]) + bup[0:1, cols]
                h2 = h * h
                t = jnp.tanh(0.7978845608028654 * h * (1.0 + 0.044715 * h2))
                act[r, cols] = (0.5 * h * (1.0 + t)).astype(bf16)
                dact[r, cols] = (0.5 * (1.0 + t) + 0.5 * h * (1.0 - t * t) * (0.7978845608028654 * (1.0 + 0.134145 * h2))).astype(bf16)
            return carry
        lax.fori_loop(0, (hi - lo) // 256, go_, 0)

    def first():
        gv.arrived(); local[0].wait(); load(2, vecs, vv)
    def vectors():
        loads[2].wait(); loads[0].wait()
        bq, bu = jnp.zeros((6, 128), f32), None
        for d in range(16):
            t = vv[pl.ds(d * 32, 32), :].astype(f32)
            cols = pl.ds(d * 128, 128)
            rowsv[0:1, cols] = t[0:1]; rowsv[1:2, cols] = t[1:2]; rowsv[2:3, cols] = t[2:3] + t[3:4]
            bq = bq + t[5:11]
            if d % 2 == 0: bu = t[4:5]
            else: bup[0:1, pl.ds((d // 2) * 128, 128)] = bu + t[4:5]
        bqkv[0:6, :] = bq
        load(6, rowsv, rows_h)
    def have_q():
        gq.arrived(); local[1].wait(); load(3, wq_f, wqv)
    def have_o():
        go.arrived(); local[2].wait(); load(4, wout_f, woutv)
    def have_u():
        gu.arrived(); local[3].wait(); load(7, wup_f, wupv)
    steps = {"first": first, "vectors": vectors, "Aq": have_q, "Ao": have_o, "Au": have_u,
             "Wq": lambda: (loads[3].wait(), loads[12].wait()), "Wo": lambda: (loads[4].wait(), loads[1].wait()), "Wu": lambda: loads[7].wait(),
             "ga": grad_attended, "k": keys_done, "sn": lambda: load(5, nrm, nrm_h), "sa": lambda: load(8, att, att_h), "sg": lambda: load(9, gp, gp_h)}
    for i in range(4):
        steps["n%d" % i] = partial(norm, i * 256, i * 256 + 256)
        steps["p%d" % i] = partial(project, i * 256, i * 256 + 256)
        steps["h%d" % i] = partial(hidden, i * 256, i * 256 + 256)
        steps["a%d" % i] = partial(attention, i)
        for p in range(2): steps["a%d%s" % (i, "xy"[p])] = partial(attention_pair, i, p)
    for nm, g in (("v", gv), ("q", gq), ("o", go), ("u", gu), ("d", gd)):
        steps[nm + "0"], steps[nm + "1"], steps[nm + "2"], steps[nm + "3"] = g.start, g.serve, g.serve2, g.serve3
    for name in PLAN: steps[name]()
    load(10, act, act_h); load(11, dact, dact_h)
    gd.arrived()
    for i in (5, 6, 8, 9, 10, 11): loads[i].wait()
    local[4].wait()
    for g in (gv, gq, go, gu, gd):
        for cp in g.sends: cp.wait_send()

def forward(vectors, wq, wout, wup, wdown, tokens, cot, tab):
    A = pl.BlockSpec(memory_space=pl.ANY); V = pl.BlockSpec(memory_space=pltpu.VMEM)
    S = jax.ShapeDtypeStruct
    vm = lambda sh, t=bf16: pltpu.VMEM(sh, t)
    return pl.pallas_call(forward_kernel,
        out_shape=[S((512, 128), bf16), S((3, 2048, 256), bf16), S((256, 2048), bf16), S((2048, 1024), bf16), S((1024, 2048), bf16),
                   S((8, 2048), f32), S((1024, 2048), bf16), S((1024, 256), bf16), S((1024, 1024), bf16), S((1024, 1024), bf16), S((1024, 768), bf16)],
        in_specs=[V] * 6 + [A] * 7, out_specs=[A] * 11,
        scratch_shapes=[vm((32, 128)), vm((3, 1024, 128), f32), vm((512, 128)), vm((3, 2048, 256)), vm((256, 2048)), vm((2048, 1024)), vm((1024, 2048)), vm((1024, 2048)), vm((1024, 2048)),
                        vm((8, 2048), f32), vm((8, 128), f32), vm((8, 1024), f32), vm((2, 1024, 128)), vm((2, 1024, 128)), vm((2, 1024, 128)), vm((2, 1024, 128)),
                        vm((1024, 256)), vm((2, 1024, 128), f32), vm((2, 1024, 128), f32), vm((1024, 768)), vm((1024, 1024)), vm((1024, 1024)),
                        pltpu.SemaphoreType.DMA((5, 16)), pltpu.SemaphoreType.DMA((5, 16)), pltpu.SemaphoreType.DMA((5,)), pltpu.SemaphoreType.DMA((13,))],
        compiler_params=pltpu.CompilerParams(collective_id=1, has_side_effects=True, vmem_limit_bytes=60 << 20),
        name="gather_and_forward")(*vectors, wq, wout, wup, wdown, tokens, cot, tab)

PLAN_B = ("L0", "bB", "L1", "bA", "bC", "bD", "h0", "h1", "n0", "n1", "bM", "n2", "n3", "gS", "s2P0", "s2P1", "s2P2", "bL", "s2p0", "s2P3",
          "gM", "bias", "s2p1", "bN", "s21", "suP0", "gL", "gN", "mS", "sup0", "suP1", "s22", "iS", "sup1", "sqP0", "su1", "sqP1", "va", "vb", "mM",
          "sqp0", "vc", "sqp1", "iM", "sq1", "su2", "mP", "s23", "mF", "vd", "sq2", "iF", "su3", "iP", "sq3", "s24", "su4", "ve", "vf", "mE",
          "sq4", "iE")

class Scatter(Link):
    def __init__(s, g, sib, mid, ss, rs, width):
        super().__init__(ss, rs)
        s.g, s.b, s.m, s.w = g, sib, mid, width
    def to_sibling(s, k):
        return pltpu.make_async_remote_copy(s.g.at[k, 1 - s.c, :, pl.ds(0, s.w)], s.b.at[k], s.ss.at[k], s.rs.at[k],
                                            device_id=s.sib, device_id_type=MESH)
    def produce(s, lhs, rhs, lo, hi):
        n = rhs.shape[1]
        def go(j, carry):
            y = (s.y + 2 + 3 * j) % 4
            for p in range(2):
                a = lhs[:, pl.ds(pl.multiple_of((p * 4 + y) * 256, 256), 256)]
                for at in range(0, n, 256):
                    r = TN(a, rhs[:, at:at + 256]).astype(bf16)
                    s.g[2 * j + p, 0, :, at:at + 256] = r[0:128]; s.g[2 * j + p, 1, :, at:at + 256] = r[128:256]
                s.to_sibling(2 * j + p).start()
            return carry
        lax.fori_loop(lo, hi, go, 0)
    def pairs(s, lo, hi):
        def go(k, carry):
            s.to_sibling(k).wait()
            mine = s.g.at[k, s.c]; dst = s.b.at[k]
            def rows(i, cc):
                r = pl.ds(pl.multiple_of(i * 32, 32), 32)
                dst[r, :] = (dst[r, :].astype(f32) + mine[r, 0:s.w].astype(f32)).astype(bf16)
                return cc
            lax.fori_loop(0, 4, rows, 0)
            return carry
        lax.fori_loop(lo, hi, go, 0)
    def serve1(s):
        s.send(8, s.b.at[0], s.m.at[0], s.yu); s.send(9, s.b.at[1], s.m.at[1], s.yd)
        s.send(10, s.b.at[3], s.m.at[4], s.yu); s.send(11, s.b.at[6], s.m.at[2], s.yd)
    def serve2(s):
        s.got(8, s.m.at[0]); add_into(s.b.at[2], [s.b.at[2], s.m.at[0]], 128, 32); s.send(12, s.b.at[2], s.m.at[3], s.yu)
        s.got(9, s.m.at[1]); add_into(s.b.at[7], [s.b.at[7], s.m.at[1]], 128, 32); s.send(13, s.b.at[7], s.m.at[5], s.yd)
    def serve3(s):
        for k, j in ((10, 4), (11, 2), (12, 3), (13, 5)): s.got(k, s.m.at[j])
        o = 1 - s.zl; b = s.b.at[4 + o]
        add_into(b, [b, s.m.at[2 + 2 * o], s.m.at[3 + 2 * o]], 128, 32); s.send(14, b, s.m.at[6], s.zn)
    def serve4(s, put):
        s.got(14, s.m.at[6])
        z = s.zl
        terms = (s.b.at[4 + z], s.m.at[2 + 2 * z], s.m.at[3 + 2 * z], s.m.at[6])
        def go(r):
            t = terms[0][r, :].astype(f32)
            for q in terms[1:]: t = t + q[r, :].astype(f32)
            put(r, t)
        by_rows(128, 32, go)

def backward_kernel(wq_f, wout_f, wup_f, wdown_f, rows_h, nrm_h, att_h, act_h, dact_h, gp_h, cot_h, tok_h,
                    mixed, ingrad, o2, oup, oq, osv,
                    wb, wch, cot, nrm, aa, pq, rowsv, tok, brp, gnp, own,
                    fa, t1a, t2a, zsa, zra, fb, t1b, t2b, zsb, zrb, g, sib2, m2, sibu, mu, sibq, mq,
                    v, rc, rz, ry, rx, rt, acc, sums, ss, rs, ld):
    c, y, zl, x, zh = place()
    t_own = zh * 4 + x
    o = 1 - zh
    loads = {}
    def load(i, src, dst):
        loads[i] = pltpu.make_async_copy(src, dst, ld.at[i]); loads[i].start()
    def wait(*ids):
        for i in ids: loads[i].wait()
    load(0, att_h, aa.at[:, pl.ds(0, 256)]); load(1, act_h, aa.at[:, pl.ds(256, 1024)])
    load(2, wout_f, wb.at[pl.ds(0, 256)]); load(3, wdown_f, wb.at[pl.ds(256, 1024)])
    enter(peers_all())
    bs = TensorSum(brp, fa, t1a, t2a, zsa, zra, ss.at[0], rs.at[0])
    gs = TensorSum(gnp, fb, t1b, t2b, zsb, zrb, ss.at[1], rs.at[1])
    mg = TensorGather(mixed, ss.at[2], rs.at[2])
    ig = TensorGather(ingrad, ss.at[3], rs.at[3])
    s2 = Scatter(g, sib2, m2, ss.at[4], rs.at[4], 1280)
    su = Scatter(g, sibu, mu, ss.at[5], rs.at[5], 1024)
    sq = Scatter(g, sibq, mq, ss.at[6], rs.at[6], 768)
    sm = SmallSum(v, rc, rz, ry, rx, rt, acc, osv, ss.at[7], rs.at[7])
    gp, gh = pq.at[:, pl.ds(0, 768)], pq.at[:, pl.ds(768, 1024)]

    def chunk(j):
        s = j % 2; r = pl.ds(j * 512, 512)
        for e in range(3): load(10 + 4 * s + e, wq_f.at[e, r], wch.at[s, :, pl.ds(e * 256, 256)])
        load(13 + 4 * s, wup_f.at[r], wch.at[s, :, pl.ds(768, 1024)])
    def first_loads(): wait(0, 1, 2, 3)
    def other_loads():
        load(4, cot_h, cot); load(5, dact_h, gh); load(6, gp_h, gp); chunk(0); chunk(1); load(7, nrm_h, nrm)
        load(8, rows_h, rowsv); load(9, tok_h.at[pl.ds(pl.multiple_of(t_own * 128, 128), 128)], tok)
    def branch(a, b):
        ra, rb = (pl.ds(pl.multiple_of(t * 128, 128), 128) for t in (a, b))
        lhs = jnp.concatenate([aa[ra, :], aa[rb, :]], 0)
        def go(j, carry):
            cols = pl.ds(pl.multiple_of(j * 512, 512), 512)
            p = NN(lhs, wb[:, cols]).astype(bf16)
            brp[a, :, cols] = p[0:128]; brp[b, :, cols] = p[128:256]
            return carry
        lax.fori_loop(0, 4, go, 0)
    def grad_hidden(lo, hi):
        if lo == 0: wait(4, 5)
        def go(i, carry):
            r = pl.ds(pl.multiple_of(i * 512, 512), 512)
            gr = cot[r, :]
            for j in range(4):
                p = NT(gr, wb[256 + j * 256:512 + j * 256, :])
                cols = pl.ds(768 + j * 256, 256)
                pq[r, cols] = (p * pq[r, cols].astype(f32)).astype(bf16)
            return carry
        lax.fori_loop(lo, hi, go, 0)
    def grad_normed(j):
        s = j % 2
        if j == 0: wait(6)
        wait(*range(10 + 4 * s, 14 + 4 * s))
        p = NT(pq[...], wch[s]).astype(bf16)
        gnp[:, :, j * 512:(j + 1) * 512] = p.reshape(8, 128, 512)
        if j + 2 < 4: chunk(j + 2)
    def bias_sums():
        ones = jnp.ones((16, 1024), bf16)
        for d in range(8):
            w = v.at[:, d // 4, d % 4]
            gb = NN(ones, cot[:, d * 256:(d + 1) * 256])[0:1]
            gu_ = NN(ones, gh[:, d * 128:(d + 1) * 128])[0:1]
            for cc in range(2):
                w[cc, 2:3, :] = gb[:, cc * 128:(cc + 1) * 128]; w[cc, 3:4, :] = gu_
        for j in range(3):
            gqb = NN(ones, gp[:, j * 256:(j + 1) * 256])[0:1]
            for d in range(16):
                w = v.at[d % 2, d // 8, (d // 2) % 4]
                w[4 + 2 * j:5 + 2 * j, :] = gqb[:, 0:128]; w[5 + 2 * j:6 + 2 * j, :] = gqb[:, 128:256]
    def mixed_start():
        bs.arrived()
        def mix(r): own[0, r, :] = (tok[r, :].astype(f32) + bs.total(r) + rowsv[2:3, :]).astype(bf16)
        wait(8, 9)
        by_rows(128, 64, mix)
        load(18, own.at[0], mixed.at[t_own])
        mg.start(own.at[0])
    def ingrad_start():
        gs.arrived()
        sums[...] = jnp.zeros_like(sums)
        cot_own = cot.at[pl.ds(pl.multiple_of(t_own * 128, 128), 128)]
        by_rows(128, 32, lambda r: norm_back_rows(r, gs.total(r), tok, cot_own, rowsv[0:1, :], own.at[1], sums))
        load(19, own.at[1], ingrad.at[t_own])
        ig.start(own.at[1])
    def norm_sums():
        sg = jnp.sum(sums[0], axis=0, keepdims=True); sb = jnp.sum(sums[1], axis=0, keepdims=True)
        for d in range(16):
            w = v.at[d % 2, d // 8, (d // 2) % 4]
            w[0:1, :] = sg[:, d * 128:(d + 1) * 128]; w[1:2, :] = sb[:, d * 128:(d + 1) * 128]
        sm.a()
    def put2(r, t): o2[r, :] = t
    def putu(r, t): oup[r, :] = t
    def putq(r, t): oq[r, :] = t
    def xp(k): return (x + k) % 4
    def far(): branch(o * 4 + xp(2), zh * 4 + xp(2)); bs.start_far()
    def near(): branch(o * 4 + xp(1), o * 4 + xp(3)); bs.start_near()
    def near2(): branch(zh * 4 + xp(1), zh * 4 + xp(3)); bs.start_near2()
    def home(): branch(o * 4 + xp(0), zh * 4 + xp(0))
    def gn_start(): gs.start_far(); gs.start_near(); gs.start_near2()
    steps = {"L0": first_loads, "L1": other_loads, "bA": far, "bB": near, "bC": near2, "bD": home, "gS": gn_start, "bias": bias_sums,
             "mS": mixed_start, "iS": ingrad_start, "va": norm_sums, "vb": sm.b, "vc": sm.c_, "vd": sm.d, "ve": sm.e, "vf": sm.f,
             "h0": partial(grad_hidden, 0, 1), "h1": partial(grad_hidden, 1, 2),
             "s24": partial(s2.serve4, put2), "su4": partial(su.serve4, putu), "sq4": partial(sq.serve4, putq)}
    for i in range(4):
        steps["n%d" % i] = partial(grad_normed, i); steps["s2P%d" % i] = partial(s2.produce, cot, aa, i, i + 1)
    def up_grads(lo, hi):
        if lo == 0: wait(7)
        su.produce(nrm, gh, lo, hi)
    for i in range(2):
        steps["suP%d" % i] = partial(up_grads, 2 * i, 2 * i + 2); steps["sqP%d" % i] = partial(sq.produce, nrm, gp, 2 * i, 2 * i + 2)
        for nm, w in (("s2", s2), ("su", su), ("sq", sq)): steps[nm + "p%d" % i] = partial(w.pairs, 4 * i, 4 * i + 4)
    for nm, w in (("s2", s2), ("su", su), ("sq", sq)): steps[nm + "1"], steps[nm + "2"], steps[nm + "3"] = w.serve1, w.serve2, w.serve3
    for nm, w in (("b", bs), ("g", gs)): steps[nm + "M"], steps[nm + "N"], steps[nm + "L"] = w.middle, w.middle2, w.last
    for nm, w in (("m", mg), ("i", ig)): steps[nm + "M"], steps[nm + "P"], steps[nm + "F"], steps[nm + "E"] = w.middle, w.plane, w.far, w.finish
    for name in PLAN_B: steps[name]()
    wait(18, 19)
    for w in (gs, bs, mg, ig, s2, su, sq, sm): w.drain()

def backward(wq_f, wout_f, wup_f, wdown_f, rows, nrm, att, act, dact, gp, cot, tok):
    S = jax.ShapeDtypeStruct
    vm = lambda sh, t=bf16: pltpu.VMEM(sh, t)
    tsum = [vm((128, 2048)), vm((128, 2048)), vm((2, 2, 128, 2048)), vm((128, 2048)), vm((128, 2048))]
    A = pl.BlockSpec(memory_space=pl.ANY); V = pl.BlockSpec(memory_space=pltpu.VMEM)
    return pl.pallas_call(backward_kernel,
        out_shape=[S((8, 128, 2048), bf16)] * 2 + [S((128, 1280), f32), S((128, 1024), f32), S((128, 768), f32), S((16, 128), f32)],
        in_specs=[A] * 12, out_specs=[A] * 2 + [V] * 4,
        scratch_shapes=[vm((1280, 2048)), vm((2, 512, 1792)), vm((1024, 2048)), vm((1024, 2048)), vm((1024, 1280)), vm((1024, 1792)),
                        vm((8, 2048), f32), vm((128, 2048)), vm((8, 128, 2048)), vm((8, 128, 2048)), vm((2, 128, 2048))]
        + tsum + tsum + [vm((8, 2, 128, 1280)), vm((8, 128, 1280)), vm((7, 128, 1280)), vm((8, 128, 1024)), vm((7, 128, 1024)), vm((8, 128, 768)), vm((7, 128, 768)),
            vm((2, 2, 4, 16, 128), f32), vm((2, 4, 16, 128), f32), vm((4, 16, 128), f32), vm((3, 16, 128), f32), vm((3, 16, 128), f32), vm((16, 128), f32),
            vm((2, 16, 128), f32), vm((2, 8, 2048), f32),
            pltpu.SemaphoreType.DMA((8, 16)), pltpu.SemaphoreType.DMA((8, 16)), pltpu.SemaphoreType.DMA((20,))],
        compiler_params=pltpu.CompilerParams(collective_id=2, has_side_effects=True, vmem_limit_bytes=64 << 20),
        name="backward_and_sums")(wq_f, wout_f, wup_f, wdown_f, rows, nrm, att, act, dact, gp, cot, tok)

def hand_over_kernel(mixed, ingrad, o2_h, oup_h, oq_h, osv, mo, io, gg, gb, gq_h, gbq, go_h, gbo, gu_h, gbu, gd_h, gbd,
                     big, o2, oup, oq, gq, go, gd, li, lo):
    dp = lax.axis_index("dp")
    def copy(a, b, sem):
        cp = pltpu.make_async_copy(a, b, sem); cp.start()
        return cp
    n = 8
    ins = [copy((mixed, ingrad)[i // 4].at[pl.ds((i % 4) * 2, 2)], big.at[i], li.at[i]) for i in range(4)]
    small = [copy(o2_h, o2, li.at[n]), copy(oup_h, oup, li.at[n + 1]), copy(oq_h, oq, li.at[n + 2])]
    ins += [copy((mixed, ingrad)[i // 4].at[pl.ds((i % 4) * 2, 2)], big.at[i], li.at[i]) for i in range(4, 8)]
    outs = []
    def pass_on(i):
        ins[i].wait()
        for h in range(2): outs.append(copy(big.at[i, h], (mo, io)[i // 4].at[pl.ds((i % 4) * 256 + h * 128, 128)], lo.at[2 * i + h]))
    pass_on(0); pass_on(1)
    small[0].wait()
    for b in range(10):
        t = o2[:, b * 128:(b + 1) * 128].T
        if b < 2: go[b * 128:(b + 1) * 128, :] = t
        else: gd[(b - 2) * 128:(b - 1) * 128, :] = t
    outs += [copy(go, go_h, lo.at[16]), copy(gd, gd_h, lo.at[17])]
    pass_on(2); pass_on(3)
    small[1].wait(); outs.append(copy(oup, gu_h, lo.at[18]))
    small[2].wait()
    for j in range(3): gq[j] = oq[:, j * 256:(j + 1) * 256]
    outs.append(copy(gq, gq_h, lo.at[19]))
    pass_on(4); pass_on(5)
    gg[...] = osv[0:1, :]; gb[...] = osv[1:2, :]; gbo[...] = osv[2:3, :]; gbd[...] = osv[2:3, :]
    l = lax.broadcasted_iota(jnp.int32, (128, 64), 0); k = lax.broadcasted_iota(jnp.int32, (128, 64), 1)
    gbu[...] = lax.dot_general(osv[3:4, :], (l == k + 64 * (dp % 2)).astype(f32), (((1,), (0,)), ((), ())), precision=lax.Precision.HIGHEST)
    l = lax.broadcasted_iota(jnp.int32, (128, 4), 0); k = lax.broadcasted_iota(jnp.int32, (128, 4), 1)
    for j in range(3):
        rows = osv[4 + 2 * j:6 + 2 * j, :]
        lo_, hi_ = (lax.dot_general(rows, (l == k + 4 * dp + 64 * h).astype(f32), (((1,), (0,)), ((), ())), precision=lax.Precision.HIGHEST) for h in (0, 1))
        gbq[j] = jnp.concatenate([lo_[0:1], hi_[0:1], lo_[1:2], hi_[1:2]], 0)
    pass_on(6); pass_on(7)
    for cp in outs: cp.wait()

def hand_over(mixed, ingrad, o2, oup, oq, osv):
    S = jax.ShapeDtypeStruct
    A = pl.BlockSpec(memory_space=pltpu.HBM)
    full = lambda sh: pl.BlockSpec(sh, lambda: (0,) * len(sh))
    outs = [((1, 128), 0), ((1, 128), 0), ((3, 128, 256), 1), ((3, 4, 4), 0), ((256, 128), 1), ((1, 128), 0), ((128, 1024), 1), ((1, 64), 0), ((1024, 128), 1), ((1, 128), 0)]
    vm = lambda sh: pltpu.VMEM(sh, f32)
    return pl.pallas_call(hand_over_kernel,
        out_shape=[S((1024, 2048), bf16)] * 2 + [S(sh, f32) for sh, _ in outs],
        in_specs=[A] * 5 + [full((16, 128))], out_specs=[A] * 2 + [A if m else full(sh) for sh, m in outs],
        scratch_shapes=[pltpu.VMEM((8, 2, 128, 2048), bf16), vm((128, 1280)), vm((128, 1024)), vm((128, 768)), vm((3, 128, 256)), vm((256, 128)), vm((1024, 128)),
                        pltpu.SemaphoreType.DMA((12,)), pltpu.SemaphoreType.DMA((20,))],
        compiler_params=pltpu.CompilerParams(vmem_limit_bytes=62 << 20),
        name="hand_over")(mixed, ingrad, o2, oup, oq, osv)

def body(tokens, ln_gain, ln_bias, w_qkv, b_qkv, w_out, b_out, w_up, b_up, w_down, b_down, cotangent):
    row = lambda a: a.reshape(1, 128)
    vecs, wq_f, wout_f, wup_f, wdown_f, rows, nrm, att, act, dact, gp = forward(
        (row(ln_gain), row(ln_bias), row(b_out), row(b_down), b_up, b_qkv), w_qkv.transpose(1, 0, 2), w_out, w_up, w_down,
        tokens, cotangent, jnp.asarray(rotary_tables()))
    parts = backward(wq_f, wout_f, wup_f, wdown_f, rows, nrm, att, act, dact, gp, cotangent, tokens)
    mixed, ingrad, gg, gb, gq, gbq, go, gbo, gu, gbu, gd, gbd = hand_over(*parts)
    return (mixed, ingrad, gg.reshape(128), gb.reshape(128), gq.transpose(1, 0, 2), gbq, go, gbo.reshape(128), gu, gbu, gd, gbd.reshape(128))


def solution(mesh):
    in_specs = (
        P("dp", None),
        P("dp"),
        P("dp"),
        P("dp", None, "tensor"),
        P(None, "tensor", "dp"),
        P("tensor", "dp"),
        P("dp"),
        P("dp", "tensor"),
        P("tensor", "dp"),
        P("tensor", "dp"),
        P("dp"),
        P("dp", None),
    )
    out_specs = (
        P("dp", None),
        P("dp", None),
        P("dp"),
        P("dp"),
        P("dp", None, "tensor"),
        P(None, "tensor", "dp"),
        P("tensor", "dp"),
        P("dp"),
        P("dp", "tensor"),
        P("tensor", "dp"),
        P("tensor", "dp"),
        P("dp"),
    )
    return jax.shard_map(body, mesh=mesh, in_specs=in_specs, out_specs=out_specs, check_vma=False)
```

```python
from functools import partial

import jax
import jax.numpy as jnp
import numpy as np
from jax import lax
from jax.sharding import PartitionSpec as P
from jax.experimental import pallas as pl
from jax.experimental.pallas import tpu as pltpu

HD = 64
ROT = 32
LEN = 1024
norm_epsilon = 1e-05
rope_base = 10000.0
MESH = pl.DeviceIdType.MESH

def place():
    dp = lax.axis_index("dp"); tn = lax.axis_index("tensor")
    return dp % 2, (dp // 2) % 4, dp // 8, tn % 4, tn // 4

def peer(c, y, zl, x, zh):
    return (zl * 8 + y * 2 + c, zh * 4 + x)

RELS = [(0, 0), (0, 1), (0, 3), (0, 2), (1, 0), (1, 1), (1, 3), (1, 2)]

def enter(devices):
    bar = pltpu.get_barrier_semaphore()
    for d in devices:
        pl.semaphore_signal(bar, inc=1, device_id=d, device_id_type=MESH)
    pl.semaphore_wait(bar, len(devices))

class Gather:
    def __init__(s, shard, full, axis, ss, rs):
        s.axis, s.ss, s.rs, s.full = axis, ss, rs, full
        s.c, s.y, s.zl, x, zh = place()
        c, y, zl = s.c, s.y, s.zl
        s.total = shard.shape[1 if axis == 2 else 0]
        s.shard = shard
        s.up = peer(c, (y + 1) % 4, zl, x, zh); s.down = peer(c, (y + 3) % 4, zl, x, zh)
        s.z = peer(c, y, 1 - zl, x, zh); s.sib = peer(1 - c, y, zl, x, zh)
        s.sends = []
    def slot(s, dz, dy, c=None, half=None):
        c = s.c if c is None else c
        d = ((s.zl + dz) % 2) * 8 + ((s.y + dy) % 4) * 2 + c
        n = s.total if half is None else s.total // 2
        lo = 0 if half is None else half * n
        if s.axis == 0: return s.full.at[pl.ds(pl.multiple_of(d * s.total + lo, 16), n)]
        if s.axis == 2: return s.full.at[:, pl.ds(pl.multiple_of(d * s.total + lo, 16), n)]
        return s.full.at[pl.ds(lo, n), pl.ds(pl.multiple_of(d * 128, 128), 128)]
    def send(s, kind, src, dst, dev):
        cp = pltpu.make_async_remote_copy(src, dst, s.ss.at[kind], s.rs.at[kind], device_id=dev, device_id_type=MESH)
        cp.start(); s.sends.append(cp)
    def got(s, kind, dst):
        pltpu.make_async_remote_copy(dst, dst, s.ss.at[kind], s.rs.at[kind], device_id=s.sib, device_id_type=MESH).wait_recv()
    def start(s):
        own = s.slot(0, 0)
        s.send(0, s.shard, own, s.up); s.send(1, s.shard, own, s.down); s.send(2, s.shard, own, s.z)
        s.send(8, s.shard, own, s.sib)
    def relay(s, rel):
        b = s.slot(*RELS[rel]); s.send(8 + rel, b, b, s.sib)
    def serve(s):
        a = s.slot(0, 3); s.got(0, a); h = s.slot(0, 3, half=0); s.send(5, h, h, s.up)
        b = s.slot(0, 1); s.got(1, b); h = s.slot(0, 1, half=1); s.send(6, h, h, s.down)
        z = s.slot(1, 0); s.got(2, z); s.send(3, z, z, s.up); s.send(4, z, z, s.down)
        s.relay(2); s.relay(1); s.relay(4)
    def serve2(s):
        s.got(5, s.slot(0, 2, half=0)); s.got(6, s.slot(0, 2, half=1))
        f = s.slot(0, 2); s.send(7, f, f, s.z); s.relay(3)
    def serve3(s):
        s.got(3, s.slot(1, 3)); s.relay(6)
        s.got(4, s.slot(1, 1)); s.relay(5)
        s.got(7, s.slot(1, 2)); s.relay(7)
    def arrived(s):
        for r in range(8): s.got(8 + r, s.slot(*RELS[r], c=1 - s.c))

f32 = jnp.float32
bf16 = jnp.bfloat16

def by_rows(rows, step, fn):
    def go(i, carry):
        fn(pl.ds(pl.multiple_of(i * step, step), step))
        return carry
    lax.fori_loop(0, rows // step, go, 0)

def add_into(dst, terms, rows, step, lo=0):
    def go(r):
        if lo: r = pl.ds(pl.multiple_of(r.start + lo, step), step)
        total = terms[0][r, :].astype(f32)
        for t in terms[1:]: total = total + t[r, :].astype(f32)
        dst[r, :] = total.astype(dst.dtype)
    by_rows(rows, step, go)

class Link:
    def __init__(s, ss, rs):
        s.ss, s.rs, s.sends = ss, rs, []
        c, y, zl, x, zh = s.at = place()
        s.c, s.y, s.zl, s.x, s.zh = s.at
        s.sib = peer(1 - c, y, zl, x, zh)
        s.yu, s.yd, s.yf = (peer(c, (y + k) % 4, zl, x, zh) for k in (1, 3, 2))
        s.zn = peer(c, y, 1 - zl, x, zh)
        s.xu, s.xd, s.xf = (peer(c, y, zl, (x + k) % 4, zh) for k in (1, 3, 2))
        s.zf = peer(c, y, zl, x, 1 - zh)
    def send(s, kind, src, dst, dev):
        cp = pltpu.make_async_remote_copy(src, dst, s.ss.at[kind], s.rs.at[kind], device_id=dev, device_id_type=MESH)
        cp.start(); s.sends.append(cp)
    def got(s, kind, dst):
        pltpu.make_async_remote_copy(dst, dst, s.ss.at[kind], s.rs.at[kind], device_id=s.sib, device_id_type=MESH).wait_recv()
    def drain(s):
        for cp in s.sends: cp.wait_send()

class TensorSum(Link):
    def __init__(s, b, f, t1, t2, zs, zr, ss, rs):
        super().__init__(ss, rs)
        s.b, s.f, s.t1, s.t2, s.zs, s.zr = b, f, t1, t2, zs, zr
    def blk(s, zh, dx): return s.b.at[zh * 4 + (s.x + dx) % 4]
    LO, HI = pl.ds(0, 64), pl.ds(64, 64)
    def start_far(s): s.send(0, s.blk(1 - s.zh, 2), s.f, s.zf)
    def start_near(s):
        o = 1 - s.zh
        s.send(1, s.blk(o, 1), s.t2.at[0, o], s.xu); s.send(2, s.blk(o, 3), s.t2.at[1, o], s.xd)
    def start_near2(s):
        s.send(3, s.blk(s.zh, 1).at[s.HI], s.t2.at[0, s.zh, s.HI], s.xu); s.send(4, s.blk(s.zh, 3).at[s.LO], s.t2.at[1, s.zh, s.LO], s.xd)
    def middle(s):
        s.got(0, s.f); add_into(s.f, [s.f, s.blk(s.zh, 2)], 128, 32)
        s.send(5, s.f.at[s.LO], s.t1.at[s.LO], s.xu); s.send(6, s.f.at[s.HI], s.t1.at[s.HI], s.xd)
    def middle2(s):
        s.got(5, s.t1.at[s.LO]); add_into(s.t1, [s.t1, s.blk(s.zh, 1)], 64, 32)
        s.send(7, s.t1.at[s.LO], s.t2.at[0, s.zh, s.LO], s.xu)
        s.got(6, s.t1.at[s.HI]); add_into(s.t1, [s.t1, s.blk(s.zh, 3)], 64, 32, lo=64)
        s.send(8, s.t1.at[s.HI], s.t2.at[1, s.zh, s.HI], s.xd)
    def last(s):
        o = 1 - s.zh
        s.got(1, s.t2.at[0, o]); s.got(2, s.t2.at[1, o])
        add_into(s.zs, [s.blk(o, 0), s.t2.at[0, o], s.t2.at[1, o]], 128, 32)
        s.send(9, s.zs, s.zr, s.zf)
    def total(s, r):
        return (s.blk(s.zh, 0)[r, :].astype(f32) + s.t2.at[0, s.zh][r, :].astype(f32)
                + s.t2.at[1, s.zh][r, :].astype(f32) + s.zr[r, :].astype(f32))
    def arrived(s):
        z = s.zh
        s.got(3, s.t2.at[0, z, s.HI]); s.got(4, s.t2.at[1, z, s.LO]); s.got(7, s.t2.at[0, z, s.LO]); s.got(8, s.t2.at[1, z, s.HI])
        s.got(9, s.zr)

class TensorGather(Link):
    def __init__(s, o, ss, rs):
        super().__init__(ss, rs); s.o = o
    def blk(s, zh, dx): return s.o.at[zh * 4 + (s.x + dx) % 4]
    LO, HI = pl.ds(0, 64), pl.ds(64, 64)
    def start(s, own):
        b = s.blk(s.zh, 0)
        s.send(0, own, b, s.xu); s.send(1, own, b, s.xd); s.send(2, own, b, s.zf)
    def middle(s):
        b = s.blk(s.zh, 3); s.got(0, b); s.send(3, b.at[s.LO], b.at[s.LO], s.xu)
        b = s.blk(s.zh, 1); s.got(1, b); s.send(4, b.at[s.HI], b.at[s.HI], s.xd)
    def plane(s):
        b = s.blk(1 - s.zh, 0); s.got(2, b); s.send(5, b, b, s.xu); s.send(6, b, b, s.xd)
    def far(s):
        b = s.blk(s.zh, 2); s.got(3, b.at[s.LO]); s.got(4, b.at[s.HI]); s.send(7, b, b, s.zf)
    def finish(s):
        o = 1 - s.zh
        s.got(5, s.blk(o, 3)); s.got(6, s.blk(o, 1)); s.got(7, s.blk(o, 2))

class SmallSum(Link):
    def __init__(s, v, rc, rz, ry, rx, rt, acc, out, ss, rs):
        super().__init__(ss, rs)
        s.v, s.rc, s.rz, s.ry, s.rx, s.rt, s.acc, s.out = v, rc, rz, ry, rx, rt, acc, out
    def a(s): s.send(0, s.v.at[1 - s.c], s.rc, s.sib)
    def b(s):
        s.got(0, s.rc); s.rc[...] = s.rc[...] + s.v[s.c]
        s.send(1, s.rc.at[1 - s.zl], s.rz, s.zn)
    def c_(s):
        s.got(1, s.rz); s.rz[...] = s.rz[...] + s.rc[s.zl]
        s.send(2, s.rz.at[(s.y + 1) % 4], s.ry.at[0], s.yu); s.send(3, s.rz.at[(s.y + 3) % 4], s.ry.at[1], s.yd)
        s.send(4, s.rz.at[(s.y + 2) % 4], s.ry.at[2], s.yf)
    def d(s):
        for k in range(3): s.got(2 + k, s.ry.at[k])
        s.acc[0] = s.rz[s.y] + s.ry[0] + s.ry[1] + s.ry[2]
        s.send(5, s.acc.at[0], s.rx.at[0], s.xu); s.send(6, s.acc.at[0], s.rx.at[1], s.xd); s.send(7, s.acc.at[0], s.rx.at[2], s.xf)
    def e(s):
        for k in range(3): s.got(5 + k, s.rx.at[k])
        s.acc[1] = s.acc[0] + s.rx[0] + s.rx[1] + s.rx[2]
        s.send(8, s.acc.at[1], s.rt, s.zf)
    def f(s):
        s.got(8, s.rt)
        first = lax.broadcasted_iota(jnp.int32, (16, 128), 0) < 2
        s.out[...] = jnp.where(first, s.acc[1] + s.rt[...], s.acc[0])

def peers_all():
    c, y, zl, x, zh = place()
    return ([peer(1 - c, y, zl, x, zh), peer(c, y, 1 - zl, x, zh), peer(c, y, zl, x, 1 - zh)]
            + [peer(c, (y + k) % 4, zl, x, zh) for k in (1, 2, 3)] + [peer(c, y, zl, (x + k) % 4, zh) for k in (1, 2, 3)])

def norm_back_rows(r, gn, tokens, cot, gain, out, sums):
    x = tokens[r, :].astype(f32)
    mean = jnp.mean(x, axis=-1, keepdims=True); cen = x - mean
    inv = lax.rsqrt(jnp.mean(cen * cen, axis=-1, keepdims=True) + 1e-5)
    xh = cen * inv
    n = x.shape[0] // 8
    sums[0] += jnp.sum((gn * xh).reshape(n, 8, 2048), axis=0)
    sums[1] += jnp.sum(gn.reshape(n, 8, 2048), axis=0)
    sc = gn * gain
    ig = cot[r, :].astype(f32) + inv * (sc - jnp.mean(sc, axis=-1, keepdims=True) - xh * jnp.mean(sc * xh, axis=-1, keepdims=True))
    out[r, :] = ig.astype(bf16)

PLAN = ("o0", "v0", "q0", "v1", "o1", "q1", "o2", "v2", "q2", "v3", "o3", "u0", "first", "vectors", "n0", "Ao", "q3", "d0", "n1", "n2",
        "n3", "Wo", "Aq", "u1", "ga", "Wq", "p0", "p3", "p1", "p2", "d1", "u2", "a3x", "a0x", "a3y", "sn", "a1x", "u3", "a0y", "d2",
        "a2x", "a2y", "Au", "a1y", "k", "Wu", "h1", "d3", "sa", "sg", "h2", "h0", "h3")

def NT(a, b): return lax.dot_general(a, b, (((1,), (1,)), ((), ())), preferred_element_type=f32)
def NN(a, b): return lax.dot_general(a, b, (((1,), (0,)), ((), ())), preferred_element_type=f32)
def TN(a, b): return lax.dot_general(a, b, (((0,), (0,)), ((), ())), preferred_element_type=f32)

def rotary_tables():
    pos = np.arange(LEN, dtype=np.float32)
    freq = (np.float32(rope_base) ** (-np.arange(0, ROT, 2, dtype=np.float32) / np.float32(ROT))).astype(np.float32)
    ang = (pos[:, None] * freq[None, :]).astype(np.float32)
    cos, sin = np.cos(ang).astype(np.float32), np.sin(ang).astype(np.float32)
    one, zero = np.ones((LEN, 32), np.float32), np.zeros((LEN, 16), np.float32)
    c = np.concatenate([cos, cos, one], 1)
    s1 = np.concatenate([-sin, zero, zero, zero], 1)
    s2 = np.concatenate([zero, sin, zero, zero], 1)
    return np.stack([np.concatenate([t, t], 1) for t in (c, s1, s2)])

def turn(u, tab, r, sign):
    other = pltpu.roll(u, 112, 1) * tab[1, r, :] + pltpu.roll(u, 16, 1) * tab[2, r, :]
    straight = u * tab[0, r, :]
    return straight + other if sign > 0 else straight - other


def pack(vec, gain, lbias, bout, bdown, bup, bqkv):
    dp = lax.axis_index("dp")
    k = lax.broadcasted_iota(jnp.int32, (64, 128), 0); l = lax.broadcasted_iota(jnp.int32, (64, 128), 1)
    up = NN(bup[...], ((l % 64 == k) & (l // 64 == dp % 2)).astype(bf16))
    k4 = k[0:4]; l4 = l[0:4]
    on = (l4 % 4 == k4) & ((l4 % 64) // 4 == dp)
    rows = [gain[...].astype(f32), lbias[...].astype(f32), bout[...].astype(f32), bdown[...].astype(f32), up]
    for j in range(3):
        lo = NN(bqkv[j], (on & (l4 < 64)).astype(bf16)); hi = NN(bqkv[j], (on & (l4 >= 64)).astype(bf16))
        rows += [lo[0:1] + hi[1:2], lo[2:3] + hi[3:4]]
    vec[...] = jnp.concatenate(rows + [jnp.zeros((21, 128), f32)], 0).astype(bf16)

def forward_kernel(gain_s, lbias_s, bout_s, bdown_s, bup_s, bqkv_s, wq, wout, wup, wdown, tok_h, cot_h, tab_h,
                   vecs, wq_f, wout_f, wup_f, wdown_f, rows_h, nrm_h, att_h, act_h, dact_h, gp_h,
                   vec, tab, vv, wqv, woutv, wupv, tok, cot, nrm, rowsv, bqkv, bup, q, k, v, ga, att, dk, dv, gp, act, dact,
                   ss, rs, ls, ld):
    c, y, zl, x, zh = place()
    loads = {}
    def load(i, src, dst):
        loads[i] = pltpu.make_async_copy(src, dst, ld.at[i]); loads[i].start()
    load(0, tok_h, tok); load(1, cot_h, cot); load(12, tab_h, tab)
    pack(vec, gain_s, lbias_s, bout_s, bdown_s, bup_s, bqkv_s)
    enter([peer(c, (y + 1) % 4, zl, x, zh), peer(c, (y + 3) % 4, zl, x, zh), peer(c, y, 1 - zl, x, zh), peer(1 - c, y, zl, x, zh)])
    gv, gq, go, gu, gd = every = [Gather(a, b, ax, ss.at[i], rs.at[i]) for i, (a, b, ax) in enumerate(
        [(vec, vecs, 0), (wq, wq_f, 2), (wout, wout_f, 1), (wup, wup_f, 0), (wdown, wdown_f, 1)])]
    local = [pltpu.make_async_copy(g.shard, g.slot(0, 0), ls.at[i]) for i, g in enumerate(every)]
    for cp in local: cp.start()

    def norm(lo, hi):
        gain, bias = rowsv[0:1, :], rowsv[1:2, :]
        def go_(i, carry):
            r = pl.ds(pl.multiple_of(lo + i * 128, 128), 128)
            a = tok[r, :].astype(f32)
            cen = a - jnp.mean(a, axis=-1, keepdims=True)
            inv = lax.rsqrt(jnp.mean(cen * cen, axis=-1, keepdims=True) + norm_epsilon)
            nrm[r, :] = (cen * inv * gain + bias).astype(bf16)
            return carry
        lax.fori_loop(0, (hi - lo) // 128, go_, 0)

    def project(lo, hi):
        def go_(i, carry):
            r = pl.ds(pl.multiple_of(lo + i * 256, 256), 256)
            n = nrm[r, :]
            for j, dst in enumerate((q, k, v)):
                p = NN(n, wqv[j])
                for h in range(2):
                    u = p[:, h * 128:(h + 1) * 128] + bqkv[2 * j + h:2 * j + h + 1, :]
                    dst[h, r, :] = (u if j == 2 else turn(u, tab, r, 1)).astype(bf16)
            return carry
        lax.fori_loop(0, (hi - lo) // 256, go_, 0)

    def grad_attended():
        def go_(i, carry):
            r = pl.ds(pl.multiple_of(i * 512, 512), 512)
            p = NT(cot[r, :], woutv[...])
            ga[0, r, :] = p[:, 0:128].astype(bf16); ga[1, r, :] = p[:, 128:256].astype(bf16)
            return carry
        lax.fori_loop(0, 2, go_, 0)

    def attention(i):
        lax.fori_loop(0, 2, lambda p, carry: attention_pair(i, p, carry), 0)
    def attention_pair(i, p, carry=0):
            n = (i + 1) * 256
            r = pl.ds(i * 256, 256)
            cols = pl.ds(pl.multiple_of(p * 128, 128), 128)
            a_, d_, tk, tv = 0.0, 0.0, 0.0, 0.0
            for hh in range(2):
                m = ((lax.broadcasted_iota(jnp.int32, (1, 128), 1) // 64) == hh).astype(bf16)
                kk = k[p, 0:n] * m; w = v[p, 0:n] * m; qq = q[p, r] * (m * 0.125); gg = ga[p, r] * m
                s = NT(kk, qq)
                key = lax.broadcasted_iota(jnp.int32, (256, 256), 0); row = lax.broadcasted_iota(jnp.int32, (256, 256), 1)
                diag = jnp.where(row >= key, s[n - 256:], -1e30)
                s = diag if i == 0 else jnp.concatenate([s[:n - 256], diag], 0)
                e = jnp.exp(s - jnp.max(s, 0, keepdims=True))
                pr = e * (1.0 / jnp.sum(e, 0, keepdims=True))
                low = pr.astype(bf16)
                dp = NT(w, gg)
                ds = (pr * (dp - jnp.sum(pr * dp, 0, keepdims=True))).astype(bf16)
                a_ = a_ + TN(low, w); d_ = d_ + TN(ds, kk)
                tk = tk + NN(ds, qq); tv = tv + NN(low, gg)
            att[r, cols] = a_.astype(bf16)
            gp[r, cols] = turn(d_ * 0.125, tab, r, -1).astype(bf16)
            if i == 3: dk[p] = tk; dv[p] = tv
            else:
                dk[p, 0:n] += tk; dv[p, 0:n] += tv
            return carry

    def keys_done():
        def go_(i, carry):
            r = pl.ds(pl.multiple_of(i * 256, 256), 256)
            for p in range(2):
                gp[r, 256 + p * 128:384 + p * 128] = turn(dk[p, r], tab, r, -1).astype(bf16)
                gp[r, 512 + p * 128:640 + p * 128] = dv[p, r].astype(bf16)
            return carry
        lax.fori_loop(0, 4, go_, 0)

    def hidden(lo, hi):
        def go_(i, carry):
            r = pl.ds(pl.multiple_of(lo + i * 256, 256), 256)
            n = nrm[r, :]
            for j in range(4):
                cols = pl.ds(j * 256, 256)
                h = NN(n, wupv[:, cols]) + bup[0:1, cols]
                h2 = h * h
                t = 0.5 + 0.5 * jnp.tanh(h * (0.7978845608028654 + 0.035677408136300125 * h2))
                y_ = h * t
                act[r, cols] = y_.astype(bf16)
                dact[r, cols] = (t + y_ * ((2.0 - 2.0 * t) * (0.7978845608028654 + 0.10703222440890037 * h2))).astype(bf16)
            return carry
        lax.fori_loop(0, (hi - lo) // 256, go_, 0)
        r = pl.ds(lo, hi - lo)
        load(13 + lo // 256, act.at[r], act_h.at[r]); load(17 + lo // 256, dact.at[r], dact_h.at[r])

    def first():
        gv.arrived(); local[0].wait(); load(2, vecs, vv)
    def vectors():
        loads[2].wait(); loads[0].wait()
        bq, bu = jnp.zeros((6, 128), f32), None
        for d in range(16):
            t = vv[pl.ds(d * 32, 32), :].astype(f32)
            cols = pl.ds(d * 128, 128)
            rowsv[0:1, cols] = t[0:1]; rowsv[1:2, cols] = t[1:2]; rowsv[2:3, cols] = t[2:3] + t[3:4]
            bq = bq + t[5:11]
            if d % 2 == 0: bu = t[4:5]
            else: bup[0:1, pl.ds((d // 2) * 128, 128)] = bu + t[4:5]
        bqkv[0:6, :] = bq
        load(6, rowsv, rows_h)
    def have_q():
        gq.arrived(); local[1].wait(); load(3, wq_f, wqv)
    def have_o():
        go.arrived(); local[2].wait(); load(4, wout_f, woutv)
    def have_u():
        gu.arrived(); local[3].wait(); load(7, wup_f, wupv)
    steps = {"first": first, "vectors": vectors, "Aq": have_q, "Ao": have_o, "Au": have_u,
             "Wq": lambda: (loads[3].wait(), loads[12].wait()), "Wo": lambda: (loads[4].wait(), loads[1].wait()), "Wu": lambda: loads[7].wait(),
             "ga": grad_attended, "k": keys_done, "sn": lambda: load(5, nrm, nrm_h), "sa": lambda: load(8, att, att_h), "sg": lambda: load(9, gp, gp_h)}
    for i in range(4):
        steps["n%d" % i] = partial(norm, i * 256, i * 256 + 256)
        steps["p%d" % i] = partial(project, i * 256, i * 256 + 256)
        steps["h%d" % i] = partial(hidden, i * 256, i * 256 + 256)
        steps["a%d" % i] = partial(attention, i)
        for p in range(2): steps["a%d%s" % (i, "xy"[p])] = partial(attention_pair, i, p)
    for nm, g in (("v", gv), ("q", gq), ("o", go), ("u", gu), ("d", gd)):
        steps[nm + "0"], steps[nm + "1"], steps[nm + "2"], steps[nm + "3"] = g.start, g.serve, g.serve2, g.serve3
    for name in PLAN: steps[name]()
    gd.arrived()
    for i in (5, 6, 8, 9, *range(13, 21)): loads[i].wait()
    local[4].wait()
    for g in (gv, gq, go, gu, gd):
        for cp in g.sends: cp.wait_send()

def forward(vectors, wq, wout, wup, wdown, tokens, cot, tab):
    A = pl.BlockSpec(memory_space=pl.ANY); V = pl.BlockSpec(memory_space=pltpu.VMEM)
    S = jax.ShapeDtypeStruct
    vm = lambda sh, t=bf16: pltpu.VMEM(sh, t)
    return pl.pallas_call(forward_kernel,
        out_shape=[S((512, 128), bf16), S((3, 2048, 256), bf16), S((256, 2048), bf16), S((2048, 1024), bf16), S((1024, 2048), bf16),
                   S((8, 2048), f32), S((1024, 2048), bf16), S((1024, 256), bf16), S((1024, 1024), bf16), S((1024, 1024), bf16), S((1024, 768), bf16)],
        in_specs=[V] * 6 + [A] * 7, out_specs=[A] * 11,
        scratch_shapes=[vm((32, 128)), vm((3, 1024, 128), f32), vm((512, 128)), vm((3, 2048, 256)), vm((256, 2048)), vm((2048, 1024)), vm((1024, 2048)), vm((1024, 2048)), vm((1024, 2048)),
                        vm((8, 2048), f32), vm((8, 128), f32), vm((8, 1024), f32), vm((2, 1024, 128)), vm((2, 1024, 128)), vm((2, 1024, 128)), vm((2, 1024, 128)),
                        vm((1024, 256)), vm((2, 1024, 128), f32), vm((2, 1024, 128), f32), vm((1024, 768)), vm((1024, 1024)), vm((1024, 1024)),
                        pltpu.SemaphoreType.DMA((5, 16)), pltpu.SemaphoreType.DMA((5, 16)), pltpu.SemaphoreType.DMA((5,)), pltpu.SemaphoreType.DMA((21,))],
        compiler_params=pltpu.CompilerParams(collective_id=1, has_side_effects=True, vmem_limit_bytes=60 << 20),
        name="gather_and_forward")(*vectors, wq, wout, wup, wdown, tokens, cot, tab)

PLAN_B = ("L0", "bB", "L1", "bA", "bD", "bC", "h0", "h1", "n0", "n1", "bM", "n2", "n3", "gS", "s2P0", "s2P1", "bL", "s2P2", "s2p0", "s2P3",
          "gM", "bN", "s2p1", "s21", "gL", "suP0", "gN", "s22", "mS", "suP1", "bias", "iS", "sup0", "sup1", "su1", "sqP0", "s23", "va", "vb", "mM",
          "sqP1", "vc", "su2", "sqp0", "iM", "sqp1", "mP", "vd", "mF", "sq1", "sq2", "su3", "iP", "s24", "iF", "ve", "mE", "sq3", "su4", "vf",
          "sq4", "iE")

class Scatter(Link):
    def __init__(s, g, sib, mid, ss, rs, width):
        super().__init__(ss, rs)
        s.g, s.b, s.m, s.w = g, sib, mid, width
    def to_sibling(s, k):
        return pltpu.make_async_remote_copy(s.g.at[k, 1 - s.c, :, pl.ds(0, s.w)], s.b.at[k], s.ss.at[k], s.rs.at[k],
                                            device_id=s.sib, device_id_type=MESH)
    def produce(s, lhs, rhs, lo, hi):
        n = rhs.shape[1]
        def go(j, carry):
            y = (s.y + 2 + 3 * j) % 4
            a = jnp.concatenate([lhs[:, pl.ds(pl.multiple_of((p * 4 + y) * 256, 256), 256)] for p in range(2)], 1)
            for at in range(0, n, 256):
                r = TN(a, rhs[:, at:at + 256]).astype(bf16)
                for p in range(2):
                    for cc in range(2): s.g[2 * j + p, cc, :, at:at + 256] = r[p * 256 + cc * 128:p * 256 + cc * 128 + 128]
            for p in range(2):
                s.to_sibling(2 * j + p).start()
            return carry
        lax.fori_loop(lo, hi, go, 0)
    def pairs(s, lo, hi):
        def go(k, carry):
            s.to_sibling(k).wait()
            mine = s.g.at[k, s.c]; dst = s.b.at[k]
            def rows(i, cc):
                r = pl.ds(pl.multiple_of(i * 32, 32), 32)
                dst[r, :] = (dst[r, :].astype(f32) + mine[r, 0:s.w].astype(f32)).astype(bf16)
                return cc
            lax.fori_loop(0, 4, rows, 0)
            return carry
        lax.fori_loop(lo, hi, go, 0)
    def serve1(s):
        s.send(8, s.b.at[0], s.m.at[0], s.yu); s.send(9, s.b.at[1], s.m.at[1], s.yd)
        s.send(10, s.b.at[3], s.m.at[4], s.yu); s.send(11, s.b.at[6], s.m.at[2], s.yd)
    def serve2(s):
        s.got(8, s.m.at[0]); add_into(s.b.at[2], [s.b.at[2], s.m.at[0]], 128, 32); s.send(12, s.b.at[2], s.m.at[3], s.yu)
        s.got(9, s.m.at[1]); add_into(s.b.at[7], [s.b.at[7], s.m.at[1]], 128, 32); s.send(13, s.b.at[7], s.m.at[5], s.yd)
    def serve3(s):
        for k, j in ((10, 4), (11, 2), (12, 3), (13, 5)): s.got(k, s.m.at[j])
        o = 1 - s.zl; b = s.b.at[4 + o]
        add_into(b, [b, s.m.at[2 + 2 * o], s.m.at[3 + 2 * o]], 128, 32); s.send(14, b, s.m.at[6], s.zn)
    def serve4(s, put):
        s.got(14, s.m.at[6])
        z = s.zl
        terms = (s.b.at[4 + z], s.m.at[2 + 2 * z], s.m.at[3 + 2 * z], s.m.at[6])
        def go(r):
            t = terms[0][r, :].astype(f32)
            for q in terms[1:]: t = t + q[r, :].astype(f32)
            put(r, t)
        by_rows(128, 32, go)

def backward_kernel(wq_f, wout_f, wup_f, wdown_f, rows_h, nrm_h, att_h, act_h, dact_h, gp_h, cot_h, tok_h,
                    mixed, ingrad, o2, oup, oq, osv,
                    wb, wch, cot, nrm, aa, pq, rowsv, tok, brp, gnp, own,
                    fa, t1a, t2a, zsa, zra, fb, t1b, t2b, zsb, zrb, g, sib2, m2, sibu, mu, sibq, mq,
                    v, rc, rz, ry, rx, rt, acc, sums, ss, rs, ld):
    c, y, zl, x, zh = place()
    t_own = zh * 4 + x
    o = 1 - zh
    loads = {}
    def load(i, src, dst):
        loads[i] = pltpu.make_async_copy(src, dst, ld.at[i]); loads[i].start()
    def wait(*ids):
        for i in ids: loads[i].wait()
    load(0, att_h, aa.at[:, pl.ds(0, 256)]); load(1, act_h, aa.at[:, pl.ds(256, 1024)])
    for j in range(4):
        cols = pl.ds(j * 512, 512)
        load(20 + j, wout_f.at[:, cols], wb.at[pl.ds(0, 256), cols]); load(24 + j, wdown_f.at[:, cols], wb.at[pl.ds(256, 1024), cols])
    enter(peers_all())
    bs = TensorSum(brp, fa, t1a, t2a, zsa, zra, ss.at[0], rs.at[0])
    gs = TensorSum(gnp, fb, t1b, t2b, zsb, zrb, ss.at[1], rs.at[1])
    mg = TensorGather(mixed, ss.at[2], rs.at[2])
    ig = TensorGather(ingrad, ss.at[3], rs.at[3])
    s2 = Scatter(g, sib2, m2, ss.at[4], rs.at[4], 1280)
    su = Scatter(g, sibu, mu, ss.at[5], rs.at[5], 1024)
    sq = Scatter(g, sibq, mq, ss.at[6], rs.at[6], 768)
    sm = SmallSum(v, rc, rz, ry, rx, rt, acc, osv, ss.at[7], rs.at[7])
    gp, gh = pq.at[:, pl.ds(0, 768)], pq.at[:, pl.ds(768, 1024)]

    def chunk(j):
        s = j % 2; r = pl.ds(j * 512, 512)
        for e in range(3): load(10 + 4 * s + e, wq_f.at[e, r], wch.at[s, :, pl.ds(e * 256, 256)])
        load(13 + 4 * s, wup_f.at[r], wch.at[s, :, pl.ds(768, 1024)])
    def first_loads(): wait(0, 1)
    def other_loads():
        load(4, cot_h, cot); load(5, dact_h, gh); load(6, gp_h, gp); chunk(0); chunk(1); load(7, nrm_h, nrm)
        load(8, rows_h, rowsv); load(9, tok_h.at[pl.ds(pl.multiple_of(t_own * 128, 128), 128)], tok)
    def branch(a, b, first=False):
        ra, rb = (pl.ds(pl.multiple_of(t * 128, 128), 128) for t in (a, b))
        lhs = jnp.concatenate([aa[ra, :], aa[rb, :]], 0)
        for j in range(4):
            if first: wait(20 + j, 24 + j)
            cols = pl.ds(j * 512, 512)
            p = NN(lhs, wb[:, cols]).astype(bf16)
            brp[a, :, cols] = p[0:128]; brp[b, :, cols] = p[128:256]
    def grad_hidden(lo, hi):
        if lo == 0: wait(4, 5)
        def go(i, carry):
            r = pl.ds(pl.multiple_of(i * 512, 512), 512)
            gr = cot[r, :]
            for j in range(4):
                p = NT(gr, wb[256 + j * 256:512 + j * 256, :])
                cols = pl.ds(768 + j * 256, 256)
                pq[r, cols] = (p * pq[r, cols].astype(f32)).astype(bf16)
            return carry
        lax.fori_loop(lo, hi, go, 0)
    def grad_normed(j):
        s = j % 2
        if j == 0: wait(6)
        wait(*range(10 + 4 * s, 14 + 4 * s))
        p = NT(pq[...], wch[s]).astype(bf16)
        gnp[:, :, j * 512:(j + 1) * 512] = p.reshape(8, 128, 512)
        if j + 2 < 4: chunk(j + 2)
    def bias_sums():
        ones = jnp.ones((16, 1024), bf16)
        for d in range(8):
            w = v.at[:, d // 4, d % 4]
            gb = NN(ones, cot[:, d * 256:(d + 1) * 256])[0:1]
            gu_ = NN(ones, gh[:, d * 128:(d + 1) * 128])[0:1]
            for cc in range(2):
                w[cc, 2:3, :] = gb[:, cc * 128:(cc + 1) * 128]; w[cc, 3:4, :] = gu_
        for j in range(3):
            gqb = NN(ones, gp[:, j * 256:(j + 1) * 256])[0:1]
            for d in range(16):
                w = v.at[d % 2, d // 8, (d // 2) % 4]
                w[4 + 2 * j:5 + 2 * j, :] = gqb[:, 0:128]; w[5 + 2 * j:6 + 2 * j, :] = gqb[:, 128:256]
    def mixed_start():
        bs.arrived()
        def mix(r): own[0, r, :] = (tok[r, :].astype(f32) + bs.total(r) + rowsv[2:3, :]).astype(bf16)
        wait(8, 9)
        by_rows(128, 64, mix)
        load(18, own.at[0], mixed.at[t_own])
        mg.start(own.at[0])
    def ingrad_start():
        gs.arrived()
        sums[...] = jnp.zeros_like(sums)
        cot_own = cot.at[pl.ds(pl.multiple_of(t_own * 128, 128), 128)]
        by_rows(128, 32, lambda r: norm_back_rows(r, gs.total(r), tok, cot_own, rowsv[0:1, :], own.at[1], sums))
        load(19, own.at[1], ingrad.at[t_own])
        ig.start(own.at[1])
    def norm_sums():
        sg = jnp.sum(sums[0], axis=0, keepdims=True); sb = jnp.sum(sums[1], axis=0, keepdims=True)
        for d in range(16):
            w = v.at[d % 2, d // 8, (d // 2) % 4]
            w[0:1, :] = sg[:, d * 128:(d + 1) * 128]; w[1:2, :] = sb[:, d * 128:(d + 1) * 128]
        sm.a()
    def put2(r, t): o2[r, :] = t
    def putu(r, t): oup[r, :] = t
    def putq(r, t): oq[r, :] = t
    def xp(k): return (x + k) % 4
    def far(): branch(o * 4 + xp(2), zh * 4 + xp(2)); bs.start_far()
    def near(): branch(o * 4 + xp(1), o * 4 + xp(3), True); bs.start_near()
    def near2(): branch(zh * 4 + xp(1), zh * 4 + xp(3)); bs.start_near2()
    def home(): branch(o * 4 + xp(0), zh * 4 + xp(0))
    def gn_start(): gs.start_far(); gs.start_near(); gs.start_near2()
    steps = {"L0": first_loads, "L1": other_loads, "bA": far, "bB": near, "bC": near2, "bD": home, "gS": gn_start, "bias": bias_sums,
             "mS": mixed_start, "iS": ingrad_start, "va": norm_sums, "vb": sm.b, "vc": sm.c_, "vd": sm.d, "ve": sm.e, "vf": sm.f,
             "h0": partial(grad_hidden, 0, 1), "h1": partial(grad_hidden, 1, 2),
             "s24": partial(s2.serve4, put2), "su4": partial(su.serve4, putu), "sq4": partial(sq.serve4, putq)}
    for i in range(4):
        steps["n%d" % i] = partial(grad_normed, i); steps["s2P%d" % i] = partial(s2.produce, cot, aa, i, i + 1)
    def up_grads(lo, hi):
        if lo == 0: wait(7)
        su.produce(nrm, gh, lo, hi)
    for i in range(2):
        steps["suP%d" % i] = partial(up_grads, 2 * i, 2 * i + 2); steps["sqP%d" % i] = partial(sq.produce, nrm, gp, 2 * i, 2 * i + 2)
        for nm, w in (("s2", s2), ("su", su), ("sq", sq)): steps[nm + "p%d" % i] = partial(w.pairs, 4 * i, 4 * i + 4)
    for nm, w in (("s2", s2), ("su", su), ("sq", sq)): steps[nm + "1"], steps[nm + "2"], steps[nm + "3"] = w.serve1, w.serve2, w.serve3
    for nm, w in (("b", bs), ("g", gs)): steps[nm + "M"], steps[nm + "N"], steps[nm + "L"] = w.middle, w.middle2, w.last
    for nm, w in (("m", mg), ("i", ig)): steps[nm + "M"], steps[nm + "P"], steps[nm + "F"], steps[nm + "E"] = w.middle, w.plane, w.far, w.finish
    for name in PLAN_B: steps[name]()
    wait(18, 19)
    for w in (gs, bs, mg, ig, s2, su, sq, sm): w.drain()

def backward(wq_f, wout_f, wup_f, wdown_f, rows, nrm, att, act, dact, gp, cot, tok):
    S = jax.ShapeDtypeStruct
    vm = lambda sh, t=bf16: pltpu.VMEM(sh, t)
    tsum = [vm((128, 2048)), vm((128, 2048)), vm((2, 2, 128, 2048)), vm((128, 2048)), vm((128, 2048))]
    A = pl.BlockSpec(memory_space=pl.ANY); V = pl.BlockSpec(memory_space=pltpu.VMEM)
    return pl.pallas_call(backward_kernel,
        out_shape=[S((8, 128, 2048), bf16)] * 2 + [S((128, 1280), f32), S((128, 1024), f32), S((128, 768), f32), S((16, 128), f32)],
        in_specs=[A] * 12, out_specs=[A] * 2 + [V] * 4,
        scratch_shapes=[vm((1280, 2048)), vm((2, 512, 1792)), vm((1024, 2048)), vm((1024, 2048)), vm((1024, 1280)), vm((1024, 1792)),
                        vm((8, 2048), f32), vm((128, 2048)), vm((8, 128, 2048)), vm((8, 128, 2048)), vm((2, 128, 2048))]
        + tsum + tsum + [vm((8, 2, 128, 1280)), vm((8, 128, 1280)), vm((7, 128, 1280)), vm((8, 128, 1024)), vm((7, 128, 1024)), vm((8, 128, 768)), vm((7, 128, 768)),
            vm((2, 2, 4, 16, 128), f32), vm((2, 4, 16, 128), f32), vm((4, 16, 128), f32), vm((3, 16, 128), f32), vm((3, 16, 128), f32), vm((16, 128), f32),
            vm((2, 16, 128), f32), vm((2, 8, 2048), f32),
            pltpu.SemaphoreType.DMA((8, 16)), pltpu.SemaphoreType.DMA((8, 16)), pltpu.SemaphoreType.DMA((28,))],
        compiler_params=pltpu.CompilerParams(collective_id=2, has_side_effects=True, vmem_limit_bytes=64 << 20),
        name="backward_and_sums")(wq_f, wout_f, wup_f, wdown_f, rows, nrm, att, act, dact, gp, cot, tok)

def hand_over_kernel(mixed, ingrad, o2_h, oup_h, oq_h, osv, mo, io, gg, gb, gq_h, gbq, go_h, gbo, gu_h, gbu, gd_h, gbd,
                     big, o2, oup, oq, gq, go, gd, li, lo):
    dp = lax.axis_index("dp")
    def copy(a, b, sem):
        cp = pltpu.make_async_copy(a, b, sem); cp.start()
        return cp
    n = 8
    ins = [copy((mixed, ingrad)[i // 4].at[pl.ds((i % 4) * 2, 2)], big.at[i], li.at[i]) for i in range(4)]
    small = [copy(o2_h, o2, li.at[n]), copy(oup_h, oup, li.at[n + 1]), copy(oq_h, oq, li.at[n + 2])]
    ins += [copy((mixed, ingrad)[i // 4].at[pl.ds((i % 4) * 2, 2)], big.at[i], li.at[i]) for i in range(4, 8)]
    outs = []
    def pass_on(i):
        ins[i].wait()
        for h in range(2): outs.append(copy(big.at[i, h], (mo, io)[i // 4].at[pl.ds((i % 4) * 256 + h * 128, 128)], lo.at[2 * i + h]))
    pass_on(0); pass_on(1)
    small[0].wait()
    for b in range(10):
        t = o2[:, b * 128:(b + 1) * 128].T
        if b < 2: go[b * 128:(b + 1) * 128, :] = t
        else: gd[(b - 2) * 128:(b - 1) * 128, :] = t
    outs += [copy(go, go_h, lo.at[16]), copy(gd, gd_h, lo.at[17])]
    pass_on(2); pass_on(3)
    small[1].wait(); outs.append(copy(oup, gu_h, lo.at[18]))
    small[2].wait()
    for j in range(3): gq[j] = oq[:, j * 256:(j + 1) * 256]
    outs.append(copy(gq, gq_h, lo.at[19]))
    pass_on(4); pass_on(5)
    gg[...] = osv[0:1, :]; gb[...] = osv[1:2, :]; gbo[...] = osv[2:3, :]; gbd[...] = osv[2:3, :]
    l = lax.broadcasted_iota(jnp.int32, (128, 64), 0); k = lax.broadcasted_iota(jnp.int32, (128, 64), 1)
    gbu[...] = lax.dot_general(osv[3:4, :], (l == k + 64 * (dp % 2)).astype(f32), (((1,), (0,)), ((), ())), precision=lax.Precision.HIGHEST)
    l = lax.broadcasted_iota(jnp.int32, (128, 4), 0); k = lax.broadcasted_iota(jnp.int32, (128, 4), 1)
    for j in range(3):
        rows = osv[4 + 2 * j:6 + 2 * j, :]
        lo_, hi_ = (lax.dot_general(rows, (l == k + 4 * dp + 64 * h).astype(f32), (((1,), (0,)), ((), ())), precision=lax.Precision.HIGHEST) for h in (0, 1))
        gbq[j] = jnp.concatenate([lo_[0:1], hi_[0:1], lo_[1:2], hi_[1:2]], 0)
    pass_on(6); pass_on(7)
    for cp in outs: cp.wait()

def hand_over(mixed, ingrad, o2, oup, oq, osv):
    S = jax.ShapeDtypeStruct
    A = pl.BlockSpec(memory_space=pltpu.HBM)
    full = lambda sh: pl.BlockSpec(sh, lambda: (0,) * len(sh))
    outs = [((1, 128), 0), ((1, 128), 0), ((3, 128, 256), 1), ((3, 4, 4), 0), ((256, 128), 1), ((1, 128), 0), ((128, 1024), 1), ((1, 64), 0), ((1024, 128), 1), ((1, 128), 0)]
    vm = lambda sh: pltpu.VMEM(sh, f32)
    return pl.pallas_call(hand_over_kernel,
        out_shape=[S((1024, 2048), bf16)] * 2 + [S(sh, f32) for sh, _ in outs],
        in_specs=[A] * 5 + [full((16, 128))], out_specs=[A] * 2 + [A if m else full(sh) for sh, m in outs],
        scratch_shapes=[pltpu.VMEM((8, 2, 128, 2048), bf16), vm((128, 1280)), vm((128, 1024)), vm((128, 768)), vm((3, 128, 256)), vm((256, 128)), vm((1024, 128)),
                        pltpu.SemaphoreType.DMA((12,)), pltpu.SemaphoreType.DMA((20,))],
        compiler_params=pltpu.CompilerParams(vmem_limit_bytes=62 << 20),
        name="hand_over")(mixed, ingrad, o2, oup, oq, osv)

def body(tokens, ln_gain, ln_bias, w_qkv, b_qkv, w_out, b_out, w_up, b_up, w_down, b_down, cotangent):
    row = lambda a: a.reshape(1, 128)
    vecs, wq_f, wout_f, wup_f, wdown_f, rows, nrm, att, act, dact, gp = forward(
        (row(ln_gain), row(ln_bias), row(b_out), row(b_down), b_up, b_qkv), w_qkv.transpose(1, 0, 2), w_out, w_up, w_down,
        tokens, cotangent, jnp.asarray(rotary_tables()))
    parts = backward(wq_f, wout_f, wup_f, wdown_f, rows, nrm, att, act, dact, gp, cotangent, tokens)
    mixed, ingrad, gg, gb, gq, gbq, go, gbo, gu, gbu, gd, gbd = hand_over(*parts)
    return (mixed, ingrad, gg.reshape(128), gb.reshape(128), gq.transpose(1, 0, 2), gbq, go, gbo.reshape(128), gu, gbu, gd, gbd.reshape(128))


def solution(mesh):
    in_specs = (
        P("dp", None),
        P("dp"),
        P("dp"),
        P("dp", None, "tensor"),
        P(None, "tensor", "dp"),
        P("tensor", "dp"),
        P("dp"),
        P("dp", "tensor"),
        P("tensor", "dp"),
        P("tensor", "dp"),
        P("dp"),
        P("dp", None),
    )
    out_specs = (
        P("dp", None),
        P("dp", None),
        P("dp"),
        P("dp"),
        P("dp", None, "tensor"),
        P(None, "tensor", "dp"),
        P("tensor", "dp"),
        P("dp"),
        P("dp", "tensor"),
        P("tensor", "dp"),
        P("tensor", "dp"),
        P("dp"),
    )
    return jax.shard_map(body, mesh=mesh, in_specs=in_specs, out_specs=out_specs, check_vma=False)
```

```python
from functools import partial

import jax
import jax.numpy as jnp
import numpy as np
from jax import lax
from jax.sharding import PartitionSpec as P
from jax.experimental import pallas as pl
from jax.experimental.pallas import tpu as pltpu

HD = 64
ROT = 32
LEN = 1024
norm_epsilon = 1e-05
rope_base = 10000.0
MESH = pl.DeviceIdType.MESH

def place():
    dp = lax.axis_index("dp"); tn = lax.axis_index("tensor")
    return dp % 2, (dp // 2) % 4, dp // 8, tn % 4, tn // 4

def peer(c, y, zl, x, zh):
    return (zl * 8 + y * 2 + c, zh * 4 + x)

RELS = [(0, 0), (0, 1), (0, 3), (0, 2), (1, 0), (1, 1), (1, 3), (1, 2)]

def enter(devices):
    bar = pltpu.get_barrier_semaphore()
    for d in devices:
        pl.semaphore_signal(bar, inc=1, device_id=d, device_id_type=MESH)
    pl.semaphore_wait(bar, len(devices))

class Gather:
    def __init__(s, shard, full, axis, ss, rs, by_z=False):
        s.by_z = by_z
        s.axis, s.ss, s.rs, s.full = axis, ss, rs, full
        s.c, s.y, s.zl, x, zh = place()
        c, y, zl = s.c, s.y, s.zl
        s.total = shard.shape[1 if axis == 2 else 0]
        s.shard = shard
        s.up = peer(c, (y + 1) % 4, zl, x, zh); s.down = peer(c, (y + 3) % 4, zl, x, zh)
        s.z = peer(c, y, 1 - zl, x, zh); s.sib = peer(1 - c, y, zl, x, zh)
        s.sends = []
    def slot(s, dz, dy, c=None, half=None):
        c = s.c if c is None else c
        d = ((s.zl + dz) % 2) * 8 + ((s.y + dy) % 4) * 2 + c
        n = s.total if half is None else s.total // 2
        lo = 0 if half is None else half * n
        if s.axis == 0: return s.full.at[pl.ds(pl.multiple_of(d * s.total + lo, 16), n)]
        if s.axis == 2: return s.full.at[:, pl.ds(pl.multiple_of(d * s.total + lo, 16), n)]
        return s.full.at[pl.ds(lo, n), pl.ds(pl.multiple_of(d * 128, 128), 128)]
    def send(s, kind, src, dst, dev):
        cp = pltpu.make_async_remote_copy(src, dst, s.ss.at[kind], s.rs.at[kind], device_id=dev, device_id_type=MESH)
        cp.start(); s.sends.append((kind, src.shape))
    def got(s, kind, dst):
        pltpu.make_async_remote_copy(dst, dst, s.ss.at[kind], s.rs.at[kind], device_id=s.sib, device_id_type=MESH).wait_recv()
    def start(s):
        own = s.slot(0, 0)
        s.send(0, s.shard, own, s.up); s.send(1, s.shard, own, s.down); s.send(2, s.shard, own, s.z)
        s.send(8, s.shard, own, s.sib)
    def relay(s, rel):
        b = s.slot(*RELS[rel]); s.send(8 + rel, b, b, s.sib)
    def serve(s):
        a = s.slot(0, 3); s.got(0, a); h = s.slot(0, 3, half=0); s.send(5, h, h, s.up)
        b = s.slot(0, 1); s.got(1, b); h = s.slot(0, 1, half=1); s.send(6, h, h, s.down)
        z = s.slot(1, 0); s.got(2, z)
        if s.by_z:
            s.send(3, a, a, s.z); s.send(4, b, b, s.z)
        else:
            s.send(3, z, z, s.up); s.send(4, z, z, s.down)
        s.relay(2); s.relay(1); s.relay(4)
    def serve2(s):
        s.got(5, s.slot(0, 2, half=0)); s.got(6, s.slot(0, 2, half=1))
        f = s.slot(0, 2); s.send(7, f, f, s.z); s.relay(3)
    def serve3(s):
        s.got(3, s.slot(1, 3)); s.relay(6)
        s.got(4, s.slot(1, 1)); s.relay(5)
        s.got(7, s.slot(1, 2)); s.relay(7)
    def arrived(s, plane=None):
        for r in range(8):
            if plane in (None, r // 4): s.got(8 + r, s.slot(*RELS[r], c=1 - s.c))
    def drain(s):
        for kind, shape in s.sends:
            r = s.shard
            if shape != r.shape: r = r.at[:, pl.ds(0, s.total // 2)] if s.axis == 2 else r.at[pl.ds(0, s.total // 2)]
            pltpu.make_async_remote_copy(r, r, s.ss.at[kind], s.rs.at[kind], device_id=s.sib, device_id_type=MESH).wait_send()

f32 = jnp.float32
bf16 = jnp.bfloat16

def by_rows(rows, step, fn):
    def go(i, carry):
        fn(pl.ds(pl.multiple_of(i * step, step), step))
        return carry
    lax.fori_loop(0, rows // step, go, 0)

def add_into(dst, terms, rows, step, lo=0):
    def go(r):
        if lo: r = pl.ds(pl.multiple_of(r.start + lo, step), step)
        total = terms[0][r, :].astype(f32)
        for t in terms[1:]: total = total + t[r, :].astype(f32)
        dst[r, :] = total.astype(dst.dtype)
    by_rows(rows, step, go)

class Link:
    def __init__(s, ss, rs):
        s.ss, s.rs, s.sends = ss, rs, []
        c, y, zl, x, zh = s.at = place()
        s.c, s.y, s.zl, s.x, s.zh = s.at
        s.sib = peer(1 - c, y, zl, x, zh)
        s.yu, s.yd, s.yf = (peer(c, (y + k) % 4, zl, x, zh) for k in (1, 3, 2))
        s.zn = peer(c, y, 1 - zl, x, zh)
        s.xu, s.xd, s.xf = (peer(c, y, zl, (x + k) % 4, zh) for k in (1, 3, 2))
        s.zf = peer(c, y, zl, x, 1 - zh)
    def send(s, kind, src, dst, dev):
        cp = pltpu.make_async_remote_copy(src, dst, s.ss.at[kind], s.rs.at[kind], device_id=dev, device_id_type=MESH)
        cp.start(); s.sends.append((kind, src.shape))
    def got(s, kind, dst):
        pltpu.make_async_remote_copy(dst, dst, s.ss.at[kind], s.rs.at[kind], device_id=s.sib, device_id_type=MESH).wait_recv()
    def like(s, shape): raise NotImplementedError
    def drain(s):
        for kind, shape in s.sends:
            r = s.like(shape)
            pltpu.make_async_remote_copy(r, r, s.ss.at[kind], s.rs.at[kind], device_id=s.sib, device_id_type=MESH).wait_send()

class TensorSum(Link):
    def __init__(s, b, f, t1, t2, zs, zr, ss, rs):
        super().__init__(ss, rs)
        s.b, s.f, s.t1, s.t2, s.zs, s.zr = b, f, t1, t2, zs, zr
    def blk(s, zh, dx): return s.b.at[zh * 4 + (s.x + dx) % 4]
    def like(s, shape): return s.b.at[0, pl.ds(0, shape[0]), pl.ds(0, shape[1])]
    LO, HI = pl.ds(0, 64), pl.ds(64, 64)
    def start_far(s): s.send(0, s.blk(1 - s.zh, 2), s.f, s.zf)
    def start_near(s, cols, k):
        o = 1 - s.zh
        s.send(k + 1, s.blk(o, 1).at[:, cols], s.t2.at[0, o, :, cols], s.xu); s.send(k + 2, s.blk(o, 3).at[:, cols], s.t2.at[1, o, :, cols], s.xd)
    def start_near2(s):
        s.send(3, s.blk(s.zh, 1).at[s.HI], s.t2.at[0, s.zh, s.HI], s.xu); s.send(4, s.blk(s.zh, 3).at[s.LO], s.t2.at[1, s.zh, s.LO], s.xd)
    def middle(s):
        s.got(0, s.f); add_into(s.f, [s.f, s.blk(s.zh, 2)], 128, 32)
        s.send(5, s.f.at[s.LO], s.t1.at[s.LO], s.xu); s.send(6, s.f.at[s.HI], s.t1.at[s.HI], s.xd)
    def middle2(s):
        s.got(5, s.t1.at[s.LO]); add_into(s.t1, [s.t1, s.blk(s.zh, 1)], 64, 32)
        s.send(7, s.t1.at[s.LO], s.t2.at[0, s.zh, s.LO], s.xu)
        s.got(6, s.t1.at[s.HI]); add_into(s.t1, [s.t1, s.blk(s.zh, 3)], 64, 32, lo=64)
        s.send(8, s.t1.at[s.HI], s.t2.at[1, s.zh, s.HI], s.xd)
    def last(s):
        o = 1 - s.zh
        for k in (1, 10):
            s.got(k, s.t2.at[0, o, :, pl.ds(0, 1024)]); s.got(k + 1, s.t2.at[1, o, :, pl.ds(0, 1024)])
        add_into(s.zs, [s.blk(o, 0), s.t2.at[0, o], s.t2.at[1, o]], 128, 32)
        s.send(9, s.zs, s.zr, s.zf)
    def total(s, r):
        return (s.blk(s.zh, 0)[r, :].astype(f32) + s.t2.at[0, s.zh][r, :].astype(f32)
                + s.t2.at[1, s.zh][r, :].astype(f32) + s.zr[r, :].astype(f32))
    def arrived(s):
        z = s.zh
        s.got(3, s.t2.at[0, z, s.HI]); s.got(4, s.t2.at[1, z, s.LO]); s.got(7, s.t2.at[0, z, s.LO]); s.got(8, s.t2.at[1, z, s.HI])
        s.got(9, s.zr)

class TensorGather(Link):
    def __init__(s, o, ss, rs):
        super().__init__(ss, rs); s.o = o
    def blk(s, zh, dx): return s.o.at[zh * 4 + (s.x + dx) % 4]
    def like(s, shape): return s.o.at[0, pl.ds(0, shape[0])]
    LO, HI = pl.ds(0, 64), pl.ds(64, 64)
    def start(s, own):
        b = s.blk(s.zh, 0)
        s.send(0, own, b, s.xu); s.send(1, own, b, s.xd); s.send(2, own, b, s.zf)
    def middle(s):
        b = s.blk(s.zh, 3); s.got(0, b); s.send(3, b.at[s.LO], b.at[s.LO], s.xu)
        b = s.blk(s.zh, 1); s.got(1, b); s.send(4, b.at[s.HI], b.at[s.HI], s.xd)
    def plane(s):
        b = s.blk(1 - s.zh, 0); s.got(2, b); s.send(5, b, b, s.xu); s.send(6, b, b, s.xd)
    def far(s):
        b = s.blk(s.zh, 2); s.got(3, b.at[s.LO]); s.got(4, b.at[s.HI]); s.send(7, b, b, s.zf)
    def finish(s):
        o = 1 - s.zh
        s.got(5, s.blk(o, 3)); s.got(6, s.blk(o, 1)); s.got(7, s.blk(o, 2))

class SmallSum(Link):
    def __init__(s, v, rc, rz, ry, rx, rt, acc, out, ss, rs):
        super().__init__(ss, rs)
        s.v, s.rc, s.rz, s.ry, s.rx, s.rt, s.acc, s.out = v, rc, rz, ry, rx, rt, acc, out
    def like(s, shape):
        return s.v.at[0] if len(shape) == 4 else s.rc.at[0] if len(shape) == 3 else s.rt
    def a(s): s.send(0, s.v.at[1 - s.c], s.rc, s.sib)
    def b(s):
        s.got(0, s.rc); s.rc[...] = s.rc[...] + s.v[s.c]
        s.send(1, s.rc.at[1 - s.zl], s.rz, s.zn)
    def c_(s):
        s.got(1, s.rz); s.rz[...] = s.rz[...] + s.rc[s.zl]
        s.send(2, s.rz.at[(s.y + 1) % 4], s.ry.at[0], s.yu); s.send(3, s.rz.at[(s.y + 3) % 4], s.ry.at[1], s.yd)
        s.send(4, s.rz.at[(s.y + 2) % 4], s.ry.at[2], s.yf)
    def d(s):
        for k in range(3): s.got(2 + k, s.ry.at[k])
        s.acc[0] = s.rz[s.y] + s.ry[0] + s.ry[1] + s.ry[2]
        s.send(5, s.acc.at[0], s.rx.at[0], s.xu); s.send(6, s.acc.at[0], s.rx.at[1], s.xd); s.send(7, s.acc.at[0], s.rx.at[2], s.xf)
    def e(s):
        for k in range(3): s.got(5 + k, s.rx.at[k])
        s.acc[1] = s.acc[0] + s.rx[0] + s.rx[1] + s.rx[2]
        s.send(8, s.acc.at[1], s.rt, s.zf)
    def f(s):
        s.got(8, s.rt)
        first = lax.broadcasted_iota(jnp.int32, (16, 128), 0) < 2
        s.out[...] = jnp.where(first, s.acc[1] + s.rt[...], s.acc[0])

def peers_all():
    c, y, zl, x, zh = place()
    return ([peer(1 - c, y, zl, x, zh), peer(c, y, 1 - zl, x, zh), peer(c, y, zl, x, 1 - zh)]
            + [peer(c, (y + k) % 4, zl, x, zh) for k in (1, 2, 3)] + [peer(c, y, zl, (x + k) % 4, zh) for k in (1, 2, 3)])

def norm_back_rows(r, gn, tokens, cot, gain, out, sums):
    x = tokens[r, :].astype(f32)
    mean = jnp.mean(x, axis=-1, keepdims=True); cen = x - mean
    inv = lax.rsqrt(jnp.mean(cen * cen, axis=-1, keepdims=True) + 1e-5)
    xh = cen * inv
    n = x.shape[0] // 8
    sums[0] += jnp.sum((gn * xh).reshape(n, 8, 2048), axis=0)
    sums[1] += jnp.sum(gn.reshape(n, 8, 2048), axis=0)
    sc = gn * gain
    ig = cot[r, :].astype(f32) + inv * (sc - jnp.mean(sc, axis=-1, keepdims=True) - xh * jnp.mean(sc * xh, axis=-1, keepdims=True))
    out[r, :] = ig.astype(bf16)

PLAN = ("v0", "o0", "q0", "v1", "o1", "q1", "o2", "v2", "q2", "u0", "v3", "first", "o3", "d0", "q3", "vectors", "N3", "Ao", "N2", "Wo",
        "Aq", "Lq", "N0", "u1", "ga", "Wq", "p2", "N1", "p0", "p3", "d1", "p1", "u2", "a3", "a1", "f2", "u3", "f1", "d2", "a2",
        "f0", "Au", "f3", "Ad1", "Wu", "H1", "d3", "H3", "H2", "H0", "Ad2", "bB1", "a0", "bB2", "bA", "bC", "bD", "h0", "k", "h1")

PLAN_B = ("n0", "n1", "bM", "n2", "n3", "gS", "s2P0", "s2P1", "s2P2", "s2P3", "gM", "bN", "bL", "s2p0", "s2p1", "s21", "suP0", "suP1", "sup0", "s22",
          "gL", "gN", "mS", "sup1", "bias", "s23", "iS", "sqP0", "su1", "sqP1", "mM", "sqp0", "su2", "iM", "s24", "va", "vb", "mF", "sqp1", "iP",
          "vc", "su3", "vd", "iF", "sq1", "su4", "mP", "sq2", "ve", "sq3", "vf", "sq4", "iE", "mE")

GC = 512

def NT(a, b): return lax.dot_general(a, b, (((1,), (1,)), ((), ())), preferred_element_type=f32)
def NN(a, b): return lax.dot_general(a, b, (((1,), (0,)), ((), ())), preferred_element_type=f32)
def TN(a, b): return lax.dot_general(a, b, (((0,), (0,)), ((), ())), preferred_element_type=f32)

def rotary_tables():
    pos = np.arange(LEN, dtype=np.float32)
    freq = (np.float32(rope_base) ** (-np.arange(0, ROT, 2, dtype=np.float32) / np.float32(ROT))).astype(np.float32)
    ang = (pos[:, None] * freq[None, :]).astype(np.float32)
    cos, sin = np.cos(ang).astype(np.float32), np.sin(ang).astype(np.float32)
    one, zero = np.ones((LEN, 32), np.float32), np.zeros((LEN, 16), np.float32)
    c = np.concatenate([cos, cos, one], 1)
    s = np.concatenate([sin, sin, zero, zero], 1)
    return np.stack([np.concatenate([t, t], 1) for t in (c, s)])

def turn(u, tab, r, sign):
    low = lax.broadcasted_iota(jnp.int32, (1, 128), 1) % 64 < 16
    other = jnp.where(low, -pltpu.roll(u, 112, 1), pltpu.roll(u, 16, 1)) * tab[1, r, :]
    straight = u * tab[0, r, :]
    return straight + other if sign > 0 else straight - other


def pack(vec, gain, lbias, bout, bdown, bup, bqkv):
    dp = lax.axis_index("dp")
    k = lax.broadcasted_iota(jnp.int32, (64, 128), 0); l = lax.broadcasted_iota(jnp.int32, (64, 128), 1)
    up = NN(bup[...], ((l % 64 == k) & (l // 64 == dp % 2)).astype(bf16))
    k4 = k[0:4]; l4 = l[0:4]
    on = (l4 % 4 == k4) & ((l4 % 64) // 4 == dp)
    rows = [gain[...].astype(f32), lbias[...].astype(f32), bout[...].astype(f32), bdown[...].astype(f32), up]
    for j in range(3):
        lo = NN(bqkv[j], (on & (l4 < 64)).astype(bf16)); hi = NN(bqkv[j], (on & (l4 >= 64)).astype(bf16))
        rows += [lo[0:1] + hi[1:2], lo[2:3] + hi[3:4]]
    vec[...] = jnp.concatenate(rows + [jnp.zeros((21, 128), f32)], 0).astype(bf16)

class Scatter(Link):
    def __init__(s, g, sib, mid, ss, rs, width):
        super().__init__(ss, rs)
        s.g, s.b, s.m, s.w = g, sib, mid, width
    def like(s, shape): return s.b.at[0]
    def to_sibling(s, k):
        return pltpu.make_async_remote_copy(s.g.at[k, 1 - s.c, :, pl.ds(0, s.w)], s.b.at[k], s.ss.at[k], s.rs.at[k],
                                            device_id=s.sib, device_id_type=MESH)
    def produce(s, lhs, rhs, lo, hi):
        n = rhs.shape[1]
        def go(j, carry):
            y = (s.y + 2 + 3 * j) % 4
            a = jnp.concatenate([lhs[:, pl.ds(pl.multiple_of((p * 4 + y) * 256, 256), 256)] for p in range(2)], 1)
            for at in range(0, n, 256):
                r = TN(a, rhs[:, at:at + 256]).astype(bf16)
                for p in range(2):
                    for cc in range(2): s.g[2 * j + p, cc, :, at:at + 256] = r[p * 256 + cc * 128:p * 256 + cc * 128 + 128]
            for p in range(2):
                s.to_sibling(2 * j + p).start()
            return carry
        lax.fori_loop(lo, hi, go, 0)
    def pairs(s, lo, hi):
        def go(k, carry):
            s.to_sibling(k).wait()
            mine = s.g.at[k, s.c]; dst = s.b.at[k]
            def rows(i, cc):
                r = pl.ds(pl.multiple_of(i * 32, 32), 32)
                dst[r, :] = (dst[r, :].astype(f32) + mine[r, 0:s.w].astype(f32)).astype(bf16)
                return cc
            lax.fori_loop(0, 4, rows, 0)
            return carry
        lax.fori_loop(lo, hi, go, 0)
    def serve1(s):
        s.send(8, s.b.at[0], s.m.at[0], s.yu); s.send(9, s.b.at[1], s.m.at[1], s.yd)
        s.send(10, s.b.at[3], s.m.at[4], s.yu); s.send(11, s.b.at[6], s.m.at[2], s.yd)
    def serve2(s):
        s.got(8, s.m.at[0]); add_into(s.b.at[2], [s.b.at[2], s.m.at[0]], 128, 32); s.send(12, s.b.at[2], s.m.at[3], s.yu)
        s.got(9, s.m.at[1]); add_into(s.b.at[7], [s.b.at[7], s.m.at[1]], 128, 32); s.send(13, s.b.at[7], s.m.at[5], s.yd)
    def serve3(s):
        for k, j in ((10, 4), (11, 2), (12, 3), (13, 5)): s.got(k, s.m.at[j])
        o = 1 - s.zl; b = s.b.at[4 + o]
        add_into(b, [b, s.m.at[2 + 2 * o], s.m.at[3 + 2 * o]], 128, 32); s.send(14, b, s.m.at[6], s.zn)
    def serve4(s, put):
        s.got(14, s.m.at[6])
        z = s.zl
        terms = (s.b.at[4 + z], s.m.at[2 + 2 * z], s.m.at[3 + 2 * z], s.m.at[6])
        def go(r):
            t = terms[0][r, :].astype(f32)
            for q in terms[1:]: t = t + q[r, :].astype(f32)
            put(r, t)
        by_rows(128, 32, go)

def layer_kernel(gain_s, lbias_s, bout_s, bdown_s, bup_s, bqkv_s, wq, wout, wup, wdown, tok_h, cot_h, tab_h,
                 vecs, wq_f, wout_f, wup_f, wdown_f, mixed, ingrad, o2_h, oup_h, oq_h, osv,
                 vec, wb, cot, nrm, aa, pq, rowsv, tok, brp, own,
                 fa, t1a, t2a, zsa, zra, fb, t1b, t2b, zsb, zrb, sib2, m2, sibu, mu, sibq, mq,
                 v, rc, rz, ry, rx, rt, acc, sums, gss, grs, gls, ss, rs, ld):
    c, y, zl, x, zh = place()
    t_own = zh * 4 + x
    o = 1 - zh
    own_rows = pl.ds(pl.multiple_of(t_own * 128, 128), 128)
    loads = {}
    def load(key, src, dst):
        loads[key] = pltpu.make_async_copy(src, dst, ld.at[len(loads)]); loads[key].start()
    def wait(*keys):
        for k in keys: loads[k].wait()
    load("tok", tok_h, nrm); load("cot", cot_h, cot); load("own", tok_h.at[own_rows], tok)
    pack(vec, gain_s, lbias_s, bout_s, bdown_s, bup_s, bqkv_s)
    gv, gq, go, gu, gd = every = [Gather(a, b, ax, gss.at[i], grs.at[i], i == 2) for i, (a, b, ax) in enumerate(
        [(vec, vecs, 0), (wq, wq_f, 2), (wout, wout_f, 1), (wup, wup_f, 0), (wdown, wdown_f, 1)])]
    local = [pltpu.make_async_copy(g.shard, g.slot(0, 0), gls.at[i]) for i, g in enumerate(every)]
    for cp in local: cp.start()
    enter(peers_all())
    bs = TensorSum(brp, fa, t1a, t2a, zsa, zra, ss.at[0], rs.at[0])
    mg = TensorGather(mixed, ss.at[2], rs.at[2])
    ig = TensorGather(ingrad, ss.at[3], rs.at[3])
    sm = SmallSum(v, rc, rz, ry, rx, rt, acc, osv, ss.at[7], rs.at[7])
    gp, gh = pq.at[:, pl.ds(0, 768)], pq.at[:, pl.ds(768, 1024)]

    def have_q():
        gq.arrived(); local[1].wait()
    def have_o():
        go.arrived(); local[2].wait(); load("o", wout_f, wb.at[pl.ds(0, 256)])
    def half(h): return pl.ds(pl.multiple_of(((zl + h) % 2) * 1024, 1024), 1024)
    def have_d(h):
        gd.arrived(h)
        if h == 0: local[4].wait()
        load(("d", h), wdown_f.at[:, half(h)], wb.at[pl.ds(256, 1024), half(h)])
    def near(h):
        ra, rb = (pl.ds(pl.multiple_of((o * 4 + (x + k) % 4) * 128, 128), 128) for k in (1, 3))
        lhs = jnp.concatenate([aa[ra, :], aa[rb, :]], 0)
        wait(("d", h))
        p = NN(lhs, wb[:, half(h)]).astype(bf16)
        brp[o * 4 + (x + 1) % 4, :, half(h)] = p[0:128]; brp[o * 4 + (x + 3) % 4, :, half(h)] = p[128:256]
        bs.start_near(half(h), 9 * h)
    def branch(a, b):
        ra, rb = (pl.ds(pl.multiple_of(t * 128, 128), 128) for t in (a, b))
        lhs = jnp.concatenate([aa[ra, :], aa[rb, :]], 0)
        for j in range(4):
            cols = pl.ds(j * 512, 512)
            p = NN(lhs, wb[:, cols]).astype(bf16)
            brp[a, :, cols] = p[0:128]; brp[b, :, cols] = p[128:256]
    def grad_hidden(lo, hi):
        def go(i, carry):
            r = pl.ds(pl.multiple_of(i * 512, 512), 512)
            gr = cot[r, :]
            for j in range(4):
                p = NT(gr, wb[256 + j * 256:512 + j * 256, :])
                cols = pl.ds(768 + j * 256, 256)
                pq[r, cols] = (p * pq[r, cols].astype(f32)).astype(bf16)
            return carry
        lax.fori_loop(lo, hi, go, 0)
    def mixed_start():
        bs.arrived()
        def mix(r): own[0, r, :] = (tok[r, :].astype(f32) + bs.total(r) + rowsv[2:3, :]).astype(bf16)
        wait("own")
        by_rows(128, 64, mix)
        load("mixed", own.at[0], mixed.at[t_own])
        mg.start(own.at[0])
    def xp(k): return (x + k) % 4
    def far(): branch(o * 4 + xp(2), zh * 4 + xp(2)); bs.start_far()
    def near2(): branch(zh * 4 + xp(1), zh * 4 + xp(3)); bs.start_near2()
    def home(): branch(o * 4 + xp(0), zh * 4 + xp(0))
    steps = {"Aq": have_q, "Ao": have_o, "Ad1": partial(have_d, 0), "Ad2": partial(have_d, 1), "Wo": lambda: wait("o", "cot"), "bA": far, "bB1": partial(near, 0), "bB2": partial(near, 1), "bC": near2, "bD": home,
             "mS": mixed_start, "h0": partial(grad_hidden, 0, 1), "h1": partial(grad_hidden, 1, 2)}
    for nm, g in (("v", gv), ("q", gq), ("o", go), ("u", gu), ("d", gd)):
        steps[nm + "0"], steps[nm + "1"], steps[nm + "2"], steps[nm + "3"] = g.start, g.serve, g.serve2, g.serve3
    steps["bM"], steps["bN"], steps["bL"] = bs.middle, bs.middle2, bs.last
    for nm, w in (("m", mg), ("i", ig)): steps[nm + "M"], steps[nm + "P"], steps[nm + "F"], steps[nm + "E"] = w.middle, w.plane, w.far, w.finish

    def forward_part(tab, vv, wqu, bqkv, bup, q, k, val, ga, dk, dv):
        load("tab", tab_h, tab)
        def first():
            gv.arrived(); local[0].wait(); load("vv", vecs, vv)
        def vectors():
            wait("vv", "tok")
            bq, bu = jnp.zeros((6, 128), f32), None
            for d in range(16):
                t = vv[pl.ds(d * 32, 32), :].astype(f32)
                cols = pl.ds(d * 128, 128)
                rowsv[0:1, cols] = t[0:1]; rowsv[1:2, cols] = t[1:2]; rowsv[2:3, cols] = t[2:3] + t[3:4]
                bq = bq + t[5:11]
                if d % 2 == 0: bu = t[4:5]
                else: bup[0:1, pl.ds((d // 2) * 128, 128)] = bu + t[4:5]
            bqkv[0:6, :] = bq
        def load_q():
            for e in range(3): load(("q", e), wq_f.at[e], wqu.at[:, pl.ds(e * 256, 256)])
        def have_u():
            gu.arrived(); local[3].wait(); load("u", wup_f, wqu)
        def norm(lo, hi):
            gain, bias = rowsv[0:1, :], rowsv[1:2, :]
            def go_(i, carry):
                r = pl.ds(pl.multiple_of(lo + i * 128, 128), 128)
                a = nrm[r, :].astype(f32)
                cen = a - jnp.mean(a, axis=-1, keepdims=True)
                inv = lax.rsqrt(jnp.mean(cen * cen, axis=-1, keepdims=True) + norm_epsilon)
                nrm[r, :] = (cen * inv * gain + bias).astype(bf16)
                return carry
            lax.fori_loop(0, (hi - lo) // 128, go_, 0)
        def project(lo):
            r = pl.ds(lo, 256)
            n = nrm[r, :]
            for j, dst in enumerate((q, k, val)):
                p = NN(n, wqu[:, j * 256:(j + 1) * 256])
                for h in range(2):
                    u = p[:, h * 128:(h + 1) * 128] + bqkv[2 * j + h:2 * j + h + 1, :]
                    dst[h, r, :] = (u if j == 2 else turn(u, tab, r, 1)).astype(bf16)
        def grad_attended():
            def go_(i, carry):
                r = pl.ds(pl.multiple_of(i * 512, 512), 512)
                p = NT(cot[r, :], wb[0:256, :])
                ga[0, r, :] = p[:, 0:128].astype(bf16); ga[1, r, :] = p[:, 128:256].astype(bf16)
                return carry
            lax.fori_loop(0, 2, go_, 0)
        def probabilities(i, p, hh):
            n = (i + 1) * 256
            r = pl.ds(i * 256, 256)
            m = ((lax.broadcasted_iota(jnp.int32, (1, 128), 1) // 64) == hh).astype(bf16)
            kk = k[p, 0:n] * m; w = val[p, 0:n] * m; qq = q[p, r] * (m * 0.125)
            s = NT(kk, qq)
            key = lax.broadcasted_iota(jnp.int32, (256, 256), 0); row = lax.broadcasted_iota(jnp.int32, (256, 256), 1)
            diag = jnp.where(row >= key, s[n - 256:], -1e30)
            s = diag if i == 0 else jnp.concatenate([s[:n - 256], diag], 0)
            e = jnp.exp(s - jnp.max(s, 0, keepdims=True))
            return m, kk, w, qq, e * (1.0 / jnp.sum(e, 0, keepdims=True))
        def attend(i):
            def go_(p, carry):
                a_ = 0.0
                for hh in range(2):
                    m, kk, w, qq, pr = probabilities(i, p, hh)
                    a_ = a_ + TN(pr.astype(bf16), w)
                aa[pl.ds(i * 256, 256), pl.ds(pl.multiple_of(p * 128, 128), 128)] = a_.astype(bf16)
                return carry
            lax.fori_loop(0, 2, go_, 0)
        def attend_back(i):
            def go_(p, carry):
                n = (i + 1) * 256
                r = pl.ds(i * 256, 256)
                d_, tk, tv = 0.0, 0.0, 0.0
                for hh in range(2):
                    m, kk, w, qq, pr = probabilities(i, p, hh)
                    gg = ga[p, r] * m
                    dp = NT(w, gg)
                    ds = (pr * (dp - jnp.sum(pr * dp, 0, keepdims=True))).astype(bf16)
                    d_ = d_ + TN(ds, kk); tk = tk + NN(ds, qq); tv = tv + NN(pr.astype(bf16), gg)
                pq[r, pl.ds(pl.multiple_of(p * 128, 128), 128)] = turn(d_ * 0.125, tab, r, -1).astype(bf16)
                if i == 3: dk[p] = tk; dv[p] = tv
                else:
                    dk[p, 0:n] += tk; dv[p, 0:n] += tv
                return carry
            lax.fori_loop(0, 2, go_, 0)
        def keys_done():
            def go_(i, carry):
                r = pl.ds(pl.multiple_of(i * 256, 256), 256)
                for p in range(2):
                    pq[r, 256 + p * 128:384 + p * 128] = turn(dk[p, r], tab, r, -1).astype(bf16)
                    pq[r, 512 + p * 128:640 + p * 128] = dv[p, r].astype(bf16)
                return carry
            lax.fori_loop(0, 4, go_, 0)
        def hidden(lo):
            r = pl.ds(lo, 256)
            n = nrm[r, :]
            for j in range(4):
                cols = pl.ds(j * 256, 256)
                h = NN(n, wqu[:, cols]) + bup[0:1, cols]
                h2 = h * h
                t = 0.5 + 0.5 * jnp.tanh(h * (0.7978845608028654 + 0.035677408136300125 * h2))
                y_ = h * t
                aa[r, pl.ds(256 + j * 256, 256)] = y_.astype(bf16)
                pq[r, pl.ds(768 + j * 256, 256)] = (t + y_ * ((2.0 - 2.0 * t) * (0.7978845608028654 + 0.10703222440890037 * h2))).astype(bf16)
        steps.update({"first": first, "vectors": vectors, "Lq": load_q, "Au": have_u, "Wq": lambda: wait(("q", 0), ("q", 1), ("q", 2), "tab"),
                      "Wu": lambda: wait("u"), "ga": grad_attended, "k": keys_done})
        for i in range(4):
            steps["N%d" % i] = partial(norm, i * 256, i * 256 + 256); steps["p%d" % i] = partial(project, i * 256)
            steps["H%d" % i] = partial(hidden, i * 256); steps["f%d" % i] = partial(attend, i); steps["a%d" % i] = partial(attend_back, i)
        for name in PLAN: steps[name]()
    vm = lambda sh, t=bf16: pltpu.VMEM(sh, t)
    pl.run_scoped(forward_part, vm((2, 1024, 128), f32), vm((512, 128)), vm((2048, 1024)), vm((8, 128), f32), vm((8, 1024), f32),
                  *[vm((2, 1024, 128)) for _ in range(4)], vm((2, 1024, 128), f32), vm((2, 1024, 128), f32))

    def backward_part(gnp, g, wch, o2, oup, oq):
        gs = TensorSum(gnp, fb, t1b, t2b, zsb, zrb, ss.at[1], rs.at[1])
        s2 = Scatter(g, sib2, m2, ss.at[4], rs.at[4], 1280)
        su = Scatter(g, sibu, mu, ss.at[5], rs.at[5], 1024)
        sq = Scatter(g, sibq, mq, ss.at[6], rs.at[6], 768)
        def chunk(j):
            s = j % 2; r = pl.ds(j * GC, GC)
            for e in range(3): load(("c", j, e), wq_f.at[e, r], wch.at[s, :, pl.ds(e * 256, 256)])
            load(("c", j, 3), wup_f.at[r], wch.at[s, :, pl.ds(768, 1024)])
        chunk(0); chunk(1)
        def grad_normed(i):
            n = 512 // GC
            for j in range(i * n, i * n + n):
                wait(*[("c", j, e) for e in range(4)])
                p = NT(pq[...], wch[j % 2]).astype(bf16)
                gnp[:, :, j * GC:(j + 1) * GC] = p.reshape(8, 128, GC)
                if j + 2 < 2048 // GC: chunk(j + 2)
        def bias_sums():
            ones = jnp.ones((16, 1024), bf16)
            for d in range(8):
                w = v.at[:, d // 4, d % 4]
                gb = NN(ones, cot[:, d * 256:(d + 1) * 256])[0:1]
                gu_ = NN(ones, gh[:, d * 128:(d + 1) * 128])[0:1]
                for cc in range(2):
                    w[cc, 2:3, :] = gb[:, cc * 128:(cc + 1) * 128]; w[cc, 3:4, :] = gu_
            for j in range(3):
                gqb = NN(ones, gp[:, j * 256:(j + 1) * 256])[0:1]
                for d in range(16):
                    w = v.at[d % 2, d // 8, (d // 2) % 4]
                    w[4 + 2 * j:5 + 2 * j, :] = gqb[:, 0:128]; w[5 + 2 * j:6 + 2 * j, :] = gqb[:, 128:256]
        def ingrad_start():
            gs.arrived()
            sums[...] = jnp.zeros_like(sums)
            cot_own = cot.at[own_rows]
            by_rows(128, 32, lambda r: norm_back_rows(r, gs.total(r), tok, cot_own, rowsv[0:1, :], own.at[1], sums))
            load("ingrad", own.at[1], ingrad.at[t_own])
            ig.start(own.at[1])
        def norm_sums():
            sg = jnp.sum(sums[0], axis=0, keepdims=True); sb = jnp.sum(sums[1], axis=0, keepdims=True)
            for d in range(16):
                w = v.at[d % 2, d // 8, (d // 2) % 4]
                w[0:1, :] = sg[:, d * 128:(d + 1) * 128]; w[1:2, :] = sb[:, d * 128:(d + 1) * 128]
            sm.a()
        def put2(r, t): o2[r, :] = t
        def putu(r, t): oup[r, :] = t
        def putq(r, t): oq[r, :] = t
        def done2(): s2.serve4(put2); load("o2", o2, o2_h)
        def doneu(): su.serve4(putu); load("oup", oup, oup_h)
        def doneq(): sq.serve4(putq); load("oq", oq, oq_h)
        def gn_start(): gs.start_far(); gs.start_near(half(0), 0); gs.start_near(half(1), 9); gs.start_near2()
        steps.update({"gS": gn_start, "bias": bias_sums, "iS": ingrad_start, "va": norm_sums, "vb": sm.b, "vc": sm.c_, "vd": sm.d, "ve": sm.e, "vf": sm.f,
                      "s24": done2, "su4": doneu, "sq4": doneq, "gM": gs.middle, "gN": gs.middle2, "gL": gs.last})
        for i in range(4):
            steps["n%d" % i] = partial(grad_normed, i); steps["s2P%d" % i] = partial(s2.produce, cot, aa, i, i + 1)
        for i in range(2):
            steps["suP%d" % i] = partial(su.produce, nrm, gh, 2 * i, 2 * i + 2); steps["sqP%d" % i] = partial(sq.produce, nrm, gp, 2 * i, 2 * i + 2)
            for nm, w in (("s2", s2), ("su", su), ("sq", sq)): steps[nm + "p%d" % i] = partial(w.pairs, 4 * i, 4 * i + 4)
        for nm, w in (("s2", s2), ("su", su), ("sq", sq)): steps[nm + "1"], steps[nm + "2"], steps[nm + "3"] = w.serve1, w.serve2, w.serve3
        for name in PLAN_B: steps[name]()
        wait("mixed", "ingrad", "o2", "oup", "oq")
        for w in (gs, bs, mg, ig, s2, su, sq, sm): w.drain()
    pl.run_scoped(backward_part, vm((8, 128, 2048)), vm((8, 2, 128, 1280)), vm((2, GC, 1792)), vm((128, 1280), f32), vm((128, 1024), f32), vm((128, 768), f32))
    for w in every: w.drain()

def layer(vectors, wq, wout, wup, wdown, tokens, cot, tab):
    S = jax.ShapeDtypeStruct
    vm = lambda sh, t=bf16: pltpu.VMEM(sh, t)
    tsum = [vm((128, 2048)), vm((128, 2048)), vm((2, 2, 128, 2048)), vm((128, 2048)), vm((128, 2048))]
    A = pl.BlockSpec(memory_space=pl.ANY); V = pl.BlockSpec(memory_space=pltpu.VMEM)
    sem = pltpu.SemaphoreType.DMA
    return pl.pallas_call(layer_kernel,
        out_shape=[S((512, 128), bf16), S((3, 2048, 256), bf16), S((256, 2048), bf16), S((2048, 1024), bf16), S((1024, 2048), bf16)]
        + [S((8, 128, 2048), bf16)] * 2 + [S((128, 1280), f32), S((128, 1024), f32), S((128, 768), f32), S((16, 128), f32)],
        in_specs=[V] * 6 + [A] * 7, out_specs=[A] * 10 + [V],
        scratch_shapes=[vm((32, 128)), vm((1280, 2048)), vm((1024, 2048)), vm((1024, 2048)), vm((1024, 1280)), vm((1024, 1792)),
                        vm((8, 2048), f32), vm((128, 2048)), vm((8, 128, 2048)), vm((2, 128, 2048))]
        + tsum + tsum + [vm((8, 128, 1280)), vm((7, 128, 1280)), vm((8, 128, 1024)), vm((7, 128, 1024)), vm((8, 128, 768)), vm((7, 128, 768)),
            vm((2, 2, 4, 16, 128), f32), vm((2, 4, 16, 128), f32), vm((4, 16, 128), f32), vm((3, 16, 128), f32), vm((3, 16, 128), f32), vm((16, 128), f32),
            vm((2, 16, 128), f32), vm((2, 8, 2048), f32),
            sem((5, 16)), sem((5, 16)), sem((5,)), sem((8, 16)), sem((8, 16)), sem((64,))],
        compiler_params=pltpu.CompilerParams(collective_id=1, has_side_effects=True, vmem_limit_bytes=64 << 20),
        name="layer")(*vectors, wq, wout, wup, wdown, tokens, cot, tab)

def hand_over_kernel(mixed, ingrad, o2_h, oup_h, oq_h, osv, mo, io, gg, gb, gq_h, gbq, go_h, gbo, gu_h, gbu, gd_h, gbd,
                     big, o2, oup, oq, gq, go, gd, li, lo):
    dp = lax.axis_index("dp")
    def copy(a, b, sem):
        cp = pltpu.make_async_copy(a, b, sem); cp.start()
        return cp
    n = 8
    ins = [copy((mixed, ingrad)[i // 4].at[pl.ds((i % 4) * 2, 2)], big.at[i], li.at[i]) for i in range(4)]
    small = [copy(o2_h, o2, li.at[n]), copy(oup_h, oup, li.at[n + 1]), copy(oq_h, oq, li.at[n + 2])]
    ins += [copy((mixed, ingrad)[i // 4].at[pl.ds((i % 4) * 2, 2)], big.at[i], li.at[i]) for i in range(4, 8)]
    outs = []
    def pass_on(i):
        ins[i].wait()
        for h in range(2): outs.append(copy(big.at[i, h], (mo, io)[i // 4].at[pl.ds((i % 4) * 256 + h * 128, 128)], lo.at[2 * i + h]))
    pass_on(0); pass_on(1)
    small[0].wait()
    for b in range(10):
        t = o2[:, b * 128:(b + 1) * 128].T
        if b < 2: go[b * 128:(b + 1) * 128, :] = t
        else: gd[(b - 2) * 128:(b - 1) * 128, :] = t
    outs += [copy(go, go_h, lo.at[16]), copy(gd, gd_h, lo.at[17])]
    pass_on(2); pass_on(3)
    small[1].wait(); outs.append(copy(oup, gu_h, lo.at[18]))
    small[2].wait()
    for j in range(3): gq[j] = oq[:, j * 256:(j + 1) * 256]
    outs.append(copy(gq, gq_h, lo.at[19]))
    pass_on(4); pass_on(5)
    gg[...] = osv[0:1, :]; gb[...] = osv[1:2, :]; gbo[...] = osv[2:3, :]; gbd[...] = osv[2:3, :]
    l = lax.broadcasted_iota(jnp.int32, (128, 64), 0); k = lax.broadcasted_iota(jnp.int32, (128, 64), 1)
    gbu[...] = lax.dot_general(osv[3:4, :], (l == k + 64 * (dp % 2)).astype(f32), (((1,), (0,)), ((), ())), precision=lax.Precision.HIGHEST)
    l = lax.broadcasted_iota(jnp.int32, (128, 4), 0); k = lax.broadcasted_iota(jnp.int32, (128, 4), 1)
    for j in range(3):
        rows = osv[4 + 2 * j:6 + 2 * j, :]
        lo_, hi_ = (lax.dot_general(rows, (l == k + 4 * dp + 64 * h).astype(f32), (((1,), (0,)), ((), ())), precision=lax.Precision.HIGHEST) for h in (0, 1))
        gbq[j] = jnp.concatenate([lo_[0:1], hi_[0:1], lo_[1:2], hi_[1:2]], 0)
    pass_on(6); pass_on(7)
    for cp in outs: cp.wait()

def hand_over(mixed, ingrad, o2, oup, oq, osv):
    S = jax.ShapeDtypeStruct
    A = pl.BlockSpec(memory_space=pltpu.HBM)
    full = lambda sh: pl.BlockSpec(sh, lambda: (0,) * len(sh))
    outs = [((1, 128), 0), ((1, 128), 0), ((3, 128, 256), 1), ((3, 4, 4), 0), ((256, 128), 1), ((1, 128), 0), ((128, 1024), 1), ((1, 64), 0), ((1024, 128), 1), ((1, 128), 0)]
    vm = lambda sh: pltpu.VMEM(sh, f32)
    return pl.pallas_call(hand_over_kernel,
        out_shape=[S((1024, 2048), bf16)] * 2 + [S(sh, f32) for sh, _ in outs],
        in_specs=[A] * 5 + [full((16, 128))], out_specs=[A] * 2 + [A if m else full(sh) for sh, m in outs],
        scratch_shapes=[pltpu.VMEM((8, 2, 128, 2048), bf16), vm((128, 1280)), vm((128, 1024)), vm((128, 768)), vm((3, 128, 256)), vm((256, 128)), vm((1024, 128)),
                        pltpu.SemaphoreType.DMA((12,)), pltpu.SemaphoreType.DMA((20,))],
        compiler_params=pltpu.CompilerParams(vmem_limit_bytes=62 << 20),
        name="hand_over")(mixed, ingrad, o2, oup, oq, osv)

def body(tokens, ln_gain, ln_bias, w_qkv, b_qkv, w_out, b_out, w_up, b_up, w_down, b_down, cotangent):
    row = lambda a: a.reshape(1, 128)
    parts = layer((row(ln_gain), row(ln_bias), row(b_out), row(b_down), b_up, b_qkv), w_qkv.transpose(1, 0, 2), w_out, w_up, w_down,
                  tokens, cotangent, jnp.asarray(rotary_tables()))[5:]
    mixed, ingrad, gg, gb, gq, gbq, go, gbo, gu, gbu, gd, gbd = hand_over(*parts)
    return (mixed, ingrad, gg.reshape(128), gb.reshape(128), gq.transpose(1, 0, 2), gbq, go, gbo.reshape(128), gu, gbu, gd, gbd.reshape(128))


def solution(mesh):
    in_specs = (
        P("dp", None),
        P("dp"),
        P("dp"),
        P("dp", None, "tensor"),
        P(None, "tensor", "dp"),
        P("tensor", "dp"),
        P("dp"),
        P("dp", "tensor"),
        P("tensor", "dp"),
        P("tensor", "dp"),
        P("dp"),
        P("dp", None),
    )
    out_specs = (
        P("dp", None),
        P("dp", None),
        P("dp"),
        P("dp"),
        P("dp", None, "tensor"),
        P(None, "tensor", "dp"),
        P("tensor", "dp"),
        P("dp"),
        P("dp", "tensor"),
        P("tensor", "dp"),
        P("tensor", "dp"),
        P("dp"),
    )
    return jax.shard_map(body, mesh=mesh, in_specs=in_specs, out_specs=out_specs, check_vma=False)
```

```python
from functools import partial

import jax
import jax.numpy as jnp
import numpy as np
from jax import lax
from jax.sharding import PartitionSpec as P
from jax.experimental import pallas as pl
from jax.experimental.pallas import tpu as pltpu

HD = 64
ROT = 32
LEN = 1024
norm_epsilon = 1e-05
rope_base = 10000.0
MESH = pl.DeviceIdType.MESH

def place():
    dp = lax.axis_index("dp"); tn = lax.axis_index("tensor")
    return dp % 2, (dp // 2) % 4, dp // 8, tn % 4, tn // 4

def peer(c, y, zl, x, zh):
    return (zl * 8 + y * 2 + c, zh * 4 + x)

RELS = [(0, 0), (0, 1), (0, 3), (0, 2), (1, 0), (1, 1), (1, 3), (1, 2)]

def enter(devices):
    bar = pltpu.get_barrier_semaphore()
    for d in devices:
        pl.semaphore_signal(bar, inc=1, device_id=d, device_id_type=MESH)
    pl.semaphore_wait(bar, len(devices))

class Gather:
    def __init__(s, shard, full, axis, ss, rs, by_z=False):
        s.by_z = by_z
        s.axis, s.ss, s.rs, s.full = axis, ss, rs, full
        s.c, s.y, s.zl, x, zh = place()
        c, y, zl = s.c, s.y, s.zl
        s.total = shard.shape[1 if axis == 2 else 0]
        s.shard = shard
        s.up = peer(c, (y + 1) % 4, zl, x, zh); s.down = peer(c, (y + 3) % 4, zl, x, zh)
        s.z = peer(c, y, 1 - zl, x, zh); s.sib = peer(1 - c, y, zl, x, zh)
        s.sends = []
    def slot(s, dz, dy, c=None, half=None):
        c = s.c if c is None else c
        d = ((s.zl + dz) % 2) * 8 + ((s.y + dy) % 4) * 2 + c
        n = s.total if half is None else s.total // 2
        lo = 0 if half is None else half * n
        if s.axis == 0: return s.full.at[pl.ds(pl.multiple_of(d * s.total + lo, 16), n)]
        if s.axis == 2: return s.full.at[:, pl.ds(pl.multiple_of(d * s.total + lo, 16), n)]
        return s.full.at[pl.ds(lo, n), pl.ds(pl.multiple_of(d * 128, 128), 128)]
    def send(s, kind, src, dst, dev):
        cp = pltpu.make_async_remote_copy(src, dst, s.ss.at[kind], s.rs.at[kind], device_id=dev, device_id_type=MESH)
        cp.start(); s.sends.append(cp)
    def got(s, kind, dst):
        pltpu.make_async_remote_copy(dst, dst, s.ss.at[kind], s.rs.at[kind], device_id=s.sib, device_id_type=MESH).wait_recv()
    def start(s):
        own = s.slot(0, 0)
        s.send(0, s.shard, own, s.up); s.send(1, s.shard, own, s.down); s.send(2, s.shard, own, s.z)
        s.send(8, s.shard, own, s.sib)
    def relay(s, rel):
        b = s.slot(*RELS[rel]); s.send(8 + rel, b, b, s.sib)
    def serve(s):
        a = s.slot(0, 3); s.got(0, a); h = s.slot(0, 3, half=0); s.send(5, h, h, s.up)
        b = s.slot(0, 1); s.got(1, b); h = s.slot(0, 1, half=1); s.send(6, h, h, s.down)
        z = s.slot(1, 0); s.got(2, z)
        if s.by_z:
            s.send(3, a, a, s.z); s.send(4, b, b, s.z)
        else:
            s.send(3, z, z, s.up); s.send(4, z, z, s.down)
        s.relay(2); s.relay(1); s.relay(4)
    def serve2(s):
        s.got(5, s.slot(0, 2, half=0)); s.got(6, s.slot(0, 2, half=1))
        f = s.slot(0, 2); s.send(7, f, f, s.z); s.relay(3)
    def serve3(s):
        s.got(3, s.slot(1, 3)); s.relay(6)
        s.got(4, s.slot(1, 1)); s.relay(5)
        s.got(7, s.slot(1, 2)); s.relay(7)
    def arrived(s):
        for r in range(8): s.got(8 + r, s.slot(*RELS[r], c=1 - s.c))

f32 = jnp.float32
bf16 = jnp.bfloat16

def by_rows(rows, step, fn):
    def go(i, carry):
        fn(pl.ds(pl.multiple_of(i * step, step), step))
        return carry
    lax.fori_loop(0, rows // step, go, 0)

def add_into(dst, terms, rows, step, lo=0):
    def go(r):
        if lo: r = pl.ds(pl.multiple_of(r.start + lo, step), step)
        total = terms[0][r, :].astype(f32)
        for t in terms[1:]: total = total + t[r, :].astype(f32)
        dst[r, :] = total.astype(dst.dtype)
    by_rows(rows, step, go)

class Link:
    def __init__(s, ss, rs):
        s.ss, s.rs, s.sends = ss, rs, []
        c, y, zl, x, zh = s.at = place()
        s.c, s.y, s.zl, s.x, s.zh = s.at
        s.sib = peer(1 - c, y, zl, x, zh)
        s.yu, s.yd, s.yf = (peer(c, (y + k) % 4, zl, x, zh) for k in (1, 3, 2))
        s.zn = peer(c, y, 1 - zl, x, zh)
        s.xu, s.xd, s.xf = (peer(c, y, zl, (x + k) % 4, zh) for k in (1, 3, 2))
        s.zf = peer(c, y, zl, x, 1 - zh)
    def send(s, kind, src, dst, dev):
        cp = pltpu.make_async_remote_copy(src, dst, s.ss.at[kind], s.rs.at[kind], device_id=dev, device_id_type=MESH)
        cp.start(); s.sends.append(cp)
    def got(s, kind, dst):
        pltpu.make_async_remote_copy(dst, dst, s.ss.at[kind], s.rs.at[kind], device_id=s.sib, device_id_type=MESH).wait_recv()
    def drain(s):
        for cp in s.sends: cp.wait_send()

class TensorSum(Link):
    def __init__(s, b, f, t1, t2, zs, zr, ss, rs):
        super().__init__(ss, rs)
        s.b, s.f, s.t1, s.t2, s.zs, s.zr = b, f, t1, t2, zs, zr
    def blk(s, zh, dx): return s.b.at[zh * 4 + (s.x + dx) % 4]
    LO, HI = pl.ds(0, 64), pl.ds(64, 64)
    def start_far(s): s.send(0, s.blk(1 - s.zh, 2), s.f, s.zf)
    def start_near(s):
        o = 1 - s.zh
        s.send(1, s.blk(o, 1), s.t2.at[0, o], s.xu); s.send(2, s.blk(o, 3), s.t2.at[1, o], s.xd)
    def start_near2(s):
        s.send(3, s.blk(s.zh, 1).at[s.HI], s.t2.at[0, s.zh, s.HI], s.xu); s.send(4, s.blk(s.zh, 3).at[s.LO], s.t2.at[1, s.zh, s.LO], s.xd)
    def middle(s):
        s.got(0, s.f); add_into(s.f, [s.f, s.blk(s.zh, 2)], 128, 32)
        s.send(5, s.f.at[s.LO], s.t1.at[s.LO], s.xu); s.send(6, s.f.at[s.HI], s.t1.at[s.HI], s.xd)
    def middle2(s):
        s.got(5, s.t1.at[s.LO]); add_into(s.t1, [s.t1, s.blk(s.zh, 1)], 64, 32)
        s.send(7, s.t1.at[s.LO], s.t2.at[0, s.zh, s.LO], s.xu)
        s.got(6, s.t1.at[s.HI]); add_into(s.t1, [s.t1, s.blk(s.zh, 3)], 64, 32, lo=64)
        s.send(8, s.t1.at[s.HI], s.t2.at[1, s.zh, s.HI], s.xd)
    def last(s):
        o = 1 - s.zh
        s.got(1, s.t2.at[0, o]); s.got(2, s.t2.at[1, o])
        add_into(s.zs, [s.blk(o, 0), s.t2.at[0, o], s.t2.at[1, o]], 128, 32)
        s.send(9, s.zs, s.zr, s.zf)
    def total(s, r):
        return (s.blk(s.zh, 0)[r, :].astype(f32) + s.t2.at[0, s.zh][r, :].astype(f32)
                + s.t2.at[1, s.zh][r, :].astype(f32) + s.zr[r, :].astype(f32))
    def arrived(s):
        z = s.zh
        s.got(3, s.t2.at[0, z, s.HI]); s.got(4, s.t2.at[1, z, s.LO]); s.got(7, s.t2.at[0, z, s.LO]); s.got(8, s.t2.at[1, z, s.HI])
        s.got(9, s.zr)

class TensorGather(Link):
    def __init__(s, o, ss, rs):
        super().__init__(ss, rs); s.o = o
    def blk(s, zh, dx): return s.o.at[zh * 4 + (s.x + dx) % 4]
    LO, HI = pl.ds(0, 64), pl.ds(64, 64)
    def start(s, own):
        b = s.blk(s.zh, 0)
        s.send(0, own, b, s.xu); s.send(1, own, b, s.xd); s.send(2, own, b, s.zf)
    def middle(s):
        b = s.blk(s.zh, 3); s.got(0, b); s.send(3, b.at[s.LO], b.at[s.LO], s.xu)
        b = s.blk(s.zh, 1); s.got(1, b); s.send(4, b.at[s.HI], b.at[s.HI], s.xd)
    def plane(s):
        b = s.blk(1 - s.zh, 0); s.got(2, b); s.send(5, b, b, s.xu); s.send(6, b, b, s.xd)
    def far(s):
        b = s.blk(s.zh, 2); s.got(3, b.at[s.LO]); s.got(4, b.at[s.HI]); s.send(7, b, b, s.zf)
    def finish(s):
        o = 1 - s.zh
        s.got(5, s.blk(o, 3)); s.got(6, s.blk(o, 1)); s.got(7, s.blk(o, 2))

class SmallSum(Link):
    def __init__(s, v, rc, rz, ry, rx, rt, acc, out, ss, rs):
        super().__init__(ss, rs)
        s.v, s.rc, s.rz, s.ry, s.rx, s.rt, s.acc, s.out = v, rc, rz, ry, rx, rt, acc, out
    def a(s): s.send(0, s.v.at[1 - s.c], s.rc, s.sib)
    def b(s):
        s.got(0, s.rc); s.rc[...] = s.rc[...] + s.v[s.c]
        s.send(1, s.rc.at[1 - s.zl], s.rz, s.zn)
    def c_(s):
        s.got(1, s.rz); s.rz[...] = s.rz[...] + s.rc[s.zl]
        s.send(2, s.rz.at[(s.y + 1) % 4], s.ry.at[0], s.yu); s.send(3, s.rz.at[(s.y + 3) % 4], s.ry.at[1], s.yd)
        s.send(4, s.rz.at[(s.y + 2) % 4], s.ry.at[2], s.yf)
    def d(s):
        for k in range(3): s.got(2 + k, s.ry.at[k])
        s.acc[0] = s.rz[s.y] + s.ry[0] + s.ry[1] + s.ry[2]
        s.send(5, s.acc.at[0], s.rx.at[0], s.xu); s.send(6, s.acc.at[0], s.rx.at[1], s.xd); s.send(7, s.acc.at[0], s.rx.at[2], s.xf)
    def e(s):
        for k in range(3): s.got(5 + k, s.rx.at[k])
        s.acc[1] = s.acc[0] + s.rx[0] + s.rx[1] + s.rx[2]
        s.send(8, s.acc.at[1], s.rt, s.zf)
    def f(s):
        s.got(8, s.rt)
        first = lax.broadcasted_iota(jnp.int32, (16, 128), 0) < 2
        s.out[...] = jnp.where(first, s.acc[1] + s.rt[...], s.acc[0])

def peers_all():
    c, y, zl, x, zh = place()
    return ([peer(1 - c, y, zl, x, zh), peer(c, y, 1 - zl, x, zh), peer(c, y, zl, x, 1 - zh)]
            + [peer(c, (y + k) % 4, zl, x, zh) for k in (1, 2, 3)] + [peer(c, y, zl, (x + k) % 4, zh) for k in (1, 2, 3)])

def norm_back_rows(r, gn, tokens, cot, gain, out, sums):
    x = tokens[r, :].astype(f32)
    mean = jnp.mean(x, axis=-1, keepdims=True); cen = x - mean
    inv = lax.rsqrt(jnp.mean(cen * cen, axis=-1, keepdims=True) + 1e-5)
    xh = cen * inv
    n = x.shape[0] // 8
    sums[0] += jnp.sum((gn * xh).reshape(n, 8, 2048), axis=0)
    sums[1] += jnp.sum(gn.reshape(n, 8, 2048), axis=0)
    sc = gn * gain
    ig = cot[r, :].astype(f32) + inv * (sc - jnp.mean(sc, axis=-1, keepdims=True) - xh * jnp.mean(sc * xh, axis=-1, keepdims=True))
    out[r, :] = ig.astype(bf16)

PLAN = ("o0", "v0", "q0", "v1", "o1", "q1", "o2", "v2", "q2", "v3", "o3", "u0", "first", "vectors", "n0", "Ao", "q3", "d0", "n1", "n2",
        "n3", "Wo", "Aq", "u1", "ga", "Wq", "p0", "p3", "p1", "p2", "d1", "u2", "a3x", "a0x", "a3y", "sn", "a1x", "u3", "a0y", "d2",
        "a2x", "a2y", "Au", "a1y", "k", "Wu", "h1", "d3", "sa", "sg", "h2", "h0", "h3")

def NT(a, b): return lax.dot_general(a, b, (((1,), (1,)), ((), ())), preferred_element_type=f32)
def NN(a, b): return lax.dot_general(a, b, (((1,), (0,)), ((), ())), preferred_element_type=f32)
def TN(a, b): return lax.dot_general(a, b, (((0,), (0,)), ((), ())), preferred_element_type=f32)

def rotary_tables():
    pos = np.arange(LEN, dtype=np.float32)
    freq = (np.float32(rope_base) ** (-np.arange(0, ROT, 2, dtype=np.float32) / np.float32(ROT))).astype(np.float32)
    ang = (pos[:, None] * freq[None, :]).astype(np.float32)
    cos, sin = np.cos(ang).astype(np.float32), np.sin(ang).astype(np.float32)
    one, zero = np.ones((LEN, 32), np.float32), np.zeros((LEN, 16), np.float32)
    c = np.concatenate([cos, cos, one], 1)
    s1 = np.concatenate([-sin, zero, zero, zero], 1)
    s2 = np.concatenate([zero, sin, zero, zero], 1)
    return np.stack([np.concatenate([t, t], 1) for t in (c, s1, s2)])

def turn(u, tab, r, sign):
    other = pltpu.roll(u, 112, 1) * tab[1, r, :] + pltpu.roll(u, 16, 1) * tab[2, r, :]
    straight = u * tab[0, r, :]
    return straight + other if sign > 0 else straight - other


def pack(vec, gain, lbias, bout, bdown, bup, bqkv):
    dp = lax.axis_index("dp")
    k = lax.broadcasted_iota(jnp.int32, (64, 128), 0); l = lax.broadcasted_iota(jnp.int32, (64, 128), 1)
    up = NN(bup[...], ((l % 64 == k) & (l // 64 == dp % 2)).astype(bf16))
    k4 = k[0:4]; l4 = l[0:4]
    on = (l4 % 4 == k4) & ((l4 % 64) // 4 == dp)
    rows = [gain[...].astype(f32), lbias[...].astype(f32), bout[...].astype(f32), bdown[...].astype(f32), up]
    for j in range(3):
        lo = NN(bqkv[j], (on & (l4 < 64)).astype(bf16)); hi = NN(bqkv[j], (on & (l4 >= 64)).astype(bf16))
        rows += [lo[0:1] + hi[1:2], lo[2:3] + hi[3:4]]
    vec[...] = jnp.concatenate(rows + [jnp.zeros((21, 128), f32)], 0).astype(bf16)

def forward_kernel(gain_s, lbias_s, bout_s, bdown_s, bup_s, bqkv_s, wq, wout, wup, wdown, tok_h, cot_h, tab_h,
                   vecs, wq_f, wout_f, wup_f, wdown_f, rows_h, nrm_h, att_h, act_h, dact_h, gp_h,
                   vec, tab, vv, wqv, woutv, wupv, tok, cot, nrm, rowsv, bqkv, bup, q, k, v, ga, att, dk, dv, gp, act, dact,
                   ss, rs, ls, ld):
    c, y, zl, x, zh = place()
    loads = {}
    def load(i, src, dst):
        loads[i] = pltpu.make_async_copy(src, dst, ld.at[i]); loads[i].start()
    load(0, tok_h, tok); load(1, cot_h, cot); load(12, tab_h, tab)
    pack(vec, gain_s, lbias_s, bout_s, bdown_s, bup_s, bqkv_s)
    enter([peer(c, (y + 1) % 4, zl, x, zh), peer(c, (y + 3) % 4, zl, x, zh), peer(c, y, 1 - zl, x, zh), peer(1 - c, y, zl, x, zh)])
    gv, gq, go, gu, gd = every = [Gather(a, b, ax, ss.at[i], rs.at[i], i == 2) for i, (a, b, ax) in enumerate(
        [(vec, vecs, 0), (wq, wq_f, 2), (wout, wout_f, 1), (wup, wup_f, 0), (wdown, wdown_f, 1)])]
    local = [pltpu.make_async_copy(g.shard, g.slot(0, 0), ls.at[i]) for i, g in enumerate(every)]
    for cp in local: cp.start()

    def norm(lo, hi):
        gain, bias = rowsv[0:1, :], rowsv[1:2, :]
        def go_(i, carry):
            r = pl.ds(pl.multiple_of(lo + i * 128, 128), 128)
            a = tok[r, :].astype(f32)
            cen = a - jnp.mean(a, axis=-1, keepdims=True)
            inv = lax.rsqrt(jnp.mean(cen * cen, axis=-1, keepdims=True) + norm_epsilon)
            nrm[r, :] = (cen * inv * gain + bias).astype(bf16)
            return carry
        lax.fori_loop(0, (hi - lo) // 128, go_, 0)

    def project(lo, hi):
        def go_(i, carry):
            r = pl.ds(pl.multiple_of(lo + i * 256, 256), 256)
            n = nrm[r, :]
            for j, dst in enumerate((q, k, v)):
                p = NN(n, wqv[j])
                for h in range(2):
                    u = p[:, h * 128:(h + 1) * 128] + bqkv[2 * j + h:2 * j + h + 1, :]
                    dst[h, r, :] = (u if j == 2 else turn(u, tab, r, 1)).astype(bf16)
            return carry
        lax.fori_loop(0, (hi - lo) // 256, go_, 0)

    def grad_attended():
        def go_(i, carry):
            r = pl.ds(pl.multiple_of(i * 512, 512), 512)
            p = NT(cot[r, :], woutv[...])
            ga[0, r, :] = p[:, 0:128].astype(bf16); ga[1, r, :] = p[:, 128:256].astype(bf16)
            return carry
        lax.fori_loop(0, 2, go_, 0)

    def attention(i):
        lax.fori_loop(0, 2, lambda p, carry: attention_pair(i, p, carry), 0)
    def attention_pair(i, p, carry=0):
            n = (i + 1) * 256
            r = pl.ds(i * 256, 256)
            cols = pl.ds(pl.multiple_of(p * 128, 128), 128)
            a_, d_, tk, tv = 0.0, 0.0, 0.0, 0.0
            for hh in range(2):
                m = ((lax.broadcasted_iota(jnp.int32, (1, 128), 1) // 64) == hh).astype(bf16)
                kk = k[p, 0:n] * m; w = v[p, 0:n] * m; qq = q[p, r] * (m * 0.125); gg = ga[p, r] * m
                s = NT(kk, qq)
                key = lax.broadcasted_iota(jnp.int32, (256, 256), 0); row = lax.broadcasted_iota(jnp.int32, (256, 256), 1)
                diag = jnp.where(row >= key, s[n - 256:], -1e30)
                s = diag if i == 0 else jnp.concatenate([s[:n - 256], diag], 0)
                e = jnp.exp(s - jnp.max(s, 0, keepdims=True))
                pr = e * (1.0 / jnp.sum(e, 0, keepdims=True))
                low = pr.astype(bf16)
                dp = NT(w, gg)
                ds = (pr * (dp - jnp.sum(pr * dp, 0, keepdims=True))).astype(bf16)
                a_ = a_ + TN(low, w); d_ = d_ + TN(ds, kk)
                tk = tk + NN(ds, qq); tv = tv + NN(low, gg)
            att[r, cols] = a_.astype(bf16)
            gp[r, cols] = turn(d_ * 0.125, tab, r, -1).astype(bf16)
            if i == 3: dk[p] = tk; dv[p] = tv
            else:
                dk[p, 0:n] += tk; dv[p, 0:n] += tv
            return carry

    def keys_done():
        def go_(i, carry):
            r = pl.ds(pl.multiple_of(i * 256, 256), 256)
            for p in range(2):
                gp[r, 256 + p * 128:384 + p * 128] = turn(dk[p, r], tab, r, -1).astype(bf16)
                gp[r, 512 + p * 128:640 + p * 128] = dv[p, r].astype(bf16)
            return carry
        lax.fori_loop(0, 4, go_, 0)

    def hidden(lo, hi):
        def go_(i, carry):
            r = pl.ds(pl.multiple_of(lo + i * 256, 256), 256)
            n = nrm[r, :]
            for j in range(4):
                cols = pl.ds(j * 256, 256)
                h = NN(n, wupv[:, cols]) + bup[0:1, cols]
                h2 = h * h
                t = 0.5 + 0.5 * jnp.tanh(h * (0.7978845608028654 + 0.035677408136300125 * h2))
                y_ = h * t
                act[r, cols] = y_.astype(bf16)
                dact[r, cols] = (t + y_ * ((2.0 - 2.0 * t) * (0.7978845608028654 + 0.10703222440890037 * h2))).astype(bf16)
            return carry
        lax.fori_loop(0, (hi - lo) // 256, go_, 0)
        r = pl.ds(lo, hi - lo)
        load(13 + lo // 256, act.at[r], act_h.at[r]); load(17 + lo // 256, dact.at[r], dact_h.at[r])

    def first():
        gv.arrived(); local[0].wait(); load(2, vecs, vv)
    def vectors():
        loads[2].wait(); loads[0].wait()
        bq, bu = jnp.zeros((6, 128), f32), None
        for d in range(16):
            t = vv[pl.ds(d * 32, 32), :].astype(f32)
            cols = pl.ds(d * 128, 128)
            rowsv[0:1, cols] = t[0:1]; rowsv[1:2, cols] = t[1:2]; rowsv[2:3, cols] = t[2:3] + t[3:4]
            bq = bq + t[5:11]
            if d % 2 == 0: bu = t[4:5]
            else: bup[0:1, pl.ds((d // 2) * 128, 128)] = bu + t[4:5]
        bqkv[0:6, :] = bq
        load(6, rowsv, rows_h)
    def have_q():
        gq.arrived(); local[1].wait(); load(3, wq_f, wqv)
    def have_o():
        go.arrived(); local[2].wait(); load(4, wout_f, woutv)
    def have_u():
        gu.arrived(); local[3].wait(); load(7, wup_f, wupv)
    steps = {"first": first, "vectors": vectors, "Aq": have_q, "Ao": have_o, "Au": have_u,
             "Wq": lambda: (loads[3].wait(), loads[12].wait()), "Wo": lambda: (loads[4].wait(), loads[1].wait()), "Wu": lambda: loads[7].wait(),
             "ga": grad_attended, "k": keys_done, "sn": lambda: load(5, nrm, nrm_h), "sa": lambda: load(8, att, att_h), "sg": lambda: load(9, gp, gp_h)}
    for i in range(4):
        steps["n%d" % i] = partial(norm, i * 256, i * 256 + 256)
        steps["p%d" % i] = partial(project, i * 256, i * 256 + 256)
        steps["h%d" % i] = partial(hidden, i * 256, i * 256 + 256)
        steps["a%d" % i] = partial(attention, i)
        for p in range(2): steps["a%d%s" % (i, "xy"[p])] = partial(attention_pair, i, p)
    for nm, g in (("v", gv), ("q", gq), ("o", go), ("u", gu), ("d", gd)):
        steps[nm + "0"], steps[nm + "1"], steps[nm + "2"], steps[nm + "3"] = g.start, g.serve, g.serve2, g.serve3
    for name in PLAN: steps[name]()
    gd.arrived()
    for i in (5, 6, 8, 9, *range(13, 21)): loads[i].wait()
    local[4].wait()
    for g in (gv, gq, go, gu, gd):
        for cp in g.sends: cp.wait_send()

def forward(vectors, wq, wout, wup, wdown, tokens, cot, tab):
    A = pl.BlockSpec(memory_space=pl.ANY); V = pl.BlockSpec(memory_space=pltpu.VMEM)
    S = jax.ShapeDtypeStruct
    vm = lambda sh, t=bf16: pltpu.VMEM(sh, t)
    return pl.pallas_call(forward_kernel,
        out_shape=[S((512, 128), bf16), S((3, 2048, 256), bf16), S((256, 2048), bf16), S((2048, 1024), bf16), S((1024, 2048), bf16),
                   S((8, 2048), f32), S((1024, 2048), bf16), S((1024, 256), bf16), S((1024, 1024), bf16), S((1024, 1024), bf16), S((1024, 768), bf16)],
        in_specs=[V] * 10 + [A] * 3, out_specs=[A] * 11,
        scratch_shapes=[vm((32, 128)), vm((3, 1024, 128), f32), vm((512, 128)), vm((3, 2048, 256)), vm((256, 2048)), vm((2048, 1024)), vm((1024, 2048)), vm((1024, 2048)), vm((1024, 2048)),
                        vm((8, 2048), f32), vm((8, 128), f32), vm((8, 1024), f32), vm((2, 1024, 128)), vm((2, 1024, 128)), vm((2, 1024, 128)), vm((2, 1024, 128)),
                        vm((1024, 256)), vm((2, 1024, 128), f32), vm((2, 1024, 128), f32), vm((1024, 768)), vm((1024, 1024)), vm((1024, 1024)),
                        pltpu.SemaphoreType.DMA((5, 16)), pltpu.SemaphoreType.DMA((5, 16)), pltpu.SemaphoreType.DMA((5,)), pltpu.SemaphoreType.DMA((21,))],
        compiler_params=pltpu.CompilerParams(collective_id=1, has_side_effects=True, vmem_limit_bytes=60 << 20),
        name="gather_and_forward")(*vectors, wq, wout, wup, wdown, tokens, cot, tab)

PLAN_B = ("L0", "bB", "L1", "bA", "bD", "bC", "h0", "h1", "n0", "n1", "bM", "n2", "n3", "gS", "s2P0", "s2P1", "bL", "s2P2", "s2p0", "s2P3",
          "gM", "bN", "s2p1", "s21", "gL", "suP0", "gN", "s22", "mS", "suP1", "bias", "iS", "sup0", "sup1", "su1", "sqP0", "s23", "va", "vb", "mM",
          "sqP1", "vc", "su2", "sqp0", "iM", "sqp1", "mP", "vd", "mF", "sq1", "sq2", "su3", "iP", "s24", "iF", "ve", "mE", "sq3", "su4", "vf",
          "sq4", "iE")

class Scatter(Link):
    def __init__(s, g, sib, mid, ss, rs, width):
        super().__init__(ss, rs)
        s.g, s.b, s.m, s.w = g, sib, mid, width
    def to_sibling(s, k):
        return pltpu.make_async_remote_copy(s.g.at[k, 1 - s.c, :, pl.ds(0, s.w)], s.b.at[k], s.ss.at[k], s.rs.at[k],
                                            device_id=s.sib, device_id_type=MESH)
    def produce(s, lhs, rhs, lo, hi):
        n = rhs.shape[1]
        def go(j, carry):
            y = (s.y + 2 + 3 * j) % 4
            a = jnp.concatenate([lhs[:, pl.ds(pl.multiple_of((p * 4 + y) * 256, 256), 256)] for p in range(2)], 1)
            for at in range(0, n, 256):
                r = TN(a, rhs[:, at:at + 256]).astype(bf16)
                for p in range(2):
                    for cc in range(2): s.g[2 * j + p, cc, :, at:at + 256] = r[p * 256 + cc * 128:p * 256 + cc * 128 + 128]
            for p in range(2):
                s.to_sibling(2 * j + p).start()
            return carry
        lax.fori_loop(lo, hi, go, 0)
    def pairs(s, lo, hi):
        def go(k, carry):
            s.to_sibling(k).wait()
            mine = s.g.at[k, s.c]; dst = s.b.at[k]
            def rows(i, cc):
                r = pl.ds(pl.multiple_of(i * 32, 32), 32)
                dst[r, :] = (dst[r, :].astype(f32) + mine[r, 0:s.w].astype(f32)).astype(bf16)
                return cc
            lax.fori_loop(0, 4, rows, 0)
            return carry
        lax.fori_loop(lo, hi, go, 0)
    def serve1(s):
        s.send(8, s.b.at[0], s.m.at[0], s.yu); s.send(9, s.b.at[1], s.m.at[1], s.yd)
        s.send(10, s.b.at[3], s.m.at[4], s.yu); s.send(11, s.b.at[6], s.m.at[2], s.yd)
    def serve2(s):
        s.got(8, s.m.at[0]); add_into(s.b.at[2], [s.b.at[2], s.m.at[0]], 128, 32); s.send(12, s.b.at[2], s.m.at[3], s.yu)
        s.got(9, s.m.at[1]); add_into(s.b.at[7], [s.b.at[7], s.m.at[1]], 128, 32); s.send(13, s.b.at[7], s.m.at[5], s.yd)
    def serve3(s):
        for k, j in ((10, 4), (11, 2), (12, 3), (13, 5)): s.got(k, s.m.at[j])
        o = 1 - s.zl; b = s.b.at[4 + o]
        add_into(b, [b, s.m.at[2 + 2 * o], s.m.at[3 + 2 * o]], 128, 32); s.send(14, b, s.m.at[6], s.zn)
    def serve4(s, put):
        s.got(14, s.m.at[6])
        z = s.zl
        terms = (s.b.at[4 + z], s.m.at[2 + 2 * z], s.m.at[3 + 2 * z], s.m.at[6])
        def go(r):
            t = terms[0][r, :].astype(f32)
            for q in terms[1:]: t = t + q[r, :].astype(f32)
            put(r, t)
        by_rows(128, 32, go)

def backward_kernel(wq_f, wout_f, wup_f, wdown_f, rows_h, nrm_h, att_h, act_h, dact_h, gp_h, cot_h, tok_h,
                    mixed, ingrad, o2, oup, oq, osv,
                    wb, wch, cot, nrm, aa, pq, rowsv, tok, brp, gnp, own,
                    fa, t1a, t2a, zsa, zra, fb, t1b, t2b, zsb, zrb, g, sib2, m2, sibu, mu, sibq, mq,
                    v, rc, rz, ry, rx, rt, acc, sums, ss, rs, ld):
    c, y, zl, x, zh = place()
    t_own = zh * 4 + x
    o = 1 - zh
    loads = {}
    def load(i, src, dst):
        loads[i] = pltpu.make_async_copy(src, dst, ld.at[i]); loads[i].start()
    def wait(*ids):
        for i in ids: loads[i].wait()
    load(0, att_h, aa.at[:, pl.ds(0, 256)]); load(1, act_h, aa.at[:, pl.ds(256, 1024)])
    for j in range(4):
        cols = pl.ds(j * 512, 512)
        load(20 + j, wout_f.at[:, cols], wb.at[pl.ds(0, 256), cols]); load(24 + j, wdown_f.at[:, cols], wb.at[pl.ds(256, 1024), cols])
    enter(peers_all())
    bs = TensorSum(brp, fa, t1a, t2a, zsa, zra, ss.at[0], rs.at[0])
    gs = TensorSum(gnp, fb, t1b, t2b, zsb, zrb, ss.at[1], rs.at[1])
    mg = TensorGather(mixed, ss.at[2], rs.at[2])
    ig = TensorGather(ingrad, ss.at[3], rs.at[3])
    s2 = Scatter(g, sib2, m2, ss.at[4], rs.at[4], 1280)
    su = Scatter(g, sibu, mu, ss.at[5], rs.at[5], 1024)
    sq = Scatter(g, sibq, mq, ss.at[6], rs.at[6], 768)
    sm = SmallSum(v, rc, rz, ry, rx, rt, acc, osv, ss.at[7], rs.at[7])
    gp, gh = pq.at[:, pl.ds(0, 768)], pq.at[:, pl.ds(768, 1024)]

    def chunk(j):
        s = j % 2; r = pl.ds(j * 512, 512)
        for e in range(3): load(10 + 4 * s + e, wq_f.at[e, r], wch.at[s, :, pl.ds(e * 256, 256)])
        load(13 + 4 * s, wup_f.at[r], wch.at[s, :, pl.ds(768, 1024)])
    def first_loads(): wait(0, 1)
    def other_loads():
        load(4, cot_h, cot); load(5, dact_h, gh); load(6, gp_h, gp); chunk(0); chunk(1); load(7, nrm_h, nrm)
        load(8, rows_h, rowsv); load(9, tok_h.at[pl.ds(pl.multiple_of(t_own * 128, 128), 128)], tok)
    def branch(a, b, first=False):
        ra, rb = (pl.ds(pl.multiple_of(t * 128, 128), 128) for t in (a, b))
        lhs = jnp.concatenate([aa[ra, :], aa[rb, :]], 0)
        for j in range(4):
            if first: wait(20 + j, 24 + j)
            cols = pl.ds(j * 512, 512)
            p = NN(lhs, wb[:, cols]).astype(bf16)
            brp[a, :, cols] = p[0:128]; brp[b, :, cols] = p[128:256]
    def grad_hidden(lo, hi):
        if lo == 0: wait(4, 5)
        def go(i, carry):
            r = pl.ds(pl.multiple_of(i * 512, 512), 512)
            gr = cot[r, :]
            for j in range(4):
                p = NT(gr, wb[256 + j * 256:512 + j * 256, :])
                cols = pl.ds(768 + j * 256, 256)
                pq[r, cols] = (p * pq[r, cols].astype(f32)).astype(bf16)
            return carry
        lax.fori_loop(lo, hi, go, 0)
    def grad_normed(j):
        s = j % 2
        if j == 0: wait(6)
        wait(*range(10 + 4 * s, 14 + 4 * s))
        p = NT(pq[...], wch[s]).astype(bf16)
        gnp[:, :, j * 512:(j + 1) * 512] = p.reshape(8, 128, 512)
        if j + 2 < 4: chunk(j + 2)
    def bias_sums():
        ones = jnp.ones((16, 1024), bf16)
        for d in range(8):
            w = v.at[:, d // 4, d % 4]
            gb = NN(ones, cot[:, d * 256:(d + 1) * 256])[0:1]
            gu_ = NN(ones, gh[:, d * 128:(d + 1) * 128])[0:1]
            for cc in range(2):
                w[cc, 2:3, :] = gb[:, cc * 128:(cc + 1) * 128]; w[cc, 3:4, :] = gu_
        for j in range(3):
            gqb = NN(ones, gp[:, j * 256:(j + 1) * 256])[0:1]
            for d in range(16):
                w = v.at[d % 2, d // 8, (d // 2) % 4]
                w[4 + 2 * j:5 + 2 * j, :] = gqb[:, 0:128]; w[5 + 2 * j:6 + 2 * j, :] = gqb[:, 128:256]
    def mixed_start():
        bs.arrived()
        def mix(r): own[0, r, :] = (tok[r, :].astype(f32) + bs.total(r) + rowsv[2:3, :]).astype(bf16)
        wait(8, 9)
        by_rows(128, 64, mix)
        load(18, own.at[0], mixed.at[t_own])
        mg.start(own.at[0])
    def ingrad_start():
        gs.arrived()
        sums[...] = jnp.zeros_like(sums)
        cot_own = cot.at[pl.ds(pl.multiple_of(t_own * 128, 128), 128)]
        by_rows(128, 32, lambda r: norm_back_rows(r, gs.total(r), tok, cot_own, rowsv[0:1, :], own.at[1], sums))
        load(19, own.at[1], ingrad.at[t_own])
        ig.start(own.at[1])
    def norm_sums():
        sg = jnp.sum(sums[0], axis=0, keepdims=True); sb = jnp.sum(sums[1], axis=0, keepdims=True)
        for d in range(16):
            w = v.at[d % 2, d // 8, (d // 2) % 4]
            w[0:1, :] = sg[:, d * 128:(d + 1) * 128]; w[1:2, :] = sb[:, d * 128:(d + 1) * 128]
        sm.a()
    def put2(r, t): o2[r, :] = t
    def putu(r, t): oup[r, :] = t
    def putq(r, t): oq[r, :] = t
    def xp(k): return (x + k) % 4
    def far(): branch(o * 4 + xp(2), zh * 4 + xp(2)); bs.start_far()
    def near(): branch(o * 4 + xp(1), o * 4 + xp(3), True); bs.start_near()
    def near2(): branch(zh * 4 + xp(1), zh * 4 + xp(3)); bs.start_near2()
    def home(): branch(o * 4 + xp(0), zh * 4 + xp(0))
    def gn_start(): gs.start_far(); gs.start_near(); gs.start_near2()
    steps = {"L0": first_loads, "L1": other_loads, "bA": far, "bB": near, "bC": near2, "bD": home, "gS": gn_start, "bias": bias_sums,
             "mS": mixed_start, "iS": ingrad_start, "va": norm_sums, "vb": sm.b, "vc": sm.c_, "vd": sm.d, "ve": sm.e, "vf": sm.f,
             "h0": partial(grad_hidden, 0, 1), "h1": partial(grad_hidden, 1, 2),
             "s24": partial(s2.serve4, put2), "su4": partial(su.serve4, putu), "sq4": partial(sq.serve4, putq)}
    for i in range(4):
        steps["n%d" % i] = partial(grad_normed, i); steps["s2P%d" % i] = partial(s2.produce, cot, aa, i, i + 1)
    def up_grads(lo, hi):
        if lo == 0: wait(7)
        su.produce(nrm, gh, lo, hi)
    for i in range(2):
        steps["suP%d" % i] = partial(up_grads, 2 * i, 2 * i + 2); steps["sqP%d" % i] = partial(sq.produce, nrm, gp, 2 * i, 2 * i + 2)
        for nm, w in (("s2", s2), ("su", su), ("sq", sq)): steps[nm + "p%d" % i] = partial(w.pairs, 4 * i, 4 * i + 4)
    for nm, w in (("s2", s2), ("su", su), ("sq", sq)): steps[nm + "1"], steps[nm + "2"], steps[nm + "3"] = w.serve1, w.serve2, w.serve3
    for nm, w in (("b", bs), ("g", gs)): steps[nm + "M"], steps[nm + "N"], steps[nm + "L"] = w.middle, w.middle2, w.last
    for nm, w in (("m", mg), ("i", ig)): steps[nm + "M"], steps[nm + "P"], steps[nm + "F"], steps[nm + "E"] = w.middle, w.plane, w.far, w.finish
    for name in PLAN_B: steps[name]()
    wait(18, 19)
    for w in (gs, bs, mg, ig, s2, su, sq, sm): w.drain()

def backward(wq_f, wout_f, wup_f, wdown_f, rows, nrm, att, act, dact, gp, cot, tok):
    S = jax.ShapeDtypeStruct
    vm = lambda sh, t=bf16: pltpu.VMEM(sh, t)
    tsum = [vm((128, 2048)), vm((128, 2048)), vm((2, 2, 128, 2048)), vm((128, 2048)), vm((128, 2048))]
    A = pl.BlockSpec(memory_space=pl.ANY); V = pl.BlockSpec(memory_space=pltpu.VMEM)
    return pl.pallas_call(backward_kernel,
        out_shape=[S((8, 128, 2048), bf16)] * 2 + [S((128, 1280), f32), S((128, 1024), f32), S((128, 768), f32), S((16, 128), f32)],
        in_specs=[A] * 12, out_specs=[A] * 2 + [V] * 4,
        scratch_shapes=[vm((1280, 2048)), vm((2, 512, 1792)), vm((1024, 2048)), vm((1024, 2048)), vm((1024, 1280)), vm((1024, 1792)),
                        vm((8, 2048), f32), vm((128, 2048)), vm((8, 128, 2048)), vm((8, 128, 2048)), vm((2, 128, 2048))]
        + tsum + tsum + [vm((8, 2, 128, 1280)), vm((8, 128, 1280)), vm((7, 128, 1280)), vm((8, 128, 1024)), vm((7, 128, 1024)), vm((8, 128, 768)), vm((7, 128, 768)),
            vm((2, 2, 4, 16, 128), f32), vm((2, 4, 16, 128), f32), vm((4, 16, 128), f32), vm((3, 16, 128), f32), vm((3, 16, 128), f32), vm((16, 128), f32),
            vm((2, 16, 128), f32), vm((2, 8, 2048), f32),
            pltpu.SemaphoreType.DMA((8, 16)), pltpu.SemaphoreType.DMA((8, 16)), pltpu.SemaphoreType.DMA((28,))],
        compiler_params=pltpu.CompilerParams(collective_id=2, has_side_effects=True, vmem_limit_bytes=64 << 20),
        name="backward_and_sums")(wq_f, wout_f, wup_f, wdown_f, rows, nrm, att, act, dact, gp, cot, tok)

def hand_over_kernel(mixed, ingrad, o2_h, oup_h, oq_h, osv, mo, io, gg, gb, gq_h, gbq, go_h, gbo, gu_h, gbu, gd_h, gbd,
                     big, o2, oup, oq, gq, go, gd, li, lo):
    dp = lax.axis_index("dp")
    def copy(a, b, sem, queue=0):
        cp = pltpu.make_async_copy(a, b, sem); cp.start(priority=queue)
        return cp
    n = 8
    ins = [copy((mixed, ingrad)[i // 4].at[pl.ds((i % 4) * 2, 2)], big.at[i], li.at[i], i % 2) for i in range(4)]
    small = [copy(o2_h, o2, li.at[n]), copy(oup_h, oup, li.at[n + 1]), copy(oq_h, oq, li.at[n + 2])]
    ins += [copy((mixed, ingrad)[i // 4].at[pl.ds((i % 4) * 2, 2)], big.at[i], li.at[i], i % 2) for i in range(4, 8)]
    outs = []
    def pass_on(i):
        ins[i].wait()
        for h in range(2): outs.append(copy(big.at[i, h], (mo, io)[i // 4].at[pl.ds((i % 4) * 256 + h * 128, 128)], lo.at[2 * i + h], (i + 1) % 2))
    pass_on(0); pass_on(1)
    small[0].wait()
    for b in range(10):
        t = o2[:, b * 128:(b + 1) * 128].T
        if b < 2: go[b * 128:(b + 1) * 128, :] = t
        else: gd[(b - 2) * 128:(b - 1) * 128, :] = t
    outs += [copy(go, go_h, lo.at[16]), copy(gd, gd_h, lo.at[17])]
    pass_on(2); pass_on(3)
    small[1].wait(); outs.append(copy(oup, gu_h, lo.at[18]))
    small[2].wait()
    for j in range(3): gq[j] = oq[:, j * 256:(j + 1) * 256]
    outs.append(copy(gq, gq_h, lo.at[19]))
    pass_on(4); pass_on(5)
    gg[...] = osv[0:1, :]; gb[...] = osv[1:2, :]; gbo[...] = osv[2:3, :]; gbd[...] = osv[2:3, :]
    l = lax.broadcasted_iota(jnp.int32, (128, 64), 0); k = lax.broadcasted_iota(jnp.int32, (128, 64), 1)
    gbu[...] = lax.dot_general(osv[3:4, :], (l == k + 64 * (dp % 2)).astype(f32), (((1,), (0,)), ((), ())), precision=lax.Precision.HIGHEST)
    l = lax.broadcasted_iota(jnp.int32, (128, 4), 0); k = lax.broadcasted_iota(jnp.int32, (128, 4), 1)
    for j in range(3):
        rows = osv[4 + 2 * j:6 + 2 * j, :]
        lo_, hi_ = (lax.dot_general(rows, (l == k + 4 * dp + 64 * h).astype(f32), (((1,), (0,)), ((), ())), precision=lax.Precision.HIGHEST) for h in (0, 1))
        gbq[j] = jnp.concatenate([lo_[0:1], hi_[0:1], lo_[1:2], hi_[1:2]], 0)
    pass_on(6); pass_on(7)
    for cp in outs: cp.wait()

def hand_over(mixed, ingrad, o2, oup, oq, osv):
    S = jax.ShapeDtypeStruct
    A = pl.BlockSpec(memory_space=pltpu.HBM)
    full = lambda sh: pl.BlockSpec(sh, lambda: (0,) * len(sh))
    outs = [((1, 128), 0), ((1, 128), 0), ((3, 128, 256), 1), ((3, 4, 4), 0), ((256, 128), 1), ((1, 128), 0), ((128, 1024), 1), ((1, 64), 0), ((1024, 128), 1), ((1, 128), 0)]
    vm = lambda sh: pltpu.VMEM(sh, f32)
    return pl.pallas_call(hand_over_kernel,
        out_shape=[S((1024, 2048), bf16)] * 2 + [S(sh, f32) for sh, _ in outs],
        in_specs=[A] * 5 + [full((16, 128))], out_specs=[A] * 2 + [A if m else full(sh) for sh, m in outs],
        scratch_shapes=[pltpu.VMEM((8, 2, 128, 2048), bf16), vm((128, 1280)), vm((128, 1024)), vm((128, 768)), vm((3, 128, 256)), vm((256, 128)), vm((1024, 128)),
                        pltpu.SemaphoreType.DMA((12,)), pltpu.SemaphoreType.DMA((20,))],
        compiler_params=pltpu.CompilerParams(vmem_limit_bytes=62 << 20),
        name="hand_over")(mixed, ingrad, o2, oup, oq, osv)

def body(tokens, ln_gain, ln_bias, w_qkv, b_qkv, w_out, b_out, w_up, b_up, w_down, b_down, cotangent):
    row = lambda a: a.reshape(1, 128)
    vecs, wq_f, wout_f, wup_f, wdown_f, rows, nrm, att, act, dact, gp = forward(
        (row(ln_gain), row(ln_bias), row(b_out), row(b_down), b_up, b_qkv), w_qkv.transpose(1, 0, 2), w_out, w_up, w_down,
        tokens, cotangent, jnp.asarray(rotary_tables()))
    parts = backward(wq_f, wout_f, wup_f, wdown_f, rows, nrm, att, act, dact, gp, cotangent, tokens)
    mixed, ingrad, gg, gb, gq, gbq, go, gbo, gu, gbu, gd, gbd = hand_over(*parts)
    return (mixed, ingrad, gg.reshape(128), gb.reshape(128), gq.transpose(1, 0, 2), gbq, go, gbo.reshape(128), gu, gbu, gd, gbd.reshape(128))


def solution(mesh):
    in_specs = (
        P("dp", None),
        P("dp"),
        P("dp"),
        P("dp", None, "tensor"),
        P(None, "tensor", "dp"),
        P("tensor", "dp"),
        P("dp"),
        P("dp", "tensor"),
        P("tensor", "dp"),
        P("tensor", "dp"),
        P("dp"),
        P("dp", None),
    )
    out_specs = (
        P("dp", None),
        P("dp", None),
        P("dp"),
        P("dp"),
        P("dp", None, "tensor"),
        P(None, "tensor", "dp"),
        P("tensor", "dp"),
        P("dp"),
        P("dp", "tensor"),
        P("tensor", "dp"),
        P("tensor", "dp"),
        P("dp"),
    )
    return jax.shard_map(body, mesh=mesh, in_specs=in_specs, out_specs=out_specs, check_vma=False)
```

```python
from functools import partial

import jax
import jax.numpy as jnp
import numpy as np
from jax import lax
from jax.sharding import PartitionSpec as P
from jax.experimental import pallas as pl
from jax.experimental.pallas import tpu as pltpu

HD = 64
ROT = 32
LEN = 1024
norm_epsilon = 1e-05
rope_base = 10000.0
MESH = pl.DeviceIdType.MESH

def place():
    dp = lax.axis_index("dp"); tn = lax.axis_index("tensor")
    return dp % 2, (dp // 2) % 4, dp // 8, tn % 4, tn // 4

def peer(c, y, zl, x, zh):
    return (zl * 8 + y * 2 + c, zh * 4 + x)

RELS = [(0, 0), (0, 1), (0, 3), (0, 2), (1, 0), (1, 1), (1, 3), (1, 2)]

def enter(devices):
    bar = pltpu.get_barrier_semaphore()
    for d in devices:
        pl.semaphore_signal(bar, inc=1, device_id=d, device_id_type=MESH)
    pl.semaphore_wait(bar, len(devices))

class Gather:
    def __init__(s, shard, full, axis, ss, rs, by_z=False):
        s.by_z = by_z
        s.axis, s.ss, s.rs, s.full = axis, ss, rs, full
        s.c, s.y, s.zl, x, zh = place()
        c, y, zl = s.c, s.y, s.zl
        s.total = shard.shape[1 if axis == 2 else 0]
        s.shard = shard
        s.up = peer(c, (y + 1) % 4, zl, x, zh); s.down = peer(c, (y + 3) % 4, zl, x, zh)
        s.z = peer(c, y, 1 - zl, x, zh); s.sib = peer(1 - c, y, zl, x, zh)
        s.sends = []
    def slot(s, dz, dy, c=None, half=None):
        c = s.c if c is None else c
        d = ((s.zl + dz) % 2) * 8 + ((s.y + dy) % 4) * 2 + c
        n = s.total if half is None else s.total // 2
        lo = 0 if half is None else half * n
        if s.axis == 0: return s.full.at[pl.ds(pl.multiple_of(d * s.total + lo, 16), n)]
        if s.axis == 2: return s.full.at[:, pl.ds(pl.multiple_of(d * s.total + lo, 16), n)]
        return s.full.at[pl.ds(lo, n), pl.ds(pl.multiple_of(d * 128, 128), 128)]
    def send(s, kind, src, dst, dev):
        cp = pltpu.make_async_remote_copy(src, dst, s.ss.at[kind], s.rs.at[kind], device_id=dev, device_id_type=MESH)
        cp.start(); s.sends.append(cp)
    def got(s, kind, dst):
        pltpu.make_async_remote_copy(dst, dst, s.ss.at[kind], s.rs.at[kind], device_id=s.sib, device_id_type=MESH).wait_recv()
    def start(s):
        own = s.slot(0, 0)
        s.send(0, s.shard, own, s.up); s.send(1, s.shard, own, s.down); s.send(2, s.shard, own, s.z)
        s.send(8, s.shard, own, s.sib)
    def relay(s, rel):
        b = s.slot(*RELS[rel]); s.send(8 + rel, b, b, s.sib)
    def serve(s):
        a = s.slot(0, 3); s.got(0, a); h = s.slot(0, 3, half=0); s.send(5, h, h, s.up)
        b = s.slot(0, 1); s.got(1, b); h = s.slot(0, 1, half=1); s.send(6, h, h, s.down)
        z = s.slot(1, 0); s.got(2, z)
        if s.by_z:
            s.send(3, a, a, s.z); s.send(4, b, b, s.z)
        else:
            s.send(3, z, z, s.up); s.send(4, z, z, s.down)
        s.relay(2); s.relay(1); s.relay(4)
    def serve2(s):
        s.got(5, s.slot(0, 2, half=0)); s.got(6, s.slot(0, 2, half=1))
        f = s.slot(0, 2); s.send(7, f, f, s.z); s.relay(3)
    def serve3(s):
        s.got(3, s.slot(1, 3)); s.relay(6)
        s.got(4, s.slot(1, 1)); s.relay(5)
        s.got(7, s.slot(1, 2)); s.relay(7)
    def arrived(s):
        for r in range(8): s.got(8 + r, s.slot(*RELS[r], c=1 - s.c))

f32 = jnp.float32
bf16 = jnp.bfloat16

def by_rows(rows, step, fn):
    def go(i, carry):
        fn(pl.ds(pl.multiple_of(i * step, step), step))
        return carry
    lax.fori_loop(0, rows // step, go, 0)

def add_into(dst, terms, rows, step, lo=0):
    def go(r):
        if lo: r = pl.ds(pl.multiple_of(r.start + lo, step), step)
        total = terms[0][r, :].astype(f32)
        for t in terms[1:]: total = total + t[r, :].astype(f32)
        dst[r, :] = total.astype(dst.dtype)
    by_rows(rows, step, go)

class Link:
    def __init__(s, ss, rs):
        s.ss, s.rs, s.sends = ss, rs, []
        c, y, zl, x, zh = s.at = place()
        s.c, s.y, s.zl, s.x, s.zh = s.at
        s.sib = peer(1 - c, y, zl, x, zh)
        s.yu, s.yd, s.yf = (peer(c, (y + k) % 4, zl, x, zh) for k in (1, 3, 2))
        s.zn = peer(c, y, 1 - zl, x, zh)
        s.xu, s.xd, s.xf = (peer(c, y, zl, (x + k) % 4, zh) for k in (1, 3, 2))
        s.zf = peer(c, y, zl, x, 1 - zh)
    def send(s, kind, src, dst, dev):
        cp = pltpu.make_async_remote_copy(src, dst, s.ss.at[kind], s.rs.at[kind], device_id=dev, device_id_type=MESH)
        cp.start(); s.sends.append(cp)
    def got(s, kind, dst):
        pltpu.make_async_remote_copy(dst, dst, s.ss.at[kind], s.rs.at[kind], device_id=s.sib, device_id_type=MESH).wait_recv()
    def drain(s):
        for cp in s.sends: cp.wait_send()

class TensorSum(Link):
    def __init__(s, b, f, t1, t2, zs, zr, ss, rs):
        super().__init__(ss, rs)
        s.b, s.f, s.t1, s.t2, s.zs, s.zr = b, f, t1, t2, zs, zr
    def blk(s, zh, dx): return s.b.at[zh * 4 + (s.x + dx) % 4]
    LO, HI = pl.ds(0, 64), pl.ds(64, 64)
    def start_far(s): s.send(0, s.blk(1 - s.zh, 2), s.f, s.zf)
    def start_near(s):
        o = 1 - s.zh
        s.send(1, s.blk(o, 1), s.t2.at[0, o], s.xu); s.send(2, s.blk(o, 3), s.t2.at[1, o], s.xd)
    def start_near2(s):
        s.send(3, s.blk(s.zh, 1).at[s.HI], s.t2.at[0, s.zh, s.HI], s.xu); s.send(4, s.blk(s.zh, 3).at[s.LO], s.t2.at[1, s.zh, s.LO], s.xd)
    def middle(s):
        s.got(0, s.f); add_into(s.f, [s.f, s.blk(s.zh, 2)], 128, 32)
        s.send(5, s.f.at[s.LO], s.t1.at[s.LO], s.xu); s.send(6, s.f.at[s.HI], s.t1.at[s.HI], s.xd)
    def middle2(s):
        s.got(5, s.t1.at[s.LO]); add_into(s.t1, [s.t1, s.blk(s.zh, 1)], 64, 32)
        s.send(7, s.t1.at[s.LO], s.t2.at[0, s.zh, s.LO], s.xu)
        s.got(6, s.t1.at[s.HI]); add_into(s.t1, [s.t1, s.blk(s.zh, 3)], 64, 32, lo=64)
        s.send(8, s.t1.at[s.HI], s.t2.at[1, s.zh, s.HI], s.xd)
    def last(s):
        o = 1 - s.zh
        s.got(1, s.t2.at[0, o]); s.got(2, s.t2.at[1, o])
        add_into(s.zs, [s.blk(o, 0), s.t2.at[0, o], s.t2.at[1, o]], 128, 32)
        s.send(9, s.zs, s.zr, s.zf)
    def total(s, r):
        return (s.blk(s.zh, 0)[r, :].astype(f32) + s.t2.at[0, s.zh][r, :].astype(f32)
                + s.t2.at[1, s.zh][r, :].astype(f32) + s.zr[r, :].astype(f32))
    def arrived(s):
        z = s.zh
        s.got(3, s.t2.at[0, z, s.HI]); s.got(4, s.t2.at[1, z, s.LO]); s.got(7, s.t2.at[0, z, s.LO]); s.got(8, s.t2.at[1, z, s.HI])
        s.got(9, s.zr)

class TensorGather(Link):
    def __init__(s, o, ss, rs):
        super().__init__(ss, rs); s.o = o
    def blk(s, zh, dx): return s.o.at[zh * 4 + (s.x + dx) % 4]
    LO, HI = pl.ds(0, 64), pl.ds(64, 64)
    def start(s, own):
        b = s.blk(s.zh, 0)
        s.send(0, own, b, s.xu); s.send(1, own, b, s.xd); s.send(2, own, b, s.zf)
    def middle(s):
        b = s.blk(s.zh, 3); s.got(0, b); s.send(3, b.at[s.LO], b.at[s.LO], s.xu)
        b = s.blk(s.zh, 1); s.got(1, b); s.send(4, b.at[s.HI], b.at[s.HI], s.xd)
    def plane(s):
        b = s.blk(1 - s.zh, 0); s.got(2, b); s.send(5, b, b, s.xu); s.send(6, b, b, s.xd)
    def far(s):
        b = s.blk(s.zh, 2); s.got(3, b.at[s.LO]); s.got(4, b.at[s.HI]); s.send(7, b, b, s.zf)
    def finish(s):
        o = 1 - s.zh
        s.got(5, s.blk(o, 3)); s.got(6, s.blk(o, 1)); s.got(7, s.blk(o, 2))

class SmallSum(Link):
    def __init__(s, v, rc, rz, ry, rx, rt, acc, out, ss, rs):
        super().__init__(ss, rs)
        s.v, s.rc, s.rz, s.ry, s.rx, s.rt, s.acc, s.out = v, rc, rz, ry, rx, rt, acc, out
    def a(s): s.send(0, s.v.at[1 - s.c], s.rc, s.sib)
    def b(s):
        s.got(0, s.rc); s.rc[...] = s.rc[...] + s.v[s.c]
        s.send(1, s.rc.at[1 - s.zl], s.rz, s.zn)
    def c_(s):
        s.got(1, s.rz); s.rz[...] = s.rz[...] + s.rc[s.zl]
        s.send(2, s.rz.at[(s.y + 1) % 4], s.ry.at[0], s.yu); s.send(3, s.rz.at[(s.y + 3) % 4], s.ry.at[1], s.yd)
        s.send(4, s.rz.at[(s.y + 2) % 4], s.ry.at[2], s.yf)
    def d(s):
        for k in range(3): s.got(2 + k, s.ry.at[k])
        s.acc[0] = s.rz[s.y] + s.ry[0] + s.ry[1] + s.ry[2]
        s.send(5, s.acc.at[0], s.rx.at[0], s.xu); s.send(6, s.acc.at[0], s.rx.at[1], s.xd); s.send(7, s.acc.at[0], s.rx.at[2], s.xf)
    def e(s):
        for k in range(3): s.got(5 + k, s.rx.at[k])
        s.acc[1] = s.acc[0] + s.rx[0] + s.rx[1] + s.rx[2]
        s.send(8, s.acc.at[1], s.rt, s.zf)
    def f(s):
        s.got(8, s.rt)
        first = lax.broadcasted_iota(jnp.int32, (16, 128), 0) < 2
        s.out[...] = jnp.where(first, s.acc[1] + s.rt[...], s.acc[0])

def peers_all():
    c, y, zl, x, zh = place()
    return ([peer(1 - c, y, zl, x, zh), peer(c, y, 1 - zl, x, zh), peer(c, y, zl, x, 1 - zh)]
            + [peer(c, (y + k) % 4, zl, x, zh) for k in (1, 2, 3)] + [peer(c, y, zl, (x + k) % 4, zh) for k in (1, 2, 3)])

def norm_back_rows(r, gn, tokens, cot, gain, out, sums):
    x = tokens[r, :].astype(f32)
    mean = jnp.mean(x, axis=-1, keepdims=True); cen = x - mean
    inv = lax.rsqrt(jnp.mean(cen * cen, axis=-1, keepdims=True) + 1e-5)
    xh = cen * inv
    n = x.shape[0] // 8
    sums[0] += jnp.sum((gn * xh).reshape(n, 8, 2048), axis=0)
    sums[1] += jnp.sum(gn.reshape(n, 8, 2048), axis=0)
    sc = gn * gain
    ig = cot[r, :].astype(f32) + inv * (sc - jnp.mean(sc, axis=-1, keepdims=True) - xh * jnp.mean(sc * xh, axis=-1, keepdims=True))
    out[r, :] = ig.astype(bf16)

PLAN = ("o0", "v0", "q0", "v1", "o1", "q1", "o2", "v2", "q2", "v3", "o3", "u0", "first", "vectors", "n0", "Ao", "q3", "d0", "n1", "n2",
        "n3", "Wo", "Aq", "u1", "ga", "Wq", "p0", "p3", "p1", "p2", "d1", "u2", "a3x", "a0x", "a3y", "sn", "a1x", "u3", "a0y", "d2",
        "a2x", "a2y", "Au", "a1y", "k", "Wu", "h1", "d3", "sa", "sg", "h2", "h0", "h3")

def NT(a, b): return lax.dot_general(a, b, (((1,), (1,)), ((), ())), preferred_element_type=f32)
def NN(a, b): return lax.dot_general(a, b, (((1,), (0,)), ((), ())), preferred_element_type=f32)
def TN(a, b): return lax.dot_general(a, b, (((0,), (0,)), ((), ())), preferred_element_type=f32)

def rotary_tables():
    pos = np.arange(LEN, dtype=np.float32)
    freq = (np.float32(rope_base) ** (-np.arange(0, ROT, 2, dtype=np.float32) / np.float32(ROT))).astype(np.float32)
    ang = (pos[:, None] * freq[None, :]).astype(np.float32)
    cos, sin = np.cos(ang).astype(np.float32), np.sin(ang).astype(np.float32)
    one, zero = np.ones((LEN, 32), np.float32), np.zeros((LEN, 16), np.float32)
    c = np.concatenate([cos, cos, one], 1)
    s1 = np.concatenate([-sin, zero, zero, zero], 1)
    s2 = np.concatenate([zero, sin, zero, zero], 1)
    return np.stack([np.concatenate([t, t], 1) for t in (c, s1, s2)])

def turn(u, tab, r, sign):
    other = pltpu.roll(u, 112, 1) * tab[1, r, :] + pltpu.roll(u, 16, 1) * tab[2, r, :]
    straight = u * tab[0, r, :]
    return straight + other if sign > 0 else straight - other


def pack(vec, gain, lbias, bout, bdown, bup, bqkv):
    dp = lax.axis_index("dp")
    k = lax.broadcasted_iota(jnp.int32, (64, 128), 0); l = lax.broadcasted_iota(jnp.int32, (64, 128), 1)
    up = NN(bup[...], ((l % 64 == k) & (l // 64 == dp % 2)).astype(bf16))
    k4 = k[0:4]; l4 = l[0:4]
    on = (l4 % 4 == k4) & ((l4 % 64) // 4 == dp)
    rows = [gain[...].astype(f32), lbias[...].astype(f32), bout[...].astype(f32), bdown[...].astype(f32), up]
    for j in range(3):
        lo = NN(bqkv[j], (on & (l4 < 64)).astype(bf16)); hi = NN(bqkv[j], (on & (l4 >= 64)).astype(bf16))
        rows += [lo[0:1] + hi[1:2], lo[2:3] + hi[3:4]]
    vec[...] = jnp.concatenate(rows + [jnp.zeros((21, 128), f32)], 0).astype(bf16)

def forward_kernel(gain_s, lbias_s, bout_s, bdown_s, bup_s, bqkv_s, wq, wout, wup, wdown, tok_h, cot_h, tab_h,
                   vecs, wq_f, wout_f, wup_f, wdown_f, rows_h, nrm_h, att_h, act_h, dact_h, gp_h,
                   vec, tab, vv, wqv, woutv, wupv, tok, cot, nrm, rowsv, bqkv, bup, q, k, v, ga, att, dk, dv, gp, act, dact,
                   ss, rs, ls, ld):
    c, y, zl, x, zh = place()
    loads = {}
    def load(i, src, dst):
        loads[i] = pltpu.make_async_copy(src, dst, ld.at[i]); loads[i].start()
    load(0, tok_h, tok); load(1, cot_h, cot); load(12, tab_h, tab)
    pack(vec, gain_s, lbias_s, bout_s, bdown_s, bup_s, bqkv_s)
    enter([peer(c, (y + 1) % 4, zl, x, zh), peer(c, (y + 3) % 4, zl, x, zh), peer(c, y, 1 - zl, x, zh), peer(1 - c, y, zl, x, zh)])
    gv, gq, go, gu, gd = every = [Gather(a, b, ax, ss.at[i], rs.at[i], i == 2) for i, (a, b, ax) in enumerate(
        [(vec, vecs, 0), (wq, wq_f, 2), (wout, wout_f, 1), (wup, wup_f, 0), (wdown, wdown_f, 1)])]
    local = [pltpu.make_async_copy(g.shard, g.slot(0, 0), ls.at[i]) for i, g in enumerate(every)]
    for cp in local: cp.start()

    def norm(lo, hi):
        gain, bias = rowsv[0:1, :], rowsv[1:2, :]
        def go_(i, carry):
            r = pl.ds(pl.multiple_of(lo + i * 128, 128), 128)
            a = tok[r, :].astype(f32)
            cen = a - jnp.mean(a, axis=-1, keepdims=True)
            inv = lax.rsqrt(jnp.mean(cen * cen, axis=-1, keepdims=True) + norm_epsilon)
            nrm[r, :] = (cen * inv * gain + bias).astype(bf16)
            return carry
        lax.fori_loop(0, (hi - lo) // 128, go_, 0)

    def project(lo, hi):
        def go_(i, carry):
            r = pl.ds(pl.multiple_of(lo + i * 256, 256), 256)
            n = nrm[r, :]
            for j, dst in enumerate((q, k, v)):
                p = NN(n, wqv[j])
                for h in range(2):
                    u = p[:, h * 128:(h + 1) * 128] + bqkv[2 * j + h:2 * j + h + 1, :]
                    dst[h, r, :] = (u if j == 2 else turn(u, tab, r, 1)).astype(bf16)
            return carry
        lax.fori_loop(0, (hi - lo) // 256, go_, 0)

    def grad_attended():
        def go_(i, carry):
            r = pl.ds(pl.multiple_of(i * 512, 512), 512)
            p = NT(cot[r, :], woutv[...])
            ga[0, r, :] = p[:, 0:128].astype(bf16); ga[1, r, :] = p[:, 128:256].astype(bf16)
            return carry
        lax.fori_loop(0, 2, go_, 0)

    def attention(i):
        lax.fori_loop(0, 2, lambda p, carry: attention_pair(i, p, carry), 0)
    def attention_pair(i, p, carry=0):
            n = (i + 1) * 256
            r = pl.ds(i * 256, 256)
            cols = pl.ds(pl.multiple_of(p * 128, 128), 128)
            a_, d_, tk, tv = 0.0, 0.0, 0.0, 0.0
            for hh in range(2):
                m = ((lax.broadcasted_iota(jnp.int32, (1, 128), 1) // 64) == hh).astype(bf16)
                kk = k[p, 0:n] * m; w = v[p, 0:n] * m; qq = q[p, r] * (m * 0.125); gg = ga[p, r] * m
                s = NT(kk, qq)
                key = lax.broadcasted_iota(jnp.int32, (256, 256), 0); row = lax.broadcasted_iota(jnp.int32, (256, 256), 1)
                diag = jnp.where(row >= key, s[n - 256:], -1e30)
                s = diag if i == 0 else jnp.concatenate([s[:n - 256], diag], 0)
                e = jnp.exp(s - jnp.max(s, 0, keepdims=True))
                pr = e * (1.0 / jnp.sum(e, 0, keepdims=True))
                low = pr.astype(bf16)
                dp = NT(w, gg)
                ds = (pr * (dp - jnp.sum(pr * dp, 0, keepdims=True))).astype(bf16)
                a_ = a_ + TN(low, w); d_ = d_ + TN(ds, kk)
                tk = tk + NN(ds, qq); tv = tv + NN(low, gg)
            att[r, cols] = a_.astype(bf16)
            gp[r, cols] = turn(d_ * 0.125, tab, r, -1).astype(bf16)
            if i == 3: dk[p] = tk; dv[p] = tv
            else:
                dk[p, 0:n] += tk; dv[p, 0:n] += tv
            return carry

    def keys_done():
        def go_(i, carry):
            r = pl.ds(pl.multiple_of(i * 256, 256), 256)
            for p in range(2):
                gp[r, 256 + p * 128:384 + p * 128] = turn(dk[p, r], tab, r, -1).astype(bf16)
                gp[r, 512 + p * 128:640 + p * 128] = dv[p, r].astype(bf16)
            return carry
        lax.fori_loop(0, 4, go_, 0)

    def hidden(lo, hi):
        def go_(i, carry):
            r = pl.ds(pl.multiple_of(lo + i * 256, 256), 256)
            n = nrm[r, :]
            for j in range(4):
                cols = pl.ds(j * 256, 256)
                h = NN(n, wupv[:, cols]) + bup[0:1, cols]
                h2 = h * h
                t = 0.5 + 0.5 * jnp.tanh(h * (0.7978845608028654 + 0.035677408136300125 * h2))
                y_ = h * t
                act[r, cols] = y_.astype(bf16)
                dact[r, cols] = (t + y_ * ((2.0 - 2.0 * t) * (0.7978845608028654 + 0.10703222440890037 * h2))).astype(bf16)
            return carry
        lax.fori_loop(0, (hi - lo) // 256, go_, 0)
        r = pl.ds(lo, hi - lo)
        load(13 + lo // 256, act.at[r], act_h.at[r]); load(17 + lo // 256, dact.at[r], dact_h.at[r])

    def first():
        gv.arrived(); local[0].wait(); load(2, vecs, vv)
    def vectors():
        loads[2].wait(); loads[0].wait()
        bq, bu = jnp.zeros((6, 128), f32), None
        for d in range(16):
            t = vv[pl.ds(d * 32, 32), :].astype(f32)
            cols = pl.ds(d * 128, 128)
            rowsv[0:1, cols] = t[0:1]; rowsv[1:2, cols] = t[1:2]; rowsv[2:3, cols] = t[2:3] + t[3:4]
            bq = bq + t[5:11]
            if d % 2 == 0: bu = t[4:5]
            else: bup[0:1, pl.ds((d // 2) * 128, 128)] = bu + t[4:5]
        bqkv[0:6, :] = bq
        load(6, rowsv, rows_h)
    def have_q():
        gq.arrived(); local[1].wait(); load(3, wq_f, wqv)
    def have_o():
        go.arrived(); local[2].wait(); load(4, wout_f, woutv)
    def have_u():
        gu.arrived(); local[3].wait(); load(7, wup_f, wupv)
    steps = {"first": first, "vectors": vectors, "Aq": have_q, "Ao": have_o, "Au": have_u,
             "Wq": lambda: (loads[3].wait(), loads[12].wait()), "Wo": lambda: (loads[4].wait(), loads[1].wait()), "Wu": lambda: loads[7].wait(),
             "ga": grad_attended, "k": keys_done, "sn": lambda: load(5, nrm, nrm_h), "sa": lambda: load(8, att, att_h), "sg": lambda: load(9, gp, gp_h)}
    for i in range(4):
        steps["n%d" % i] = partial(norm, i * 256, i * 256 + 256)
        steps["p%d" % i] = partial(project, i * 256, i * 256 + 256)
        steps["h%d" % i] = partial(hidden, i * 256, i * 256 + 256)
        steps["a%d" % i] = partial(attention, i)
        for p in range(2): steps["a%d%s" % (i, "xy"[p])] = partial(attention_pair, i, p)
    for nm, g in (("v", gv), ("q", gq), ("o", go), ("u", gu), ("d", gd)):
        steps[nm + "0"], steps[nm + "1"], steps[nm + "2"], steps[nm + "3"] = g.start, g.serve, g.serve2, g.serve3
    for name in PLAN: steps[name]()
    gd.arrived()
    for i in (5, 6, 8, 9, *range(13, 21)): loads[i].wait()
    local[4].wait()
    for g in (gv, gq, go, gu, gd):
        for cp in g.sends: cp.wait_send()

def forward(vectors, wq, wout, wup, wdown, tokens, cot, tab):
    A = pl.BlockSpec(memory_space=pl.ANY); V = pl.BlockSpec(memory_space=pltpu.VMEM)
    S = jax.ShapeDtypeStruct
    vm = lambda sh, t=bf16: pltpu.VMEM(sh, t)
    return pl.pallas_call(forward_kernel,
        out_shape=[S((512, 128), bf16), S((3, 2048, 256), bf16), S((256, 2048), bf16), S((2048, 1024), bf16), S((1024, 2048), bf16),
                   S((8, 2048), f32), S((1024, 2048), bf16), S((1024, 256), bf16), S((1024, 1024), bf16), S((1024, 1024), bf16), S((1024, 768), bf16)],
        in_specs=[V] * 10 + [A] * 3, out_specs=[A] * 11,
        scratch_shapes=[vm((32, 128)), vm((3, 1024, 128), f32), vm((512, 128)), vm((3, 2048, 256)), vm((256, 2048)), vm((2048, 1024)), vm((1024, 2048)), vm((1024, 2048)), vm((1024, 2048)),
                        vm((8, 2048), f32), vm((8, 128), f32), vm((8, 1024), f32), vm((2, 1024, 128)), vm((2, 1024, 128)), vm((2, 1024, 128)), vm((2, 1024, 128)),
                        vm((1024, 256)), vm((2, 1024, 128), f32), vm((2, 1024, 128), f32), vm((1024, 768)), vm((1024, 1024)), vm((1024, 1024)),
                        pltpu.SemaphoreType.DMA((5, 16)), pltpu.SemaphoreType.DMA((5, 16)), pltpu.SemaphoreType.DMA((5,)), pltpu.SemaphoreType.DMA((21,))],
        compiler_params=pltpu.CompilerParams(collective_id=1, has_side_effects=True, vmem_limit_bytes=60 << 20),
        name="gather_and_forward")(*vectors, wq, wout, wup, wdown, tokens, cot, tab)

PLAN_B = ("L0", "bB", "L1", "bA", "bD", "bC", "h0", "h1", "n0", "n1", "bM", "n2", "n3", "gS", "s2P0", "s2P1", "bL", "s2P2", "s2p0", "s2P3",
          "gM", "bN", "s2p1", "s21", "gL", "suP0", "gN", "s22", "mS", "suP1", "bias", "iS", "sup0", "sup1", "su1", "sqP0", "s23", "va", "vb", "mM",
          "sqP1", "vc", "su2", "sqp0", "iM", "sqp1", "mP", "vd", "mF", "sq1", "sq2", "su3", "iP", "s24", "iF", "ve", "mE", "sq3", "su4", "vf",
          "sq4", "iE")

class Scatter(Link):
    def __init__(s, g, sib, mid, ss, rs, width):
        super().__init__(ss, rs)
        s.g, s.b, s.m, s.w = g, sib, mid, width
    def to_sibling(s, k):
        return pltpu.make_async_remote_copy(s.g.at[k, 1 - s.c, :, pl.ds(0, s.w)], s.b.at[k], s.ss.at[k], s.rs.at[k],
                                            device_id=s.sib, device_id_type=MESH)
    def produce(s, lhs, rhs, lo, hi):
        n = rhs.shape[1]
        def go(j, carry):
            y = (s.y + 2 + 3 * j) % 4
            a = jnp.concatenate([lhs[:, pl.ds(pl.multiple_of((p * 4 + y) * 256, 256), 256)] for p in range(2)], 1)
            for at in range(0, n, 256):
                r = TN(a, rhs[:, at:at + 256]).astype(bf16)
                for p in range(2):
                    for cc in range(2): s.g[2 * j + p, cc, :, at:at + 256] = r[p * 256 + cc * 128:p * 256 + cc * 128 + 128]
            for p in range(2):
                s.to_sibling(2 * j + p).start()
            return carry
        lax.fori_loop(lo, hi, go, 0)
    def pairs(s, lo, hi):
        def go(k, carry):
            s.to_sibling(k).wait()
            mine = s.g.at[k, s.c]; dst = s.b.at[k]
            def rows(i, cc):
                r = pl.ds(pl.multiple_of(i * 32, 32), 32)
                dst[r, :] = (dst[r, :].astype(f32) + mine[r, 0:s.w].astype(f32)).astype(bf16)
                return cc
            lax.fori_loop(0, 4, rows, 0)
            return carry
        lax.fori_loop(lo, hi, go, 0)
    def serve1(s):
        s.send(8, s.b.at[0], s.m.at[0], s.yu); s.send(9, s.b.at[1], s.m.at[1], s.yd)
        s.send(10, s.b.at[3], s.m.at[4], s.yu); s.send(11, s.b.at[6], s.m.at[2], s.yd)
    def serve2(s):
        s.got(8, s.m.at[0]); add_into(s.b.at[2], [s.b.at[2], s.m.at[0]], 128, 32); s.send(12, s.b.at[2], s.m.at[3], s.yu)
        s.got(9, s.m.at[1]); add_into(s.b.at[7], [s.b.at[7], s.m.at[1]], 128, 32); s.send(13, s.b.at[7], s.m.at[5], s.yd)
    def serve3(s):
        for k, j in ((10, 4), (11, 2), (12, 3), (13, 5)): s.got(k, s.m.at[j])
        o = 1 - s.zl; b = s.b.at[4 + o]
        add_into(b, [b, s.m.at[2 + 2 * o], s.m.at[3 + 2 * o]], 128, 32); s.send(14, b, s.m.at[6], s.zn)
    def serve4(s, put, step=32):
        s.got(14, s.m.at[6])
        z = s.zl
        terms = (s.b.at[4 + z], s.m.at[2 + 2 * z], s.m.at[3 + 2 * z], s.m.at[6])
        def go(r):
            t = terms[0][r, :].astype(f32)
            for q in terms[1:]: t = t + q[r, :].astype(f32)
            put(r, t)
        by_rows(128, step, go)

def backward_kernel(wq_f, wout_f, wup_f, wdown_f, rows_h, nrm_h, att_h, act_h, dact_h, gp_h, cot_h, tok_h,
                    mixed, ingrad, o2, oup, oq, osv,
                    wb, wch, cot, nrm, aa, pq, rowsv, tok, brp, gnp, own,
                    fa, t1a, t2a, zsa, zra, fb, t1b, t2b, zsb, zrb, g, sib2, m2, sibu, mu, sibq, mq,
                    v, rc, rz, ry, rx, rt, acc, sums, ss, rs, ld):
    c, y, zl, x, zh = place()
    t_own = zh * 4 + x
    o = 1 - zh
    loads = {}
    def load(i, src, dst):
        loads[i] = pltpu.make_async_copy(src, dst, ld.at[i]); loads[i].start()
    def wait(*ids):
        for i in ids: loads[i].wait()
    load(0, att_h, aa.at[:, pl.ds(0, 256)]); load(1, act_h, aa.at[:, pl.ds(256, 1024)])
    for j in range(4):
        cols = pl.ds(j * 512, 512)
        load(20 + j, wout_f.at[:, cols], wb.at[pl.ds(0, 256), cols]); load(24 + j, wdown_f.at[:, cols], wb.at[pl.ds(256, 1024), cols])
    enter(peers_all())
    bs = TensorSum(brp, fa, t1a, t2a, zsa, zra, ss.at[0], rs.at[0])
    gs = TensorSum(gnp, fb, t1b, t2b, zsb, zrb, ss.at[1], rs.at[1])
    mg = TensorGather(mixed, ss.at[2], rs.at[2])
    ig = TensorGather(ingrad, ss.at[3], rs.at[3])
    s2 = Scatter(g, sib2, m2, ss.at[4], rs.at[4], 1280)
    su = Scatter(g, sibu, mu, ss.at[5], rs.at[5], 1024)
    sq = Scatter(g, sibq, mq, ss.at[6], rs.at[6], 768)
    sm = SmallSum(v, rc, rz, ry, rx, rt, acc, osv, ss.at[7], rs.at[7])
    gp, gh = pq.at[:, pl.ds(0, 768)], pq.at[:, pl.ds(768, 1024)]

    def chunk(j):
        s = j % 2; r = pl.ds(j * 512, 512)
        for e in range(3): load(10 + 4 * s + e, wq_f.at[e, r], wch.at[s, :, pl.ds(e * 256, 256)])
        load(13 + 4 * s, wup_f.at[r], wch.at[s, :, pl.ds(768, 1024)])
    def first_loads(): wait(0, 1)
    def other_loads():
        load(4, cot_h, cot); load(5, dact_h, gh); load(6, gp_h, gp); chunk(0); chunk(1); load(7, nrm_h, nrm)
        load(8, rows_h, rowsv); load(9, tok_h.at[pl.ds(pl.multiple_of(t_own * 128, 128), 128)], tok)
    def branch(a, b, first=False):
        ra, rb = (pl.ds(pl.multiple_of(t * 128, 128), 128) for t in (a, b))
        lhs = jnp.concatenate([aa[ra, :], aa[rb, :]], 0)
        for j in range(4):
            if first: wait(20 + j, 24 + j)
            cols = pl.ds(j * 512, 512)
            p = NN(lhs, wb[:, cols]).astype(bf16)
            brp[a, :, cols] = p[0:128]; brp[b, :, cols] = p[128:256]
    def grad_hidden(lo, hi):
        if lo == 0: wait(4, 5)
        def go(i, carry):
            r = pl.ds(pl.multiple_of(i * 512, 512), 512)
            gr = cot[r, :]
            for j in range(4):
                p = NT(gr, wb[256 + j * 256:512 + j * 256, :])
                cols = pl.ds(768 + j * 256, 256)
                pq[r, cols] = (p * pq[r, cols].astype(f32)).astype(bf16)
            return carry
        lax.fori_loop(lo, hi, go, 0)
    def grad_normed(j):
        s = j % 2
        if j == 0: wait(6)
        wait(*range(10 + 4 * s, 14 + 4 * s))
        p = NT(pq[...], wch[s]).astype(bf16)
        gnp[:, :, j * 512:(j + 1) * 512] = p.reshape(8, 128, 512)
        if j + 2 < 4: chunk(j + 2)
    def bias_sums():
        ones = jnp.ones((16, 1024), bf16)
        for d in range(8):
            w = v.at[:, d // 4, d % 4]
            gb = NN(ones, cot[:, d * 256:(d + 1) * 256])[0:1]
            gu_ = NN(ones, gh[:, d * 128:(d + 1) * 128])[0:1]
            for cc in range(2):
                w[cc, 2:3, :] = gb[:, cc * 128:(cc + 1) * 128]; w[cc, 3:4, :] = gu_
        for j in range(3):
            gqb = NN(ones, gp[:, j * 256:(j + 1) * 256])[0:1]
            for d in range(16):
                w = v.at[d % 2, d // 8, (d // 2) % 4]
                w[4 + 2 * j:5 + 2 * j, :] = gqb[:, 0:128]; w[5 + 2 * j:6 + 2 * j, :] = gqb[:, 128:256]
    def mixed_start():
        bs.arrived()
        def mix(r): own[0, r, :] = (tok[r, :].astype(f32) + bs.total(r) + rowsv[2:3, :]).astype(bf16)
        wait(8, 9)
        by_rows(128, 64, mix)
        load(18, own.at[0], mixed.at[t_own])
        mg.start(own.at[0])
    def ingrad_start():
        gs.arrived()
        sums[...] = jnp.zeros_like(sums)
        cot_own = cot.at[pl.ds(pl.multiple_of(t_own * 128, 128), 128)]
        by_rows(128, 32, lambda r: norm_back_rows(r, gs.total(r), tok, cot_own, rowsv[0:1, :], own.at[1], sums))
        load(19, own.at[1], ingrad.at[t_own])
        ig.start(own.at[1])
    def norm_sums():
        sg = jnp.sum(sums[0], axis=0, keepdims=True); sb = jnp.sum(sums[1], axis=0, keepdims=True)
        for d in range(16):
            w = v.at[d % 2, d // 8, (d // 2) % 4]
            w[0:1, :] = sg[:, d * 128:(d + 1) * 128]; w[1:2, :] = sb[:, d * 128:(d + 1) * 128]
        sm.a()
    def put2(r, t):
        for b in range(10): o2[b * 128:(b + 1) * 128, :] = t[:, b * 128:(b + 1) * 128].T
    def putu(r, t): oup[r, :] = t
    def putq(r, t): oq[r, :] = t
    def xp(k): return (x + k) % 4
    def far(): branch(o * 4 + xp(2), zh * 4 + xp(2)); bs.start_far()
    def near(): branch(o * 4 + xp(1), o * 4 + xp(3), True); bs.start_near()
    def near2(): branch(zh * 4 + xp(1), zh * 4 + xp(3)); bs.start_near2()
    def home(): branch(o * 4 + xp(0), zh * 4 + xp(0))
    def gn_start(): gs.start_far(); gs.start_near(); gs.start_near2()
    steps = {"L0": first_loads, "L1": other_loads, "bA": far, "bB": near, "bC": near2, "bD": home, "gS": gn_start, "bias": bias_sums,
             "mS": mixed_start, "iS": ingrad_start, "va": norm_sums, "vb": sm.b, "vc": sm.c_, "vd": sm.d, "ve": sm.e, "vf": sm.f,
             "h0": partial(grad_hidden, 0, 1), "h1": partial(grad_hidden, 1, 2),
             "s24": partial(s2.serve4, put2, 128), "su4": partial(su.serve4, putu), "sq4": partial(sq.serve4, putq)}
    for i in range(4):
        steps["n%d" % i] = partial(grad_normed, i); steps["s2P%d" % i] = partial(s2.produce, cot, aa, i, i + 1)
    def up_grads(lo, hi):
        if lo == 0: wait(7)
        su.produce(nrm, gh, lo, hi)
    for i in range(2):
        steps["suP%d" % i] = partial(up_grads, 2 * i, 2 * i + 2); steps["sqP%d" % i] = partial(sq.produce, nrm, gp, 2 * i, 2 * i + 2)
        for nm, w in (("s2", s2), ("su", su), ("sq", sq)): steps[nm + "p%d" % i] = partial(w.pairs, 4 * i, 4 * i + 4)
    for nm, w in (("s2", s2), ("su", su), ("sq", sq)): steps[nm + "1"], steps[nm + "2"], steps[nm + "3"] = w.serve1, w.serve2, w.serve3
    for nm, w in (("b", bs), ("g", gs)): steps[nm + "M"], steps[nm + "N"], steps[nm + "L"] = w.middle, w.middle2, w.last
    for nm, w in (("m", mg), ("i", ig)): steps[nm + "M"], steps[nm + "P"], steps[nm + "F"], steps[nm + "E"] = w.middle, w.plane, w.far, w.finish
    for name in PLAN_B: steps[name]()
    wait(18, 19)
    for w in (gs, bs, mg, ig, s2, su, sq, sm): w.drain()

def backward(wq_f, wout_f, wup_f, wdown_f, rows, nrm, att, act, dact, gp, cot, tok):
    S = jax.ShapeDtypeStruct
    vm = lambda sh, t=bf16: pltpu.VMEM(sh, t)
    tsum = [vm((128, 2048)), vm((128, 2048)), vm((2, 2, 128, 2048)), vm((128, 2048)), vm((128, 2048))]
    A = pl.BlockSpec(memory_space=pl.ANY); V = pl.BlockSpec(memory_space=pltpu.VMEM)
    return pl.pallas_call(backward_kernel,
        out_shape=[S((8, 128, 2048), bf16)] * 2 + [S((1280, 128), f32), S((128, 1024), f32), S((128, 768), f32), S((16, 128), f32)],
        in_specs=[A] * 12, out_specs=[A] * 2 + [V] * 4,
        scratch_shapes=[vm((1280, 2048)), vm((2, 512, 1792)), vm((1024, 2048)), vm((1024, 2048)), vm((1024, 1280)), vm((1024, 1792)),
                        vm((8, 2048), f32), vm((128, 2048)), vm((8, 128, 2048)), vm((8, 128, 2048)), vm((2, 128, 2048))]
        + tsum + tsum + [vm((8, 2, 128, 1280)), vm((8, 128, 1280)), vm((7, 128, 1280)), vm((8, 128, 1024)), vm((7, 128, 1024)), vm((8, 128, 768)), vm((7, 128, 768)),
            vm((2, 2, 4, 16, 128), f32), vm((2, 4, 16, 128), f32), vm((4, 16, 128), f32), vm((3, 16, 128), f32), vm((3, 16, 128), f32), vm((16, 128), f32),
            vm((2, 16, 128), f32), vm((2, 8, 2048), f32),
            pltpu.SemaphoreType.DMA((8, 16)), pltpu.SemaphoreType.DMA((8, 16)), pltpu.SemaphoreType.DMA((28,))],
        compiler_params=pltpu.CompilerParams(collective_id=2, has_side_effects=True, vmem_limit_bytes=64 << 20),
        name="backward_and_sums")(wq_f, wout_f, wup_f, wdown_f, rows, nrm, att, act, dact, gp, cot, tok)

def hand_over_kernel(mixed, ingrad, o2_h, oup_h, oq_h, osv, mo, io, gg, gb, gq_h, gbq, go_h, gbo, gu_h, gbu, gd_h, gbd,
                     big, o2, oup, oq, li, lo):
    dp = lax.axis_index("dp")
    def copy(a, b, sem, queue=0):
        cp = pltpu.make_async_copy(a, b, sem); cp.start(priority=queue)
        return cp
    n = 8
    ins = [copy((mixed, ingrad)[i // 4].at[pl.ds((i % 4) * 2, 2)], big.at[i], li.at[i], i % 2) for i in range(4)]
    small = [copy(o2_h, o2, li.at[n]), copy(oup_h, oup, li.at[n + 1]), copy(oq_h, oq, li.at[n + 2])]
    ins += [copy((mixed, ingrad)[i // 4].at[pl.ds((i % 4) * 2, 2)], big.at[i], li.at[i], i % 2) for i in range(4, 8)]
    outs = []
    def pass_on(i):
        ins[i].wait()
        for h in range(2): outs.append(copy(big.at[i, h], (mo, io)[i // 4].at[pl.ds((i % 4) * 256 + h * 128, 128)], lo.at[2 * i + h], (i + 1) % 2))
    pass_on(0); pass_on(1)
    small[0].wait()
    outs += [copy(o2.at[pl.ds(0, 256)], go_h, lo.at[16]), copy(o2.at[pl.ds(256, 1024)], gd_h, lo.at[17])]
    pass_on(2); pass_on(3)
    small[1].wait(); outs.append(copy(oup, gu_h, lo.at[18]))
    small[2].wait()
    for j in range(3): outs.append(copy(oq.at[:, pl.ds(j * 256, 256)], gq_h.at[j], lo.at[19 + j]))
    pass_on(4); pass_on(5)
    gg[...] = osv[0:1, :]; gb[...] = osv[1:2, :]; gbo[...] = osv[2:3, :]; gbd[...] = osv[2:3, :]
    l = lax.broadcasted_iota(jnp.int32, (128, 64), 0); k = lax.broadcasted_iota(jnp.int32, (128, 64), 1)
    gbu[...] = lax.dot_general(osv[3:4, :], (l == k + 64 * (dp % 2)).astype(f32), (((1,), (0,)), ((), ())), precision=lax.Precision.HIGHEST)
    l = lax.broadcasted_iota(jnp.int32, (128, 4), 0); k = lax.broadcasted_iota(jnp.int32, (128, 4), 1)
    for j in range(3):
        rows = osv[4 + 2 * j:6 + 2 * j, :]
        lo_, hi_ = (lax.dot_general(rows, (l == k + 4 * dp + 64 * h).astype(f32), (((1,), (0,)), ((), ())), precision=lax.Precision.HIGHEST) for h in (0, 1))
        gbq[j] = jnp.concatenate([lo_[0:1], hi_[0:1], lo_[1:2], hi_[1:2]], 0)
    pass_on(6); pass_on(7)
    for cp in outs: cp.wait()

def hand_over(mixed, ingrad, o2, oup, oq, osv):
    S = jax.ShapeDtypeStruct
    A = pl.BlockSpec(memory_space=pltpu.HBM)
    full = lambda sh: pl.BlockSpec(sh, lambda: (0,) * len(sh))
    outs = [((1, 128), 0), ((1, 128), 0), ((3, 128, 256), 1), ((3, 4, 4), 0), ((256, 128), 1), ((1, 128), 0), ((128, 1024), 1), ((1, 64), 0), ((1024, 128), 1), ((1, 128), 0)]
    vm = lambda sh: pltpu.VMEM(sh, f32)
    return pl.pallas_call(hand_over_kernel,
        out_shape=[S((1024, 2048), bf16)] * 2 + [S(sh, f32) for sh, _ in outs],
        in_specs=[A] * 5 + [full((16, 128))], out_specs=[A] * 2 + [A if m else full(sh) for sh, m in outs],
        scratch_shapes=[pltpu.VMEM((8, 2, 128, 2048), bf16), vm((1280, 128)), vm((128, 1024)), vm((128, 768)),
                        pltpu.SemaphoreType.DMA((12,)), pltpu.SemaphoreType.DMA((22,))],
        compiler_params=pltpu.CompilerParams(vmem_limit_bytes=62 << 20),
        name="hand_over")(mixed, ingrad, o2, oup, oq, osv)

def body(tokens, ln_gain, ln_bias, w_qkv, b_qkv, w_out, b_out, w_up, b_up, w_down, b_down, cotangent):
    row = lambda a: a.reshape(1, 128)
    vecs, wq_f, wout_f, wup_f, wdown_f, rows, nrm, att, act, dact, gp = forward(
        (row(ln_gain), row(ln_bias), row(b_out), row(b_down), b_up, b_qkv), w_qkv.transpose(1, 0, 2), w_out, w_up, w_down,
        tokens, cotangent, jnp.asarray(rotary_tables()))
    parts = backward(wq_f, wout_f, wup_f, wdown_f, rows, nrm, att, act, dact, gp, cotangent, tokens)
    mixed, ingrad, gg, gb, gq, gbq, go, gbo, gu, gbu, gd, gbd = hand_over(*parts)
    return (mixed, ingrad, gg.reshape(128), gb.reshape(128), gq.transpose(1, 0, 2), gbq, go, gbo.reshape(128), gu, gbu, gd, gbd.reshape(128))


def solution(mesh):
    in_specs = (
        P("dp", None),
        P("dp"),
        P("dp"),
        P("dp", None, "tensor"),
        P(None, "tensor", "dp"),
        P("tensor", "dp"),
        P("dp"),
        P("dp", "tensor"),
        P("tensor", "dp"),
        P("tensor", "dp"),
        P("dp"),
        P("dp", None),
    )
    out_specs = (
        P("dp", None),
        P("dp", None),
        P("dp"),
        P("dp"),
        P("dp", None, "tensor"),
        P(None, "tensor", "dp"),
        P("tensor", "dp"),
        P("dp"),
        P("dp", "tensor"),
        P("tensor", "dp"),
        P("tensor", "dp"),
        P("dp"),
    )
    return jax.shard_map(body, mesh=mesh, in_specs=in_specs, out_specs=out_specs, check_vma=False)
```
